32 devices in a mesh: dp: 16 (over z, x, core), blk: 2 (over y).
Axes of the slice: x: 2, y: 2, z: 4, core: 2. Of those that a mesh axis runs over, the one named last changes fastest.
Arguments:
- latents: bfloat16 [64, 64, 768], P('dp', 'blk'), may hold values from -6 to 6
- restore: int32 [64, 256], P('dp', 'blk'), may hold values from 0 to 64, as said below
- bucket: int32 [64], P('dp'), may hold values from 0 to 2, as said below
- cotangent: bfloat16 [64, 256, 512], P('dp', 'blk'), may hold values from -6 to 6
- flat_weights: float32 [3538944], P(('dp', 'blk')), may hold values from -1 to 1
- flat_first: float32 [3538944], P(('dp', 'blk')), may hold values from -0.0008544922 to 0.0008544922
- flat_second: float32 [3538944], P(('dp', 'blk')), may hold values from 1.4833147e-08 to 5.9219786e-08
- vectors: float32 [14, 512], replicated, may hold values from -3 to 3
- vector_first: float32 [14, 512], replicated, may hold values from -0.0034179688 to 0.0034179688
- vector_second: float32 [14, 512], replicated, may hold values from 2.3687915e-07 to 9.587966e-07
Outputs:
- block_out: float32 [64, 256, 512], P('dp', 'blk')
- latent_grad: float32 [64, 64, 768], P('dp', 'blk')
- new_first: float32 [3538944], P(('dp', 'blk'))
- new_second: float32 [3538944], P(('dp', 'blk'))
- new_weights: float32 [3538944], P(('dp', 'blk'))
- vector_first_new: float32 [14, 512], replicated
- vector_second_new: float32 [14, 512], replicated
- vectors_new: float32 [14, 512], replicated
- reduce_bias_grad: float32 [512], replicated
- grad_norm: float32 [], replicated
The draws below stay inside these ranges and needn't reach their ends.
Inputs may be any that keep to these rules, and one draw needn't show every extreme that they name: In each micro-batch of the images of one index of dp, images m * 2 to (m+1) * 2 - 1 of that index, at least one image has bucket 2. `restore`: for an image of length L, the L // 4 valid slots whose values are below 64 hold 0 to L // 4 - 1, each once; every other slot holds 64; latent rows from L // 4 on are never named.
All inputs are finite; a program needn't handle non-finite values.
Results may differ from the reference program's by a relative error of at most 0.014.
Values may be sent and summed in bfloat16 or wider, within the bound.
No kernel may reach another device: no remote copies, remote signals or barrier semaphores. Data moves between devices by JAX's collectives and lax.ppermute only.
A program may use at most 128 MiB of HBM per device.

```python
import math
import jax
import jax.numpy as jnp
from jax import lax

DIN = 768
D = 512
HEADS = 16
HD = 32
FF = 2048
SLOTS = 256
KMAX = 64
IMG_MB = 2
STEP = 10
IMAGES = 64
NPARAM = 3538944


def image_lengths_drawn(bucket):
    return jnp.where(bucket == 0, SLOTS * 100 // 256, jnp.where(bucket == 1, SLOTS * 196 // 256, SLOTS)).astype(jnp.int32)


def bucket_helper(key):
    base = jax.random.randint(jax.random.fold_in(key, 11), (IMAGES,), 0, 3)
    chosen = jax.random.randint(jax.random.fold_in(key, 12), (IMAGES // IMG_MB,), 0, IMG_MB)
    place = jnp.arange(IMAGES, dtype=jnp.int32) % IMG_MB
    forced = place == jnp.repeat(chosen, IMG_MB)
    return jnp.where(forced, 2, base).astype(jnp.int32)


def draw_bucket(key, part):
    return bucket_helper(key)


def draw_restore(key, part):
    buckets = bucket_helper(key)
    key = jax.random.fold_in(key, 5)
    lengths = image_lengths_drawn(buckets)
    noise = jax.random.randint(key, (IMAGES, SLOTS), 0, 1 << 20)
    slot = jnp.arange(SLOTS, dtype=jnp.int32)[None, :]
    score = noise * SLOTS + slot + jnp.where(slot >= lengths[:, None], 1 << 29, 0)
    order = jnp.argsort(score, axis=1)
    placing = jnp.argsort(order, axis=1).astype(jnp.int32)
    kept = lengths[:, None] // 4
    return jnp.where(placing < kept, placing, KMAX).astype(jnp.int32)


def draw_flat_weights(key, part):
    key = jax.random.fold_in(key, 7)
    layout = [(DIN * D, DIN ** (-0.5)), (3 * D * D, D ** (-0.5)), (D * D, SLOTS ** 0.5 / 4.0 * D ** (-0.5)), (D * FF, D ** (-0.5)), (FF * D, FF ** (-0.5))]
    pieces = []
    for index, (count, factor) in enumerate(layout):
        normal = jax.random.truncated_normal(jax.random.fold_in(key, index), -3.0, 3.0, (count,), jnp.float32)
        pieces.append(normal * factor)
    return jnp.concatenate(pieces).astype(jnp.float32)


def draw_vectors(key, part):
    key = jax.random.fold_in(key, 9)
    normal = jax.random.truncated_normal(jax.random.fold_in(key, 1), -3.0, 3.0, (14, D), jnp.float32)
    jitter = jax.random.uniform(jax.random.fold_in(key, 2), (14, D), jnp.float32, 0.8, 1.2)
    column = jnp.arange(D, dtype=jnp.int32).astype(jnp.float32)[None, :]
    rising = (0.6 + 1.2 * column / D) * jitter
    row = jnp.arange(14, dtype=jnp.int32)[:, None]
    is_gain = (row == 2) | (row == 7)
    is_token = row == 1
    value = jnp.where(is_gain, rising, jnp.where(is_token, normal, 0.3 * normal))
    return value.astype(jnp.float32)


def level_of(own_key, dims, shards, least, largest):
    def one(axis_at, shards_of):
        draws = jax.random.uniform(jax.random.fold_in(jax.random.fold_in(own_key, 6), axis_at), (shards_of,), jnp.float32, least / len(shards), largest / len(shards))
        return jnp.repeat(jnp.exp(draws), dims[axis_at] // shards_of).reshape((-1,) + (1,) * (len(dims) - axis_at - 1))

    factor_of = one(*shards[0])
    for cut in shards[1:]:
        factor_of = factor_of * one(*cut)
    return factor_of


def bell_draw(stream_key, extent, scale, reach, cuts=(), held_as=jnp.bfloat16):
    entries = jax.random.normal(stream_key, extent, jnp.float32) * scale
    if len(cuts) > 0:
        entries = level_of(stream_key, extent, cuts, -0.22, 0.18) * entries
    return jnp.clip(entries, min=-reach, max=reach).astype(held_as)


def setup_inputs(seed: int = 0) -> dict:
    streams_of = jax.random.split(jax.random.key(seed), 11)
    latents = bell_draw(streams_of[0], (IMAGES, KMAX, DIN), 1.0, 6.0, ((0, 16), (1, 2)))
    restore = draw_restore(jax.random.fold_in(streams_of[10], 71), 0)
    bucket = draw_bucket(jax.random.fold_in(streams_of[10], 71), 0)
    cotangent = bell_draw(streams_of[3], (IMAGES, SLOTS, D), 1.0, 6.0, ((0, 16), (1, 2)))
    flat_weights = draw_flat_weights(jax.random.fold_in(streams_of[10], 71), 0)
    flat_first = bell_draw(streams_of[5], (NPARAM,), (0.111 * (NPARAM + 14 * D) ** -0.5), 0.0008544922, ((0, 32),), jnp.float32)
    flat_second = jnp.clip(jnp.exp(math.log(5.9219786407993524e-08) - 1.3843913668352015 * jax.random.uniform(streams_of[6], (NPARAM,), jnp.float32) ** level_of(streams_of[6], (NPARAM,), ((0, 32),), -0.2, 0.2)), 1.483314715500228e-08, 5.9219786407993524e-08)
    vectors = draw_vectors(jax.random.fold_in(streams_of[10], 71), 0)
    vector_first = bell_draw(streams_of[8], (14, D), (0.444 * (NPARAM + 14 * D) ** -0.5), 0.0034179688, (), jnp.float32)
    vector_second = jnp.clip(jnp.exp(jax.random.uniform(streams_of[9], (14, D), jnp.float32, math.log(2.368791456319741e-07), math.log(9.587965905666351e-07))), 2.368791456319741e-07, 9.587965905666351e-07)
    return {"latents": latents, "restore": restore, "bucket": bucket, "cotangent": cotangent, "flat_weights": flat_weights, "flat_first": flat_first, "flat_second": flat_second, "vectors": vectors, "vector_first": vector_first, "vector_second": vector_second}


@jax.custom_vjp
def low(v):
    return lax.optimization_barrier(v.astype(jnp.bfloat16)).astype(jnp.float32)

@jax.custom_vjp
def low_back(v):
    return v

def low_keep(v):
    return (low(v), None)

def low_pass(kept, grad):
    return (grad,)

def back_keep(v):
    return (v, None)

def back_low(kept, grad):
    return (low(grad),)
low.defvjp(low_keep, low_pass)
low_back.defvjp(back_keep, back_low)
first_decay = 0.9
second_decay = 0.95
learn_rate = 0.05
vector_rate = 0.5
decay_weight = 0.05
adam_eps = 1e-08
clip_norm = 1.0

def matrix_product(form, left, right):
    return jnp.einsum(form, left, right, precision=lax.Precision.HIGHEST, preferred_element_type=jnp.float32)

def unpack(flat):
    shapes = [(DIN, D), (D, 3 * D), (D, D), (D, FF), (FF, D)]
    pieces = []
    offset = 0
    for height, width in shapes:
        pieces.append(flat[offset:offset + height * width].reshape(height, width))
        offset = offset + height * width
    return pieces

def image_lengths(bucket):
    return jnp.where(bucket == 0, SLOTS * 100 // 256, jnp.where(bucket == 1, SLOTS * 196 // 256, SLOTS)).astype(jnp.int32)

def positional_embedding_table():
    slot = jnp.arange(SLOTS, dtype=jnp.int32).astype(jnp.float32)[:, None]
    column = jnp.arange(D // 2, dtype=jnp.int32).astype(jnp.float32)[None, :]
    angle = slot * jnp.exp(-math.log(10000.0) * column / (D // 2))
    return jnp.concatenate([jnp.sin(angle), jnp.cos(angle)], axis=1)

def layer_norm(value, gain, shift):
    centred = value - lax.optimization_barrier(jnp.mean(value, axis=-1, keepdims=True))
    spread = lax.optimization_barrier(jnp.mean(centred * centred, axis=-1, keepdims=True))
    return centred * lax.rsqrt(spread + 1e-06) * gain + shift

def forward(flat, vectors, encoder_rows, restore_rows, length_rows):
    embedding_matrix, joint_weight, output_weight, expand_weight, reduce_weight = unpack(low(flat))
    count = encoder_rows.shape[0]
    embedded_rows = low(low_back(matrix_product('tqx,xj->tqj', encoder_rows, embedding_matrix) + vectors[0]))
    select_rows = (restore_rows[:, :, None] == jnp.arange(KMAX, dtype=jnp.int32)[None, None, :]).astype(jnp.float32)
    mask_token_rows = (restore_rows >= KMAX).astype(jnp.float32)[:, :, None]
    start_offset = matrix_product('ywq,yqj->ywj', select_rows, embedded_rows) + mask_token_rows * vectors[1] + positional_embedding_table()[None]
    normed = low(layer_norm(start_offset, vectors[2], vectors[3]))
    query = low(low_back(matrix_product('bsd,de->bse', normed, joint_weight[:, :D]) + vectors[4]))
    keys = low(low_back(matrix_product('bsd,de->bse', normed, joint_weight[:, D:2 * D])))
    values = low(low_back(matrix_product('bsd,de->bse', normed, joint_weight[:, 2 * D:]) + vectors[5]))
    query = query.reshape(count, SLOTS, HEADS, HD)
    keys = keys.reshape(count, SLOTS, HEADS, HD)
    values = values.reshape(count, SLOTS, HEADS, HD)
    scores = low_back(matrix_product('bqhe,bkhe->bhqk', query, keys)) * HD ** (-0.5)
    key_valid = jnp.arange(SLOTS, dtype=jnp.int32)[None, :] < length_rows[:, None]
    scores = jnp.where(key_valid[:, None, None, :], scores, -1e+30)
    probs = low(jax.nn.softmax(scores, axis=-1))
    mixed = low(low_back(matrix_product('bhqk,bkhe->bqhe', probs, values).reshape(count, SLOTS, D)))
    middle = start_offset + low_back(matrix_product('bsd,de->bse', mixed, output_weight) + vectors[6])
    normed_two = low(layer_norm(middle, vectors[7], vectors[8]))
    hidden = low_back(matrix_product('bsd,df->bsf', normed_two, expand_weight) + vectors[10:14].reshape(FF))
    active = low(jax.nn.gelu(hidden, approximate=False))
    return middle + low_back(matrix_product('bsf,fd->bsd', active, reduce_weight) + vectors[9])

def adam_update(grad, first, second, weight, rate, shrink):
    first_new = first_decay * first + (1.0 - first_decay) * grad
    second_new = second_decay * second + (1.0 - second_decay) * grad * grad
    first_hat = first_new / (1.0 - first_decay ** STEP)
    second_hat = second_new / (1.0 - second_decay ** STEP)
    weight_new = weight - rate * (first_hat / (jnp.sqrt(second_hat) + adam_eps) + shrink * weight)
    return (first_new, second_new, weight_new)

def reference(latents, restore, bucket, cotangent, flat_weights, flat_first, flat_second, vectors, vector_first, vector_second):
    lengths = image_lengths(bucket)
    group = math.gcd(IMAGES, max(1, 4096 // SLOTS))
    blocks = IMAGES // group

    def split(array):
        return array.reshape((blocks, group) + array.shape[1:])

    def one_group(carry, items):
        flat_sum, vector_sum = carry
        encoder_rows, restore_rows, length_rows, cot_rows = items
        row_valid = (jnp.arange(SLOTS, dtype=jnp.int32)[None, :] < length_rows[:, None]).astype(jnp.float32)[:, :, None]

        def run(weights, vecs, inputs):
            return forward(weights, vecs, inputs, restore_rows, length_rows)
        result, pull = jax.vjp(run, flat_weights, vectors, encoder_rows.astype(jnp.float32))
        flat_grad, vector_grad, latent_grad = pull(cot_rows.astype(jnp.float32) * row_valid)
        return ((flat_sum + flat_grad, vector_sum + vector_grad), (result, latent_grad))
    init = (jnp.zeros(flat_weights.shape, jnp.float32), jnp.zeros(vectors.shape, jnp.float32))
    (flat_grad, vector_grad), (result, latent_grad) = lax.scan(one_group, init, (split(latents), split(restore), split(lengths), split(cotangent)))
    block_out = result.reshape(IMAGES, SLOTS, D)
    latent_grad = latent_grad.reshape(IMAGES, KMAX, DIN)
    grad_norm = jnp.sqrt(jnp.sum(flat_grad * flat_grad) + jnp.sum(vector_grad * vector_grad))
    factor = jnp.minimum(1.0, clip_norm / (grad_norm + 1e-06))
    new_first, new_second, new_weights = adam_update(flat_grad * factor, flat_first, flat_second, flat_weights, learn_rate, decay_weight)
    vector_first_new, vector_second_new, vectors_new = adam_update(vector_grad * factor, vector_first, vector_second, vectors, vector_rate, 0.0)
    reduce_bias_grad = vector_grad[9] * factor
    return (block_out, latent_grad, new_first, new_second, new_weights, vector_first_new, vector_second_new, vectors_new, reduce_bias_grad, grad_norm)
```

```python
import math

import jax
import jax.numpy as jnp
from jax import lax
from jax.experimental import pallas as pl
from jax.experimental.pallas import tpu as pltpu
from jax.sharding import PartitionSpec as P

DIN = 768
D = 512
HEADS = 16
HD = 32
FF = 2048
SLOTS = 256
KMAX = 64
STEP = 10
NPARAM = 3538944

first_decay = 0.9
second_decay = 0.95
learn_rate = 0.05
vector_rate = 0.5
decay_weight = 0.05
adam_eps = 1e-08
clip_norm = 1.0

BF = jnp.bfloat16
F32 = jnp.float32

LANES = 128
LINES = NPARAM // LANES
EMBED_AT = 0
JOINT_AT = EMBED_AT + DIN * D // LANES
OUTPUT_AT = JOINT_AT + 3 * D * D // LANES
EXPAND_AT = OUTPUT_AT + D * D // LANES
REDUCE_AT = EXPAND_AT + D * FF // LANES
BLOCK = LINES // 32
HALF = 16 * BLOCK
FIRST_BLOCKS = -(-EXPAND_AT // BLOCK)
SECOND_FROM = EXPAND_AT // BLOCK
SECOND_BLOCKS = 32 - SECOND_FROM
TILE = 256
TILES = FF // TILE
GROUP = 4
GROUPS = HEADS // GROUP
MINE = 2
TOKENS = MINE * SLOTS
VMEM = pl.BlockSpec(memory_space=pltpu.VMEM)
SMEM = pl.BlockSpec(memory_space=pltpu.SMEM)
ANY = pl.BlockSpec(memory_space=pl.ANY)


def image_lengths(bucket):
    return jnp.where(
        bucket == 0, SLOTS * 100 // 256, jnp.where(bucket == 1, SLOTS * 196 // 256, SLOTS)
    ).astype(jnp.int32)


def position_rows(slot):
    column = jnp.arange(D // 2, dtype=jnp.int32).astype(F32)[None, :]
    angle = slot.astype(F32)[:, None] * jnp.exp(-math.log(10000.0) * column / (D // 2))
    return jnp.concatenate([jnp.sin(angle), jnp.cos(angle)], axis=1)


def adam_update(grad, first, second, weight, rate, shrink):
    first_new = first_decay * first + (1.0 - first_decay) * grad
    second_new = second_decay * second + (1.0 - second_decay) * grad * grad
    first_hat = first_new / (1.0 - first_decay**STEP)
    second_hat = second_new / (1.0 - second_decay**STEP)
    weight_new = weight - rate * (first_hat / (jnp.sqrt(second_hat) + adam_eps) + shrink * weight)
    return (first_new, second_new, weight_new)


def dot(left, right, over=(1, 0)):
    return lax.dot_general(
        left, right, (((over[0],), (over[1],)), ((), ())), preferred_element_type=F32
    )


def fetch_lines(table, pieces, lines, sem, low, high):
    span = pieces[0].shape[0]
    if len(pieces) == 1:
        pltpu.make_async_copy(
            pieces[0].at[pl.ds(low * BLOCK, (high - low) * BLOCK)], lines, sem
        ).start()
        return
    for index, piece in enumerate(pieces):
        block = table[index]

        @pl.when((block >= low) & (block < high))
        def _(piece=piece, block=block):
            at = pl.multiple_of((block - low) * span, 16)
            pltpu.make_async_copy(piece, lines.at[pl.ds(at, span)], sem).start()


def wait_lines(lines, sem):
    pltpu.make_async_copy(lines, lines, sem).wait()


def lines_to_matrix(lines, stage, matrix, at, rows, wide, batch):
    size = batch * wide

    def body(index, carry):
        for part in range(2):
            row = pl.multiple_of((2 * index + part) * batch, batch)
            source = pl.multiple_of(at + (2 * index + part) * size, 16)
            stage[part, :size, :] = lines[pl.ds(source, size), :].astype(F32)
            for j in range(wide):
                matrix[pl.ds(row, batch), j * LANES : (j + 1) * LANES] = stage[
                    part, pl.ds(j, batch, stride=wide), :
                ].astype(BF)
        return carry

    lax.fori_loop(0, rows // batch // 2, body, 0)


def norm_parts(value):
    centred = value - jnp.mean(value, axis=-1, keepdims=True)
    scale = lax.rsqrt(jnp.mean(centred * centred, axis=-1, keepdims=True) + 1e-06)
    return centred * scale, scale


def norm_back(grad, hat, scale, gain):
    inner = grad * gain
    return scale * (
        inner
        - jnp.mean(inner, axis=-1, keepdims=True)
        - hat * jnp.mean(inner * hat, axis=-1, keepdims=True)
    )


def total(value):
    return jnp.sum(value.astype(F32), axis=0, keepdims=True)


def slot_column(side):
    local = lax.broadcasted_iota(jnp.int32, (SLOTS, 1), 0)
    return (local + side * (SLOTS // 2)) & (SLOTS - 1)


def select_rows(restore, side):
    rows = (lax.broadcasted_iota(jnp.int32, (1, KMAX), 1) + side * (KMAX // 2)) & (KMAX - 1)
    return (restore == rows).astype(F32).astype(BF)


def head_mask(head):
    lane = lax.broadcasted_iota(jnp.int32, (1, LANES), 1)
    return (lane // HD) == head


def mask_head(value, head):
    return jnp.where(head_mask(head), value, jnp.zeros_like(value))


def forward_kernel(
    meta, table, latents, restore, position, vectors, *rest, pieces
):
    sources = rest[:pieces]
    (
        probs,
        joint,
        normed,
        start,
        middle,
        mixed,
        embed_w,
        joint_w,
        output_w,
        lines,
        stage,
        query_t,
        value_t,
        mixed_t,
        sem,
    ) = rest[pieces:]
    step = pl.program_id(0)
    side = meta[0]

    @pl.when(step == 0)
    def _():
        fetch_lines(table, sources, lines, sem, 0, FIRST_BLOCKS)
        wait_lines(lines, sem)
        lines_to_matrix(lines, stage, embed_w, EMBED_AT, DIN, 4, 128)
        lines_to_matrix(lines, stage, joint_w, JOINT_AT, D, 12, 64)
        lines_to_matrix(lines, stage, output_w, OUTPUT_AT, D, 4, 128)
        embedded = (dot(latents[...], embed_w[...]) + vectors[0:1, :]).astype(BF)
        for image in range(MINE):
            rows = slice(image * SLOTS, (image + 1) * SLOTS)
            picked = restore[rows, :]
            chosen = dot(
                select_rows(picked, side), embedded[image * KMAX : (image + 1) * KMAX, :]
            )
            value = (
                chosen + (picked >= KMAX).astype(F32) * vectors[1:2, :] + position[...]
            )
            start[rows, :] = value
            hat, _ = norm_parts(value)
            normed[rows, :] = (hat * vectors[2:3, :] + vectors[3:4, :]).astype(BF)
        for part, bias in enumerate((4, None, 5)):
            columns = slice(part * D, (part + 1) * D)
            out = dot(normed[...], joint_w[:, columns])
            if bias is not None:
                out = out + vectors[bias : bias + 1, :]
            joint[:, columns] = out.astype(BF)
        query_t[...] = joint[:, :D].T
        value_t[...] = joint[:, 2 * D :].T

    image = step // GROUPS
    group = step % GROUPS
    rows = pl.ds(pl.multiple_of(image * SLOTS, SLOTS), SLOTS)
    lanes = pl.ds(pl.multiple_of(group * LANES, LANES), LANES)
    keys = joint[rows, pl.ds(pl.multiple_of(D + group * LANES, LANES), LANES)]
    queries = query_t[lanes, rows]
    hidden_key = jnp.where(slot_column(side) < meta[1 + image], 0.0, -1e30)
    rate = HD**-0.5 * math.log2(math.e)
    for head in range(GROUP):
        scores = dot(mask_head(keys, head), queries) + hidden_key
        top = jnp.max(scores, axis=0, keepdims=True)
        raised = jnp.exp2((scores - top) * rate)
        low = (raised * (1.0 / jnp.sum(raised, axis=0, keepdims=True))).astype(BF)
        probs[head] = low
        features = pl.ds(pl.multiple_of(group * LANES + head * HD, HD), HD)
        mixed_t[features, rows] = dot(value_t[features, rows], low).astype(BF)

    @pl.when(step == MINE * GROUPS - 1)
    def _():
        mixed[...] = mixed_t[...].T
        middle[...] = start[...] + dot(mixed[...], output_w[...]) + vectors[6:7, :]


def forward_call(meta, table, latents, restore, position, vectors, sources):
    shape = jax.ShapeDtypeStruct
    count = len(sources)
    whole = lambda *dims: pl.BlockSpec(dims, lambda i: (0,) * len(dims))
    return pl.pallas_call(
        lambda *refs: forward_kernel(*refs, pieces=count),
        grid=(MINE * GROUPS,),
        in_specs=[SMEM, SMEM, VMEM, VMEM, VMEM, VMEM] + [ANY] * count,
        out_shape=(
            shape((MINE * HEADS, SLOTS, SLOTS), BF),
            shape((TOKENS, 3 * D), BF),
            shape((TOKENS, D), BF),
            shape((TOKENS, D), F32),
            shape((TOKENS, D), F32),
            shape((TOKENS, D), BF),
            shape((DIN, D), BF),
            shape((D, 3 * D), BF),
            shape((D, D), BF),
        ),
        out_specs=(
            pl.BlockSpec((GROUP, SLOTS, SLOTS), lambda i: (i, 0, 0)),
            whole(TOKENS, 3 * D),
            whole(TOKENS, D),
            whole(TOKENS, D),
            whole(TOKENS, D),
            whole(TOKENS, D),
            whole(DIN, D),
            whole(D, 3 * D),
            whole(D, D),
        ),
        scratch_shapes=[
            pltpu.VMEM((FIRST_BLOCKS * BLOCK, LANES), BF),
            pltpu.VMEM((2, 768, LANES), F32),
            pltpu.VMEM((D, TOKENS), BF),
            pltpu.VMEM((D, TOKENS), BF),
            pltpu.VMEM((D, TOKENS), BF),
            pltpu.SemaphoreType.DMA,
        ],
        compiler_params=pltpu.CompilerParams(vmem_limit_bytes=56 * 2**20),
        cost_estimate=pl.CostEstimate(
            flops=6 * 10**9, bytes_accessed=16 * 2**20, transcendentals=2 * 10**6
        ),
    )(meta, table, latents, restore, position, vectors, *sources)


def middle_kernel(meta, table, slots, middle, mixed, cotangent, output_w, vectors, *rest, pieces):
    sources = rest[:pieces]
    (
        own_out,
        far_out,
        back_middle,
        back_mixed,
        low_lines,
        far_lines,
        near_lines,
        rows_out,
        expand_out,
        lines,
        stage,
        expand_w,
        reduce_w,
        hat,
        scale,
        normed,
        normed_t,
        back_out,
        acc,
        acc_back,
        grads,
        out_grads,
        sem,
    ) = rest[pieces:]
    step = pl.program_id(0)
    side = meta[0]
    base = SECOND_FROM * BLOCK

    @pl.when(step == 0)
    def _():
        fetch_lines(table, sources, lines, sem, SECOND_FROM, 32)
        value, spread = norm_parts(middle[...])
        hat[...] = value
        scale[...] = spread
        normed[...] = (value * vectors[7:8, :] + vectors[8:9, :]).astype(BF)
        normed_t[...] = normed[...].T
        for image in range(MINE):
            rows = slice(image * SLOTS, (image + 1) * SLOTS)
            valid = slot_column(side) < meta[1 + image]
            back_out[rows, :] = jnp.where(valid, cotangent[rows, :].astype(F32), 0.0).astype(BF)
        acc[...] = jnp.zeros_like(acc)
        acc_back[...] = jnp.zeros_like(acc_back)
        wait_lines(lines, sem)
        lines_to_matrix(lines, stage, expand_w, EXPAND_AT - base, D, 16, 32)
        lines_to_matrix(lines, stage, reduce_w, REDUCE_AT - base, FF, 4, 128)

    columns = pl.ds(pl.multiple_of(step * TILE, TILE), TILE)
    expand = expand_w[:, columns]
    reduce = reduce_w[columns, :]
    bias = jnp.concatenate(
        [
            vectors[pl.ds(10 + step // 2, 1), pl.ds(pl.multiple_of((step % 2) * TILE, TILE), TILE)]
        ],
        axis=1,
    )
    hidden = dot(normed[...], expand) + bias
    density = jnp.exp(hidden * hidden * -0.5) * (1.0 / math.sqrt(2.0 * math.pi))
    below = 0.5 + 0.5 * lax.erf(hidden * math.sqrt(0.5))
    active = (hidden * below).astype(BF)
    back_active = dot(back_out[...], reduce, (1, 1))
    back_hidden = (back_active * (below + hidden * density)).astype(BF)
    acc[...] += dot(active, reduce)
    acc_back[...] += dot(back_hidden, expand, (1, 1))
    grad_reduce = dot(active, back_out[...], (0, 0))
    for j in range(4):
        grads[pl.ds(D * 16 + step * (TILE * 4) + j, TILE, stride=4), :] = grad_reduce[
            :, j * LANES : (j + 1) * LANES
        ]
    grad_expand = dot(normed_t[...], back_hidden)
    for j in range(TILE // LANES):
        grads[pl.ds(step * (TILE // LANES) + j, D, stride=16), :] = grad_expand[
            :, j * LANES : (j + 1) * LANES
        ]
    expand_out[pl.ds(step, 1), :] = total(back_hidden)

    @pl.when(step == TILES - 1)
    def _():
        for image in range(MINE):
            near = slice(image * SLOTS, image * SLOTS + SLOTS // 2)
            far = slice(image * SLOTS + SLOTS // 2, (image + 1) * SLOTS)
            own_out[image] = middle[near, :] + acc[near, :] + vectors[9:10, :]
            far_out[image] = (middle[far, :] + acc[far, :] + vectors[9:10, :]).astype(BF)
        grad = acc_back[...]
        rows_out[...] = jnp.zeros_like(rows_out)
        rows_out[1:2, :] = total(grad * hat[...])
        rows_out[2:3, :] = total(grad)
        rows_out[3:4, :] = total(back_out[...])
        back = back_out[...].astype(F32) + norm_back(grad, hat[...], scale[...], vectors[7:8, :])
        back_middle[...] = back
        branch = back.astype(BF)
        rows_out[0:1, :] = total(branch)
        back_mixed[...] = dot(branch, output_w[...], (1, 1)).astype(BF)
        grad_output = dot(mixed[...], branch, (0, 0))
        for j in range(4):
            out_grads[pl.ds(j, D, stride=4), :] = grad_output[:, j * LANES : (j + 1) * LANES]
        head = EXPAND_AT - OUTPUT_AT
        low_lines[:head, :] = out_grads[...].astype(BF)
        low_lines[head:, :] = grads[: HALF - EXPAND_AT, :].astype(BF)
        put_blocks(slots, far_lines, near_lines, lambda q: grads[pl.ds(HALF - EXPAND_AT + q * BLOCK, BLOCK), :].astype(BF))


def put_blocks(slots, far_lines, near_lines, block_of):
    def body(index, carry):
        slot = slots[index]
        value = block_of(index)

        @pl.when(slot < 8)
        def _():
            far_lines[pl.ds(pl.multiple_of(slot * BLOCK, 16), BLOCK), :] = value

        @pl.when(slot >= 8)
        def _():
            near_lines[pl.ds(pl.multiple_of((slot - 8) * BLOCK, 16), BLOCK), :] = value

        return carry

    lax.fori_loop(0, 16, body, 0)


def middle_call(meta, table, slots, middle, mixed, cotangent, output_w, vectors, sources):
    shape = jax.ShapeDtypeStruct
    count = len(sources)
    outs = (
        shape((MINE, SLOTS // 2, D), F32),
        shape((MINE, SLOTS // 2, D), BF),
        shape((TOKENS, D), F32),
        shape((TOKENS, D), BF),
        shape((HALF - OUTPUT_AT, LANES), BF),
        shape((8 * BLOCK, LANES), BF),
        shape((8 * BLOCK, LANES), BF),
        shape((8, D), F32),
        shape((TILES, TILE), F32),
    )
    return pl.pallas_call(
        lambda *refs: middle_kernel(*refs, pieces=count),
        grid=(TILES,),
        in_specs=[SMEM, SMEM, SMEM] + [VMEM] * 5 + [ANY] * count,
        out_shape=outs,
        out_specs=tuple(VMEM for _ in outs),
        scratch_shapes=[
            pltpu.VMEM((SECOND_BLOCKS * BLOCK, LANES), BF),
            pltpu.VMEM((2, 768, LANES), F32),
            pltpu.VMEM((D, FF), BF),
            pltpu.VMEM((FF, D), BF),
            pltpu.VMEM((TOKENS, D), F32),
            pltpu.VMEM((TOKENS, 1), F32),
            pltpu.VMEM((TOKENS, D), BF),
            pltpu.VMEM((D, TOKENS), BF),
            pltpu.VMEM((TOKENS, D), BF),
            pltpu.VMEM((TOKENS, D), F32),
            pltpu.VMEM((TOKENS, D), F32),
            pltpu.VMEM((2 * D * 16, LANES), F32),
            pltpu.VMEM((D * 4, LANES), F32),
            pltpu.SemaphoreType.DMA,
        ],
        compiler_params=pltpu.CompilerParams(vmem_limit_bytes=56 * 2**20),
        cost_estimate=pl.CostEstimate(
            flops=8 * 10**9, bytes_accessed=16 * 2**20, transcendentals=2 * 10**6
        ),
    )(meta, table, slots, middle, mixed, cotangent, output_w, vectors, *sources)


def backward_kernel(
    meta,
    slots,
    probs,
    joint,
    normed,
    start,
    back_middle,
    back_mixed,
    latents,
    restore,
    vectors,
    embed_w,
    joint_w,
    low_lines,
    far_lines,
    near_lines,
    rows_out,
    own_latent,
    far_latent,
    key_t,
    back_t,
    query_back_t,
    joint_back,
    grads,
):
    step = pl.program_id(0)
    side = meta[0]

    @pl.when(step == 0)
    def _():
        key_t[...] = joint[:, D : 2 * D].T
        back_t[...] = back_mixed[...].T

    image = step // GROUPS
    group = step % GROUPS
    rows = pl.ds(pl.multiple_of(image * SLOTS, SLOTS), SLOTS)
    lanes = pl.ds(pl.multiple_of(group * LANES, LANES), LANES)
    queries = joint[rows, lanes]
    values = joint[rows, pl.ds(pl.multiple_of(2 * D + group * LANES, LANES), LANES)]
    back = back_mixed[rows, lanes]
    back_lanes = back_t[lanes, rows]
    key_back = jnp.zeros((SLOTS, LANES), F32)
    value_back = jnp.zeros((SLOTS, LANES), F32)
    for head in range(GROUP):
        low = probs[head]
        wide = low.astype(F32)
        back_probs = dot(mask_head(values, head), back_lanes)
        pull = jnp.sum(wide * back_probs, axis=0, keepdims=True)
        score_back = (wide * (back_probs - pull) * HD**-0.5).astype(BF)
        value_back = value_back + dot(low, mask_head(back, head))
        key_back = key_back + dot(score_back, mask_head(queries, head))
        features = pl.ds(pl.multiple_of(group * LANES + head * HD, HD), HD)
        query_back_t[features, rows] = dot(key_t[features, rows], score_back).astype(BF)
    joint_back[rows, pl.ds(pl.multiple_of(D + group * LANES, LANES), LANES)] = key_back.astype(BF)
    joint_back[rows, pl.ds(pl.multiple_of(2 * D + group * LANES, LANES), LANES)] = (
        value_back.astype(BF)
    )

    @pl.when(step == MINE * GROUPS - 1)
    def _():
        joint_back[:, :D] = query_back_t[...].T
        rows_out[...] = jnp.zeros_like(rows_out)
        rows_out[4:5, :] = total(joint_back[:, :D])
        rows_out[5:6, :] = total(joint_back[:, 2 * D :])
        normed_t = normed[...].T
        for part in range(3):
            grad_joint = dot(normed_t, joint_back[:, part * D : (part + 1) * D])
            for j in range(4):
                grads[pl.ds(JOINT_AT + part * 4 + j, D, stride=12), :] = grad_joint[
                    :, j * LANES : (j + 1) * LANES
                ]
        grad = dot(joint_back[...], joint_w[...], (1, 1))
        hat, scale = norm_parts(start[...])
        rows_out[2:3, :] = total(grad * hat)
        rows_out[3:4, :] = total(grad)
        back_start = back_middle[...] + norm_back(grad, hat, scale, vectors[2:3, :])
        masked = (restore[...] >= KMAX).astype(F32)
        rows_out[1:2, :] = total(masked * back_start)
        low_start = back_start.astype(BF)
        picked = []
        for image_at in range(MINE):
            part = slice(image_at * SLOTS, (image_at + 1) * SLOTS)
            picked.append(
                dot(select_rows(restore[part, :], side), low_start[part, :], (0, 0)).astype(BF)
            )
        embedded_back = jnp.concatenate(picked, axis=0)
        rows_out[0:1, :] = total(embedded_back)
        grad_embed = dot(latents[...], embedded_back, (0, 0))
        for j in range(4):
            grads[pl.ds(EMBED_AT + j, DIN, stride=4), :] = grad_embed[:, j * LANES : (j + 1) * LANES]
        latent_back = dot(embedded_back, embed_w[...], (1, 1))
        for image_at in range(MINE):
            at = image_at * KMAX
            own_latent[image_at] = latent_back[at : at + KMAX // 2, :]
            far_latent[image_at] = latent_back[at + KMAX // 2 : at + KMAX, :].astype(BF)
        whole = OUTPUT_AT // BLOCK

        def block_of(index):
            return grads[pl.ds(index * BLOCK, BLOCK), :].astype(BF)

        put_low(slots, far_lines, near_lines, block_of, grads, low_lines, whole)


def put_low(slots, far_lines, near_lines, block_of, grads, low_lines, whole):
    def store(slot, value):
        @pl.when(slot < 8)
        def _():
            far_lines[pl.ds(pl.multiple_of(slot * BLOCK, 16), BLOCK), :] = value

        @pl.when(slot >= 8)
        def _():
            near_lines[pl.ds(pl.multiple_of((slot - 8) * BLOCK, 16), BLOCK), :] = value

    def early(index, carry):
        store(slots[index], block_of(index))
        return carry

    def late(index, carry):
        at = pl.multiple_of(index * BLOCK - OUTPUT_AT, 16)
        store(slots[index], low_lines[pl.ds(at, BLOCK), :])
        return carry

    lax.fori_loop(0, whole, early, 0)
    cut = OUTPUT_AT - whole * BLOCK
    store(
        slots[whole],
        jnp.concatenate(
            [grads[whole * BLOCK : OUTPUT_AT, :].astype(BF), low_lines[: BLOCK - cut, :]], axis=0
        ),
    )
    lax.fori_loop(whole + 1, 16, late, 0)


def backward_call(
    meta, slots, probs, joint, normed, start, back_middle, back_mixed, latents, restore, vectors,
    embed_w, joint_w, low_lines,
):
    shape = jax.ShapeDtypeStruct
    outs = (
        shape((8 * BLOCK, LANES), BF),
        shape((8 * BLOCK, LANES), BF),
        shape((8, D), F32),
        shape((MINE, KMAX // 2, DIN), F32),
        shape((MINE, KMAX // 2, DIN), BF),
    )
    return pl.pallas_call(
        backward_kernel,
        grid=(MINE * GROUPS,),
        in_specs=[SMEM, SMEM, pl.BlockSpec((GROUP, SLOTS, SLOTS), lambda i: (i, 0, 0))]
        + [VMEM] * 11,
        out_shape=outs,
        out_specs=tuple(VMEM for _ in outs),
        scratch_shapes=[
            pltpu.VMEM((D, TOKENS), BF),
            pltpu.VMEM((D, TOKENS), BF),
            pltpu.VMEM((D, TOKENS), BF),
            pltpu.VMEM((TOKENS, 3 * D), BF),
            pltpu.VMEM((OUTPUT_AT, LANES), F32),
        ],
        compiler_params=pltpu.CompilerParams(vmem_limit_bytes=56 * 2**20),
        cost_estimate=pl.CostEstimate(
            flops=8 * 10**9, bytes_accessed=16 * 2**20, transcendentals=10**5
        ),
    )(
        meta, slots, probs, joint, normed, start, back_middle, back_mixed, latents, restore,
        vectors, embed_w, joint_w, low_lines,
    )


class Grid:
    def __init__(self, mesh):
        self.axes = ("dp", "blk")
        self.count = mesh.shape["dp"] * mesh.shape["blk"]
        self.by_hand = self.count == 32 and mesh.shape["blk"] == 2

    def send(self, value, bits, other=None, only=None):
        other = bits if other is None else other
        pairs = [(i, i ^ (other if i & 2 else bits)) for i in range(self.count)]
        if only is not None:
            pairs = [(i, j) for i, j in pairs if (i & 16 == 0) == (only == 0)]
        return lax.ppermute(value, self.axes, pairs)

    def place(self):
        return (lax.axis_index("dp") * lax.axis_size("blk") + lax.axis_index("blk")).astype(
            jnp.int32
        )

    def gather(self, block):
        if not self.by_hand:
            whole = lax.all_gather(block, self.axes, axis=0, tiled=True)
            return [whole.reshape(LINES, LANES)], jnp.zeros((1,), jnp.int32)
        me = self.place()
        odd = (me >> 1) & 1
        held = {0: block}
        near, side, far = {}, {}, {}

        def plane(k):
            near[k] = self.send(held[k], 4, 1)
            side[k] = self.send(held[k], 1, 4)

        def corner(k):
            far[k] = self.send(near[k], 1, 4)

        held[16] = self.send(block, 16)
        plane(0)
        held[8] = self.send(block, 8)
        corner(0)
        plane(8)
        held[24] = self.send(held[16], 8)
        plane(16)
        corner(16)
        far[8] = self.send(far[0], 8)
        plane(24)
        far[24] = self.send(far[16], 8)
        pieces, table = [], []
        for k in (0, 8, 16, 24):
            for value, even, uneven in (
                (held[k], 0, 0),
                (near[k], 4, 1),
                (side[k], 1, 4),
                (far[k], 5, 5),
            ):
                pieces.append(value)
                table.append(me ^ k ^ jnp.where(odd == 0, even, uneven))
                pieces.append(self.send(value, 2))
                table.append(me ^ k ^ 2 ^ jnp.where(odd == 0, uneven, even))
        return pieces, jnp.stack(table).astype(jnp.int32)

    def slots(self):
        index = jnp.arange(16, dtype=jnp.int32)
        if not self.by_hand:
            return index
        me = self.place()
        rel = index ^ (me & 15)
        other = (rel >> 1) & 1
        odd = ((me >> 1) & 1) ^ other
        cross = rel & 5
        side = jnp.where(odd == 0, 1, 4)
        kind = jnp.where(cross == 5, 0, jnp.where(cross == 0, 3, jnp.where(cross == side, 1, 2)))
        return ((rel >> 3) * 4 + kind + jnp.where(other == 1, 0, 8)).astype(jnp.int32)

    def reduce_half(self, far_lines, near_lines, half):
        def add(left, right):
            return (left.astype(F32) + right.astype(F32)).astype(BF)

        both = add(near_lines, self.send(far_lines, 2)).reshape(2, 4, BLOCK, LANES)
        level = []
        for k in (1, 0):
            quarter = both[k]
            pair = add(quarter[2:], self.send(quarter[:2], 1, 4))
            level.append(add(pair[1], self.send(pair[0], 4, 1)))
        chip = add(level[1], self.send(level[0], 8))
        return chip.astype(F32) + self.send(chip, 16, only=1 - half).astype(F32)

    def sum_all(self, value):
        if not self.by_hand:
            return lax.psum(value, self.axes)
        for bits in (2, 1, 4, 8, 16):
            value = value + self.send(value, bits)
        return value


def local(
    grid,
    latents,
    restore,
    bucket,
    cotangent,
    flat_weights,
    flat_first,
    flat_second,
    vectors,
    vector_first,
    vector_second,
):
    me = grid.place()
    side = lax.axis_index("blk").astype(jnp.int32)
    swap = [(0, 1), (1, 0)]

    def mine(value):
        return lax.dynamic_slice_in_dim(value, side * MINE, MINE, axis=0)

    def trade(value):
        sent = lax.dynamic_slice_in_dim(value, (1 - side) * MINE, MINE, axis=0)
        return jnp.concatenate([mine(value), lax.ppermute(sent, "blk", swap)], axis=1)

    own_weights = flat_weights.reshape(-1, LANES)
    pieces, table = grid.gather(own_weights.astype(BF))
    slots = grid.slots()
    meta = jnp.concatenate([side[None], image_lengths(mine(bucket))]).astype(jnp.int32)
    my_latents = trade(latents).reshape(MINE * KMAX, DIN)
    my_restore = trade(restore).reshape(TOKENS, 1)
    my_cotangent = trade(cotangent).reshape(TOKENS, D)
    slot = (jnp.arange(SLOTS, dtype=jnp.int32) + side * (SLOTS // 2)) & (SLOTS - 1)
    position = position_rows(slot)

    probs, joint, normed, start, middle, mixed, embed_w, joint_w, output_w = forward_call(
        meta, table, my_latents, my_restore, position, vectors, pieces
    )
    (
        own_out, far_out, back_middle, back_mixed, low_lines, far_high, near_high, rows_b, expand_b,
    ) = middle_call(meta, table, slots, middle, mixed, my_cotangent, output_w, vectors, pieces)
    far_low, near_low, rows_c, own_latent, far_latent = backward_call(
        meta, slots, probs, joint, normed, start, back_middle, back_mixed, my_latents, my_restore,
        vectors, embed_w, joint_w, low_lines,
    )

    def join(own, far):
        other = lax.ppermute(far, "blk", swap).astype(F32)
        return jnp.where(
            side == 0,
            jnp.concatenate([own, other], axis=0),
            jnp.concatenate([other, own], axis=0),
        )

    block_out = join(own_out, far_out)
    latent_out = join(own_latent, far_latent)

    vector_sum = grid.sum_all(
        jnp.concatenate([rows_c[:6], rows_b[:4], expand_b.reshape(4, D)], axis=0)
    )
    if grid.by_hand:
        high = grid.reduce_half(far_high, near_high, 1)
        low = grid.reduce_half(far_low, near_low, 0)
        shard_grad = jnp.where(me & 16 == 0, low, high)
    else:
        flat = jnp.concatenate([far_low, near_low, far_high, near_high], axis=0).reshape(-1)
        shard_grad = lax.psum_scatter(
            flat, grid.axes, scatter_dimension=0, tiled=True
        ).astype(F32).reshape(-1, LANES)
    square_sum = grid.sum_all(jnp.sum(shard_grad * shard_grad))
    grad_norm = jnp.sqrt(square_sum + jnp.sum(vector_sum * vector_sum))
    factor = jnp.minimum(1.0, clip_norm / (grad_norm + 1e-06))
    new_first, new_second, new_weights = adam_update(
        shard_grad.reshape(-1) * factor,
        flat_first,
        flat_second,
        flat_weights,
        learn_rate,
        decay_weight,
    )
    vector_first_new, vector_second_new, vectors_new = adam_update(
        vector_sum * factor, vector_first, vector_second, vectors, vector_rate, 0.0
    )
    reduce_bias_grad = vector_sum[9] * factor
    return (
        block_out,
        latent_out,
        new_first,
        new_second,
        new_weights,
        vector_first_new,
        vector_second_new,
        vectors_new,
        reduce_bias_grad,
        grad_norm,
    )


def solution(mesh):
    grid = Grid(mesh)
    return jax.shard_map(
        lambda *args: local(grid, *args),
        mesh=mesh,
        in_specs=(
            P("dp", "blk", None),
            P("dp", "blk"),
            P("dp"),
            P("dp", "blk", None),
            P(("dp", "blk")),
            P(("dp", "blk")),
            P(("dp", "blk")),
            P(),
            P(),
            P(),
        ),
        out_specs=(
            P("dp", "blk", None),
            P("dp", "blk", None),
            P(("dp", "blk")),
            P(("dp", "blk")),
            P(("dp", "blk")),
            P(),
            P(),
            P(),
            P(),
            P(),
        ),
        check_vma=False,
    )
```

```python
import math

import jax
import jax.numpy as jnp
from jax import lax
from jax.experimental import pallas as pl
from jax.experimental.pallas import tpu as pltpu
from jax.sharding import PartitionSpec as P

DIN = 768
D = 512
HEADS = 16
HD = 32
FF = 2048
SLOTS = 256
KMAX = 64
STEP = 10
NPARAM = 3538944

first_decay = 0.9
second_decay = 0.95
learn_rate = 0.05
vector_rate = 0.5
decay_weight = 0.05
adam_eps = 1e-08
clip_norm = 1.0

BF = jnp.bfloat16
F32 = jnp.float32

LANES = 128
LINES = NPARAM // LANES
EMBED_AT = 0
JOINT_AT = EMBED_AT + DIN * D // LANES
OUTPUT_AT = JOINT_AT + 3 * D * D // LANES
EXPAND_AT = OUTPUT_AT + D * D // LANES
REDUCE_AT = EXPAND_AT + D * FF // LANES
BLOCK = LINES // 32
HALF = 16 * BLOCK
TAIL = 16
ROWS = 16
PART = BLOCK // 2
PARTS = (PART, PART + TAIL)
FIRST_BLOCKS = -(-EXPAND_AT // BLOCK)
SECOND_FROM = EXPAND_AT // BLOCK
SECOND_BLOCKS = 32 - SECOND_FROM
TILE = 256
TILES = FF // TILE
GROUP = 4
GROUPS = HEADS // GROUP
MINE = 2
TOKENS = MINE * SLOTS
PICKS = KMAX + 16
VMEM = pl.BlockSpec(memory_space=pltpu.VMEM)
SMEM = pl.BlockSpec(memory_space=pltpu.SMEM)
ANY = pl.BlockSpec(memory_space=pl.ANY)


def position_rows(slot):
    column = jnp.arange(D // 2, dtype=jnp.int32).astype(F32)[None, :]
    angle = slot.astype(F32)[:, None] * jnp.exp(-math.log(10000.0) * column / (D // 2))
    return jnp.concatenate([jnp.sin(angle), jnp.cos(angle)], axis=1)


def adam_update(grad, first, second, weight, rate, shrink):
    first_new = first_decay * first + (1.0 - first_decay) * grad
    second_new = second_decay * second + (1.0 - second_decay) * grad * grad
    first_hat = first_new / (1.0 - first_decay**STEP)
    second_hat = second_new / (1.0 - second_decay**STEP)
    weight_new = weight - rate * (first_hat / (jnp.sqrt(second_hat) + adam_eps) + shrink * weight)
    return (first_new, second_new, weight_new)


def dot(left, right, over=(1, 0)):
    return lax.dot_general(
        left, right, (((over[0],), (over[1],)), ((), ())), preferred_element_type=F32
    )


def place():
    return lax.axis_index("dp") * lax.axis_size("blk") + lax.axis_index("blk")


def fetch_lines(places, pieces, low_lines, high_lines, low_sem, high_sem):
    if places is None:
        for lines, low, sem in ((low_lines, 0, low_sem), (high_lines, SECOND_FROM, high_sem)):
            rows = pl.ds(low * BLOCK, lines.shape[0])
            pltpu.make_async_copy(pieces[0].at[rows], lines, sem).start()
            wait_lines(lines, sem)
        return
    me = place()
    odd = (me >> 1) & 1
    for (bits, even, uneven), piece in zip(places, pieces, strict=True):
        block = me ^ bits ^ jnp.where(odd == 0, even, uneven)

        @pl.when(block < FIRST_BLOCKS)
        def _(piece=piece, block=block):
            low_lines[pl.ds(pl.multiple_of(block * BLOCK, 16), BLOCK), :] = piece[...]

        @pl.when(block >= SECOND_FROM)
        def _(piece=piece, block=block):
            at = pl.multiple_of((block - SECOND_FROM) * BLOCK, 16)
            high_lines[pl.ds(at, BLOCK), :] = piece[...]


def wait_lines(lines, sem):
    pltpu.make_async_copy(lines, lines, sem).wait()


def lines_to_matrix(lines, stage, matrix, at, rows, wide, batch):
    size = batch * wide

    def body(index, carry):
        for part in range(2):
            row = pl.multiple_of((2 * index + part) * batch, batch)
            source = pl.multiple_of(at + (2 * index + part) * size, 16)
            stage[part, :size, :] = lines[pl.ds(source, size), :].astype(F32)
            for j in range(wide):
                matrix[pl.ds(row, batch), j * LANES : (j + 1) * LANES] = stage[
                    part, pl.ds(j, batch, stride=wide), :
                ].astype(BF)
        return carry

    lax.fori_loop(0, rows // batch // 2, body, 0)


def norm_parts(value):
    centred = value - jnp.mean(value, axis=-1, keepdims=True)
    scale = lax.rsqrt(jnp.mean(centred * centred, axis=-1, keepdims=True) + 1e-06)
    return centred * scale, scale


def norm_back(grad, hat, scale, gain):
    inner = grad * gain
    return scale * (
        inner
        - jnp.mean(inner, axis=-1, keepdims=True)
        - hat * jnp.mean(inner * hat, axis=-1, keepdims=True)
    )


def total(value):
    return jnp.sum(value.astype(F32), axis=0, keepdims=True)


def slot_column(side):
    local = lax.broadcasted_iota(jnp.int32, (SLOTS, 1), 0)
    return (local + side * (SLOTS // 2)) & (SLOTS - 1)


def image_length(bucket, image):
    kind = bucket[image]
    return jnp.where(
        kind == 0, SLOTS * 100 // 256, jnp.where(kind == 1, SLOTS * 196 // 256, SLOTS)
    )


def select_rows(own, far, image, side):
    half = SLOTS // 2
    row = lax.broadcasted_iota(jnp.int32, (PICKS, half), 0)
    row = jnp.where(row < KMAX, (row + side * (KMAX // 2)) & (KMAX - 1), row)
    parts = [
        (row == ref[pl.ds(image, 1), :]).astype(F32) for ref in (own, far)
    ]
    return jnp.concatenate(parts, axis=1).astype(BF)


def three_parts(value):
    high = value.astype(BF)
    rest = value - high.astype(F32)
    mid = rest.astype(BF)
    return high, mid, (rest - mid.astype(F32)).astype(BF)


def head_mask(head):
    lane = lax.broadcasted_iota(jnp.int32, (1, LANES), 1)
    return (lane // HD) == head


def mask_head(value, head):
    return jnp.where(head_mask(head), value, jnp.zeros_like(value))


def prepare_kernel(
    latents, far_latents, restore, far_restore, position, my_latents, choice, my_position,
    near_buffer, far_buffer, sem,
):
    side = lax.axis_index("blk")
    copies = []
    for index, (source, target) in enumerate(((latents, near_buffer), (far_latents, far_buffer))):
        copies.append(
            pltpu.make_async_copy(source.at[pl.ds(side * MINE, MINE)], target, sem.at[index])
        )
        copies[-1].start()
    my_position[...] = position[...]
    for image in range(MINE):
        choice[image] = select_rows(restore, far_restore, side * MINE + image, side)
    for copy in copies:
        copy.wait()
    half = KMAX // 2
    for image in range(MINE):
        at = image * KMAX
        my_latents[at : at + half, :] = near_buffer[image]
        my_latents[at + half : at + KMAX, :] = far_buffer[image]


def prepare_call(*operands):
    outs = (
        pltpu.VMEM((MINE * KMAX, DIN), BF),
        pltpu.VMEM((MINE, PICKS, SLOTS), BF),
        pltpu.VMEM((SLOTS, D), F32),
    )
    return pl.pallas_call(
        prepare_kernel,
        in_specs=[ANY, ANY, VMEM, VMEM, VMEM],
        out_shape=outs,
        out_specs=tuple(VMEM for _ in outs),
        scratch_shapes=[
            pltpu.VMEM((MINE, KMAX // 2, DIN), BF),
            pltpu.VMEM((MINE, KMAX // 2, DIN), BF),
            pltpu.SemaphoreType.DMA((2,)),
        ],
        compiler_params=pltpu.CompilerParams(vmem_limit_bytes=4 * 2**20),
        cost_estimate=pl.CostEstimate(flops=10**6, bytes_accessed=2**20, transcendentals=0),
    )(*operands)


def forward_kernel(bucket, my_latents, choice, position, vectors, *rest, places):
    pieces = len(rest) - 17
    sources = rest[:pieces]
    (
        probs,
        joint,
        normed,
        start,
        middle,
        mixed,
        embed_w,
        joint_w,
        output_w,
        high_lines,
        lines,
        stage,
        query_t,
        value_t,
        mixed_t,
        sem,
        high_sem,
    ) = rest[pieces:]
    step = pl.program_id(0)
    side = lax.axis_index("blk")

    @pl.when(step == 0)
    def _():
        fetch_lines(places, sources, lines, high_lines, sem, high_sem)
        lines_to_matrix(lines, stage, embed_w, EMBED_AT, DIN, 4, 128)
        lines_to_matrix(lines, stage, joint_w, JOINT_AT, D, 12, 64)
        lines_to_matrix(lines, stage, output_w, OUTPUT_AT, D, 4, 128)
        embedded = (dot(my_latents[...], embed_w[...]) + vectors[0:1, :]).astype(BF)
        token = list(three_parts(vectors[1:2, :]))
        for image in range(MINE):
            rows = slice(image * SLOTS, (image + 1) * SLOTS)
            picked = choice[image]
            value = dot(picked[:KMAX], embedded[image * KMAX : (image + 1) * KMAX, :], (0, 0))
            masked = jnp.broadcast_to(picked[KMAX : KMAX + 1], (16, SLOTS))
            table = jnp.concatenate(token + [jnp.zeros((13, D), BF)], axis=0)
            value = value + dot(masked, table, (0, 0)) + position[...]
            start[rows, :] = value
            hat, _ = norm_parts(value)
            normed[rows, :] = (hat * vectors[2:3, :] + vectors[3:4, :]).astype(BF)
        for part, bias in enumerate((4, None, 5)):
            columns = slice(part * D, (part + 1) * D)
            out = dot(normed[...], joint_w[:, columns])
            if bias is not None:
                out = out + vectors[bias : bias + 1, :]
            joint[:, columns] = out.astype(BF)
        query_t[...] = joint[:, :D].T
        value_t[...] = joint[:, 2 * D :].T

    image = step // GROUPS
    group = step % GROUPS
    rows = pl.ds(pl.multiple_of(image * SLOTS, SLOTS), SLOTS)
    lanes = pl.ds(pl.multiple_of(group * LANES, LANES), LANES)
    keys = joint[rows, pl.ds(pl.multiple_of(D + group * LANES, LANES), LANES)]
    queries = query_t[lanes, rows]
    length = image_length(bucket, side * MINE + image)
    hidden_key = jnp.where(slot_column(side) < length, 0.0, -1e30)
    rate = HD**-0.5 * math.log2(math.e)
    for head in range(GROUP):
        scores = dot(mask_head(keys, head), queries) + hidden_key
        top = jnp.max(scores, axis=0, keepdims=True)
        raised = jnp.exp2((scores - top) * rate)
        low = (raised * (1.0 / jnp.sum(raised, axis=0, keepdims=True))).astype(BF)
        probs[step * GROUP + head] = low
        features = pl.ds(pl.multiple_of(group * LANES + head * HD, HD), HD)
        mixed_t[features, rows] = dot(value_t[features, rows], low).astype(BF)

    @pl.when(step == MINE * GROUPS - 1)
    def _():
        mixed[...] = mixed_t[...].T
        middle[...] = start[...] + dot(mixed[...], output_w[...]) + vectors[6:7, :]


def forward_call(bucket, my_latents, choice, position, vectors, sources, places):
    outs = (
        pltpu.VMEM((MINE * HEADS, SLOTS, SLOTS), BF),
        pltpu.VMEM((TOKENS, 3 * D), BF),
        pltpu.VMEM((TOKENS, D), BF),
        pltpu.VMEM((TOKENS, D), F32),
        pltpu.VMEM((TOKENS, D), F32),
        pltpu.VMEM((TOKENS, D), BF),
        pltpu.VMEM((DIN, D), BF),
        pltpu.VMEM((D, 3 * D), BF),
        pltpu.VMEM((D, D), BF),
        pltpu.VMEM((SECOND_BLOCKS * BLOCK, LANES), BF),
    )
    return pl.pallas_call(
        lambda *refs: forward_kernel(*refs, places=places),
        grid=(MINE * GROUPS,),
        in_specs=[SMEM] + [VMEM] * 4 + [VMEM if places else ANY] * len(sources),
        out_shape=outs,
        out_specs=tuple(VMEM for _ in outs),
        scratch_shapes=[
            pltpu.VMEM((FIRST_BLOCKS * BLOCK, LANES), BF),
            pltpu.VMEM((2, 768, LANES), F32),
            pltpu.VMEM((D, TOKENS), BF),
            pltpu.VMEM((D, TOKENS), BF),
            pltpu.VMEM((D, TOKENS), BF),
            pltpu.SemaphoreType.DMA,
            pltpu.SemaphoreType.DMA,
        ],
        compiler_params=pltpu.CompilerParams(vmem_limit_bytes=16 * 2**20),
        cost_estimate=pl.CostEstimate(
            flops=6 * 10**9, bytes_accessed=16 * 2**20, transcendentals=2 * 10**6
        ),
    )(bucket, my_latents, choice, position, vectors, *sources)


def middle_kernel(
    by_hand, bucket, middle, cotangent, far_cotangent, vectors, lines, *rest
):
    (
        own_out,
        far_out,
        hat,
        scale,
        back_out,
        acc_back,
        head_lines,
        far_lines,
        near_lines,
        expand_out,
        stage,
        expand_w,
        reduce_w,
        normed,
        normed_t,
        acc,
        grads,
    ) = rest
    step = pl.program_id(0)
    side = lax.axis_index("blk")
    base = SECOND_FROM * BLOCK

    @pl.when(step == 0)
    def _():
        value, spread = norm_parts(middle[...])
        hat[...] = value
        scale[...] = jnp.broadcast_to(spread, scale.shape)
        normed[...] = (value * vectors[7:8, :] + vectors[8:9, :]).astype(BF)
        normed_t[...] = normed[...].T
        for image in range(MINE):
            valid = slot_column(side) < image_length(bucket, side * MINE + image)
            half = SLOTS // 2
            for part, ref in enumerate((cotangent, far_cotangent)):
                at = image * SLOTS + part * half
                back_out[at : at + half, :] = jnp.where(
                    valid[part * half : (part + 1) * half, :],
                    ref[side * MINE + image].astype(F32),
                    0.0,
                ).astype(BF)
        acc[...] = jnp.zeros_like(acc)
        acc_back[...] = jnp.zeros_like(acc_back)
        lines_to_matrix(lines, stage, expand_w, EXPAND_AT - base, D, 16, 32)
        lines_to_matrix(lines, stage, reduce_w, REDUCE_AT - base, FF, 4, 128)

    columns = pl.ds(pl.multiple_of(step * TILE, TILE), TILE)
    expand = expand_w[:, columns]
    reduce = reduce_w[columns, :]
    bias = vectors[pl.ds(10 + step // 2, 1), pl.ds(pl.multiple_of((step % 2) * TILE, TILE), TILE)]
    hidden = dot(normed[...], expand) + bias
    density = jnp.exp(hidden * hidden * -0.5) * (1.0 / math.sqrt(2.0 * math.pi))
    below = 0.5 + 0.5 * lax.erf(hidden * math.sqrt(0.5))
    active = (hidden * below).astype(BF)
    back_active = dot(back_out[...], reduce, (1, 1))
    back_hidden = (back_active * (below + hidden * density)).astype(BF)
    acc[...] += dot(active, reduce)
    acc_back[...] += dot(back_hidden, expand, (1, 1))
    grad_reduce = dot(active, back_out[...], (0, 0))
    for j in range(4):
        grads[pl.ds(D * 16 + step * (TILE * 4) + j, TILE, stride=4), :] = grad_reduce[
            :, j * LANES : (j + 1) * LANES
        ]
    grad_expand = dot(normed_t[...], back_hidden)
    for j in range(TILE // LANES):
        grads[pl.ds(step * (TILE // LANES) + j, D, stride=16), :] = grad_expand[
            :, j * LANES : (j + 1) * LANES
        ]
    expand_out[pl.ds(step, 1), :] = total(back_hidden)

    @pl.when(step == TILES - 1)
    def _():
        for image in range(MINE):
            near = slice(image * SLOTS, image * SLOTS + SLOTS // 2)
            far = slice(image * SLOTS + SLOTS // 2, (image + 1) * SLOTS)
            own_out[image] = middle[near, :] + acc[near, :] + vectors[9:10, :]
            far_out[image] = (middle[far, :] + acc[far, :] + vectors[9:10, :]).astype(BF)
        cut = HALF - EXPAND_AT
        head_lines[...] = grads[:cut, :].astype(BF)
        put_blocks(
            by_hand,
            far_lines,
            near_lines,
            lambda q: grads[pl.ds(cut + q * BLOCK, BLOCK), :].astype(BF),
        )


def slot_of(index, by_hand):
    if not by_hand:
        return index
    me = place()
    rel = index ^ (me & 15)
    other = (rel >> 1) & 1
    odd = ((me >> 1) & 1) ^ other
    along_y, along_x, along_z = rel & 1, (rel >> 2) & 1, rel >> 3
    first = jnp.where(odd == 0, along_y, along_x)
    second = jnp.where(odd == 0, along_x, along_y)
    slot = (1 - first) * 4 + (1 - second) * 2 + (1 - along_z)
    return slot + jnp.where(other == 1, 0, 8)


def put_blocks(by_hand, far_lines, near_lines, block_of):
    def body(index, carry):
        slot = slot_of(index, by_hand)
        value = block_of(index)

        @pl.when(slot < 8)
        def _():
            far_lines[pl.ds(pl.multiple_of(slot * BLOCK, 16), BLOCK), :] = value

        @pl.when(slot >= 8)
        def _():
            near_lines[pl.ds(pl.multiple_of((slot - 8) * BLOCK, 16), BLOCK), :] = value

        return carry

    lax.fori_loop(0, 16, body, 0)


def middle_call(by_hand, *operands):
    outs = (
        pltpu.VMEM((MINE, SLOTS // 2, D), F32),
        jax.ShapeDtypeStruct((MINE, SLOTS // 2, D), BF),
        pltpu.VMEM((TOKENS, D), F32),
        pltpu.VMEM((TOKENS, LANES), F32),
        pltpu.VMEM((TOKENS, D), BF),
        pltpu.VMEM((TOKENS, D), F32),
        pltpu.VMEM((HALF - EXPAND_AT, LANES), BF),
        pltpu.VMEM((8 * BLOCK, LANES), BF),
        pltpu.VMEM((8 * BLOCK, LANES), BF),
        pltpu.VMEM((TILES, TILE), F32),
    )
    return pl.pallas_call(
        lambda *refs: middle_kernel(by_hand, *refs),
        grid=(TILES,),
        in_specs=[SMEM] + [VMEM] * (len(operands) - 1),
        out_shape=outs,
        out_specs=tuple(VMEM for _ in outs),
        scratch_shapes=[
            pltpu.VMEM((2, 768, LANES), F32),
            pltpu.VMEM((D, FF), BF),
            pltpu.VMEM((FF, D), BF),
            pltpu.VMEM((TOKENS, D), BF),
            pltpu.VMEM((D, TOKENS), BF),
            pltpu.VMEM((TOKENS, D), F32),
            pltpu.VMEM((2 * D * 16, LANES), F32),
        ],
        compiler_params=pltpu.CompilerParams(vmem_limit_bytes=24 * 2**20),
        cost_estimate=pl.CostEstimate(
            flops=8 * 10**9, bytes_accessed=16 * 2**20, transcendentals=2 * 10**6
        ),
    )(*operands)


def branch_kernel(
    hat, scale, back_out, acc_back, mixed, output_w, vectors,
    back_middle, back_mixed, out_lines, rows_out, out_grads,
):
    grad = acc_back[...]
    rows_out[...] = jnp.zeros_like(rows_out)
    rows_out[1:2, :] = total(grad * hat[...])
    rows_out[2:3, :] = total(grad)
    rows_out[3:4, :] = total(back_out[...])
    back = back_out[...].astype(F32) + norm_back(
        grad, hat[...], scale[:, :1], vectors[7:8, :]
    )
    back_middle[...] = back
    branch = back.astype(BF)
    rows_out[0:1, :] = total(branch)
    back_mixed[...] = dot(branch, output_w[...], (1, 1)).astype(BF)
    grad_output = dot(mixed[...], branch, (0, 0))
    for j in range(4):
        out_grads[pl.ds(j, D, stride=4), :] = grad_output[:, j * LANES : (j + 1) * LANES]
    out_lines[...] = out_grads[...].astype(BF)


def branch_call(hat, scale, back_out, acc_back, mixed, output_w, vectors):
    outs = (
        pltpu.VMEM((TOKENS, D), F32),
        pltpu.VMEM((TOKENS, D), BF),
        pltpu.VMEM((EXPAND_AT - OUTPUT_AT, LANES), BF),
        pltpu.VMEM((8, D), F32),
    )
    return pl.pallas_call(
        branch_kernel,
        in_specs=[VMEM] * 7,
        out_shape=outs,
        out_specs=tuple(VMEM for _ in outs),
        scratch_shapes=[pltpu.VMEM((D * 4, LANES), F32)],
        compiler_params=pltpu.CompilerParams(vmem_limit_bytes=16 * 2**20),
        cost_estimate=pl.CostEstimate(
            flops=2 * 10**9, bytes_accessed=4 * 2**20, transcendentals=0
        ),
    )(hat, scale, back_out, acc_back, mixed, output_w, vectors)


def attention_back_kernel(
    probs, joint, back_mixed, joint_back, key_t, back_t, query_back_t
):
    step = pl.program_id(0)

    @pl.when(step == 0)
    def _():
        key_t[...] = joint[:, D : 2 * D].T
        back_t[...] = back_mixed[...].T

    image = step // GROUPS
    group = step % GROUPS
    rows = pl.ds(pl.multiple_of(image * SLOTS, SLOTS), SLOTS)
    lanes = pl.ds(pl.multiple_of(group * LANES, LANES), LANES)
    queries = joint[rows, lanes]
    values = joint[rows, pl.ds(pl.multiple_of(2 * D + group * LANES, LANES), LANES)]
    back = back_mixed[rows, lanes]
    back_lanes = back_t[lanes, rows]
    key_back = jnp.zeros((SLOTS, LANES), F32)
    value_back = jnp.zeros((SLOTS, LANES), F32)
    for head in range(GROUP):
        low = probs[step * GROUP + head]
        wide = low.astype(F32)
        back_probs = dot(mask_head(values, head), back_lanes)
        pull = jnp.sum(wide * back_probs, axis=0, keepdims=True)
        score_back = (wide * (back_probs - pull) * HD**-0.5).astype(BF)
        value_back = value_back + dot(low, mask_head(back, head))
        key_back = key_back + dot(score_back, mask_head(queries, head))
        features = pl.ds(pl.multiple_of(group * LANES + head * HD, HD), HD)
        query_back_t[features, rows] = dot(key_t[features, rows], score_back).astype(BF)
    joint_back[rows, pl.ds(pl.multiple_of(D + group * LANES, LANES), LANES)] = key_back.astype(BF)
    joint_back[rows, pl.ds(pl.multiple_of(2 * D + group * LANES, LANES), LANES)] = (
        value_back.astype(BF)
    )

    @pl.when(step == MINE * GROUPS - 1)
    def _():
        joint_back[:, :D] = query_back_t[...].T


def attention_back_call(probs, joint, back_mixed):
    return pl.pallas_call(
        attention_back_kernel,
        grid=(MINE * GROUPS,),
        in_specs=[VMEM] * 3,
        out_shape=pltpu.VMEM((TOKENS, 3 * D), BF),
        out_specs=VMEM,
        scratch_shapes=[
            pltpu.VMEM((D, TOKENS), BF),
            pltpu.VMEM((D, TOKENS), BF),
            pltpu.VMEM((D, TOKENS), BF),
        ],
        compiler_params=pltpu.CompilerParams(vmem_limit_bytes=16 * 2**20),
        cost_estimate=pl.CostEstimate(
            flops=8 * 10**9, bytes_accessed=4 * 2**20, transcendentals=0
        ),
    )(probs, joint, back_mixed)


def input_back_kernel(
    by_hand,
    joint_back,
    normed,
    start,
    back_middle,
    my_latents,
    choices,
    vectors,
    embed_w,
    joint_w,
    out_lines,
    head_lines,
    rows_in,
    expand_in,
    far_first,
    near_first,
    far_second,
    near_second,
    rows_out,
    own_latent,
    far_latent,
    grads,
    tails,
):
    rows_out[...] = jnp.zeros_like(rows_out)
    rows_out[4:5, :] = total(joint_back[:, :D])
    rows_out[5:6, :] = total(joint_back[:, 2 * D :])
    normed_t = normed[...].T
    for part in range(3):
        grad_joint = dot(normed_t, joint_back[:, part * D : (part + 1) * D])
        for j in range(4):
            grads[pl.ds(JOINT_AT + part * 4 + j, D, stride=12), :] = grad_joint[
                :, j * LANES : (j + 1) * LANES
            ]
    grad = dot(joint_back[...], joint_w[...], (1, 1))
    hat, scale = norm_parts(start[...])
    rows_out[2:3, :] = total(grad * hat)
    rows_out[3:4, :] = total(grad)
    back_start = back_middle[...] + norm_back(grad, hat, scale, vectors[2:3, :])
    low_start = back_start.astype(BF)
    low_rest = (back_start - low_start.astype(F32)).astype(BF)
    picked = []
    token_back = jnp.zeros((1, D), F32)
    for image in range(MINE):
        part = slice(image * SLOTS, (image + 1) * SLOTS)
        choice = choices[image]
        chosen = dot(choice, low_start[part, :])
        picked.append(chosen[:KMAX, :].astype(BF))
        token_back = token_back + chosen[KMAX : KMAX + 1, :]
        token_back = token_back + dot(choice[KMAX:, :], low_rest[part, :])[:1, :]
    rows_out[1:2, :] = token_back
    embedded_back = jnp.concatenate(picked, axis=0)
    rows_out[0:1, :] = total(embedded_back)
    grad_embed = dot(my_latents[...], embedded_back, (0, 0))
    for j in range(4):
        grads[pl.ds(EMBED_AT + j, DIN, stride=4), :] = grad_embed[:, j * LANES : (j + 1) * LANES]
    latent_back = dot(embedded_back, embed_w[...], (1, 1))
    for image in range(MINE):
        at = image * KMAX
        own_latent[image] = latent_back[at : at + KMAX // 2, :]
        far_latent[image] = latent_back[at + KMAX // 2 : at + KMAX, :].astype(BF)
    rows_out[6:10, :] = rows_in[0:4, :]
    for j in range(4):
        rows_out[10 + j : 11 + j, :TILE] = expand_in[2 * j : 2 * j + 1, :]
        rows_out[10 + j : 11 + j, TILE:] = expand_in[2 * j + 1 : 2 * j + 2, :]
    tails[...] = jnp.zeros_like(tails)
    for row in range(ROWS):
        for j in range(D // LANES):
            tails[row * TAIL + j : row * TAIL + j + 1, :] = rows_out[
                row : row + 1, j * LANES : (j + 1) * LANES
            ]

    def store(index, value):
        slot = slot_of(index, by_hand)
        tail = tails[pl.ds(pl.multiple_of(index * TAIL, TAIL), TAIL), :].astype(BF)

        def put(first, second, at):
            first[pl.ds(pl.multiple_of(at * PART, 16), PART), :] = value[:PART]
            row = pl.multiple_of(at * PARTS[1], 16)
            second[pl.ds(row, PART), :] = value[PART:]
            second[pl.ds(row + PART, TAIL), :] = tail

        @pl.when(slot < 8)
        def _():
            put(far_first, far_second, slot)

        @pl.when(slot >= 8)
        def _():
            put(near_first, near_second, slot - 8)

    first = OUTPUT_AT // BLOCK
    last = -(-EXPAND_AT // BLOCK)

    def early(index, carry):
        store(index, grads[pl.ds(pl.multiple_of(index * BLOCK, 16), BLOCK), :].astype(BF))
        return carry

    def late(index, carry):
        at = pl.multiple_of(index * BLOCK - EXPAND_AT, 16)
        store(index, head_lines[pl.ds(at, BLOCK), :])
        return carry

    lax.fori_loop(0, first, early, 0)
    for index in range(first, last):
        low, high = index * BLOCK, (index + 1) * BLOCK
        parts = []
        if low < OUTPUT_AT:
            parts.append(grads[low:OUTPUT_AT, :].astype(BF))
        parts.append(out_lines[max(low - OUTPUT_AT, 0) : min(high, EXPAND_AT) - OUTPUT_AT, :])
        if high > EXPAND_AT:
            parts.append(head_lines[: high - EXPAND_AT, :])
        store(index, jnp.concatenate(parts, axis=0) if len(parts) > 1 else parts[0])
    lax.fori_loop(last, 16, late, 0)


def input_back_call(by_hand, *operands):
    shape = jax.ShapeDtypeStruct
    outs = (
        pltpu.VMEM((8 * PARTS[0], LANES), BF),
        pltpu.VMEM((8 * PARTS[0], LANES), BF),
        pltpu.VMEM((8 * PARTS[1], LANES), BF),
        pltpu.VMEM((8 * PARTS[1], LANES), BF),
        shape((ROWS, D), F32),
        pltpu.VMEM((MINE, KMAX // 2, DIN), F32),
        shape((MINE, KMAX // 2, DIN), BF),
    )
    return pl.pallas_call(
        lambda *refs: input_back_kernel(by_hand, *refs),
        in_specs=[VMEM] * len(operands),
        out_shape=outs,
        out_specs=tuple(VMEM for _ in outs),
        scratch_shapes=[
            pltpu.VMEM((OUTPUT_AT, LANES), F32),
            pltpu.VMEM((ROWS * TAIL, LANES), F32),
        ],
        compiler_params=pltpu.CompilerParams(vmem_limit_bytes=24 * 2**20),
        cost_estimate=pl.CostEstimate(
            flops=4 * 10**9, bytes_accessed=8 * 2**20, transcendentals=0
        ),
    )(*operands)


class Grid:
    def __init__(self, mesh):
        self.axes = ("dp", "blk")
        self.count = mesh.shape["dp"] * mesh.shape["blk"]
        self.by_hand = self.count == 32 and mesh.shape["blk"] == 2

    def send(self, value, bits, other=None, only=None):
        other = bits if other is None else other
        pairs = [(i, i ^ (other if i & 2 else bits)) for i in range(self.count)]
        if only is not None:
            pairs = [(i, j) for i, j in pairs if (i & 16 == 0) == (only == 0)]
        return lax.ppermute(value, self.axes, pairs)

    def gather(self, block):
        if not self.by_hand:
            whole = lax.all_gather(block, self.axes, axis=0, tiled=True)
            return [whole.reshape(LINES, LANES)], None
        held = {0: block}
        near, side, far = {}, {}, {}

        def plane(k):
            near[k] = self.send(held[k], 4, 1)
            side[k] = self.send(held[k], 1, 4)

        def corner(k):
            far[k] = self.send(near[k], 1, 4)

        held[16] = self.send(block, 16)
        plane(0)
        held[8] = self.send(block, 8)
        corner(0)
        plane(8)
        held[24] = self.send(held[16], 8)
        plane(16)
        corner(16)
        far[8] = self.send(far[0], 8)
        plane(24)
        far[24] = self.send(far[16], 8)
        pieces, places = [], []
        for k in (0, 8, 16, 24):
            for value, even, uneven in (
                (held[k], 0, 0),
                (near[k], 4, 1),
                (side[k], 1, 4),
                (far[k], 5, 5),
            ):
                pieces.append(value)
                places.append((k, even, uneven))
                pieces.append(self.send(value, 2))
                places.append((k ^ 2, uneven, even))
        return [in_vmem(piece) for piece in pieces], tuple(places)


def add_call(rows, *terms):
    def kernel(*refs):
        out = refs[-1]
        value = None
        for ref, (_, at) in zip(refs[:-1], terms, strict=True):
            part = ref[at : at + rows, :].astype(F32)
            value = part if value is None else value + part
        out[...] = value.astype(BF)

    return pl.pallas_call(
        kernel,
        in_specs=[VMEM] * len(terms),
        out_shape=pltpu.VMEM((rows, LANES), BF),
        out_specs=VMEM,
        compiler_params=pltpu.CompilerParams(vmem_limit_bytes=4 * 2**20),
        cost_estimate=pl.CostEstimate(flops=10**5, bytes_accessed=2**20, transcendentals=0),
    )(*(in_vmem(array) for array, _ in terms))


def in_vmem(value):
    return pltpu.with_memory_space_constraint(value, pltpu.VMEM)


class Reduction:
    HOPS = ((2, 2), (1, 4), (4, 1), (8, 8))

    def __init__(self, grid, far_lines, near_lines, half):
        self.grid = grid
        self.near = near_lines
        self.half = half
        self.rows = far_lines.shape[0] // 8
        self.head = far_lines
        self.came = []

    def hop(self, *behind):
        step = len(self.came)
        self.came.append(self.grid.send(self.head, *self.HOPS[step]))
        left = 8 >> (step + 1)
        count = max(left, 1) if step < 3 else 1
        begin = 8 - 2 * left if step < 3 else 7
        terms = [(after(self.near, *behind), begin * self.rows)]
        for level, value in enumerate(self.came):
            terms.append((value, (begin - (8 - (8 >> level))) * self.rows))
        self.head = add_call(count * self.rows, *terms)
        return self.head

    def last(self):
        self.across = self.grid.send(self.head, 16, only=1 - self.half)


def finish_kernel(high, high_far, one, one_far, two, two_far, grad, notes):
    lower = (place() & 16) == 0

    def both(near, far):
        return near[...].astype(F32) + far[...].astype(F32)

    low_one, low_two, upper = both(one, one_far), both(two, two_far), both(high, high_far)
    grad[:PART, :] = jnp.where(lower, low_one, upper[:PART])
    grad[PART:, :] = jnp.where(lower, low_two[:PART], upper[PART:])
    row = jnp.where(lower, low_two[PART:], 0.0)
    value = grad[...]
    square = jnp.sum(jnp.sum(value * value, axis=0, keepdims=True), axis=1, keepdims=True)
    square = square + jnp.sum(jnp.sum(row * row, axis=0, keepdims=True), axis=1, keepdims=True)
    line = lax.broadcasted_iota(jnp.int32, (8, LANES), 0)
    note = jnp.where(line < 4, row[:8], square)
    for device in range(notes.shape[0]):
        notes[device] = note


def finish_call(count, *operands):
    outs = (pltpu.VMEM((BLOCK, LANES), F32), pltpu.VMEM((count, 8, LANES), F32))
    return pl.pallas_call(
        finish_kernel,
        in_specs=[VMEM] * len(operands),
        out_shape=outs,
        out_specs=tuple(VMEM for _ in outs),
        compiler_params=pltpu.CompilerParams(vmem_limit_bytes=8 * 2**20),
        cost_estimate=pl.CostEstimate(flops=10**6, bytes_accessed=2**20, transcendentals=0),
    )(*(in_vmem(value) for value in operands))


def update_kernel(
    grad, notes, first, second, weights, vectors, vector_first, vector_second,
    first_out, second_out, weights_out, vectors_first_out, vectors_second_out, vectors_out,
    bias_out, norm_out, sums,
):
    square = jnp.sum(notes[:, 4, :], axis=0, keepdims=True)
    norm = jnp.sqrt(square)
    factor = jnp.minimum(1.0, clip_norm / (norm + 1e-06))
    norm_out[...] = norm
    for row in range(sums.shape[0]):
        for j in range(D // LANES):
            sums[row : row + 1, j * LANES : (j + 1) * LANES] = notes[row, j : j + 1, :]
    first_out[...], second_out[...], weights_out[...] = adam_update(
        grad[...] * factor, first[...], second[...], weights[...], learn_rate, decay_weight
    )
    clipped = sums[...] * jnp.concatenate([factor] * (D // LANES), axis=1)
    bias_out[...] = clipped[9:10, :]
    vectors_first_out[...], vectors_second_out[...], vectors_out[...] = adam_update(
        clipped, vector_first[...], vector_second[...], vectors[...], vector_rate, 0.0
    )


def update_call(*operands):
    shape = jax.ShapeDtypeStruct
    lines, rows = operands[2].shape, operands[5].shape
    outs = (
        [shape(lines, F32)] * 3
        + [shape(rows, F32)] * 3
        + [shape((1, rows[1]), F32), shape((1, LANES), F32)]
    )
    return pl.pallas_call(
        update_kernel,
        in_specs=[VMEM] * len(operands),
        out_shape=outs,
        out_specs=[VMEM for _ in outs],
        scratch_shapes=[pltpu.VMEM(rows, F32)],
        compiler_params=pltpu.CompilerParams(vmem_limit_bytes=12 * 2**20),
        cost_estimate=pl.CostEstimate(flops=10**7, bytes_accessed=2**22, transcendentals=10**6),
    )(*operands)


def after(value, *others):
    if not others:
        return value
    return lax.optimization_barrier((value, *others))[0]


def local(
    grid,
    latents,
    restore,
    bucket,
    cotangent,
    flat_weights,
    flat_first,
    flat_second,
    vectors,
    vector_first,
    vector_second,
):
    side = lax.axis_index("blk").astype(jnp.int32)
    by_hand = grid.by_hand

    def trade(value):
        return lax.ppermute(value, "blk", [(0, 1), (1, 0)])

    pieces, places = grid.gather(flat_weights.reshape(-1, LANES).astype(BF))
    slot = (jnp.arange(SLOTS, dtype=jnp.int32) + side * (SLOTS // 2)) & (SLOTS - 1)
    position = position_rows(slot)
    my_latents, choice, my_position = prepare_call(
        latents, trade(after(latents, pieces[0])), restore, trade(after(restore, pieces[0])), position
    )
    far_cotangent = trade(after(cotangent, *pieces[-2:]))
    (
        probs, joint, normed, start, middle, mixed, embed_w, joint_w, output_w, high_lines,
    ) = forward_call(bucket, my_latents, choice, my_position, vectors, pieces, places)
    (
        own_out, far_out, hat, scale, back_out, acc_back, head_lines, far_high, near_high, expand_b,
    ) = middle_call(by_hand, bucket, middle, cotangent, far_cotangent, vectors, high_lines)
    if by_hand:
        high = Reduction(grid, far_high, near_high, 1)
    back_middle, back_mixed, out_lines, rows_b = branch_call(
        hat, scale, back_out, acc_back, mixed, output_w, vectors
    )
    if by_hand:
        back_mixed = after(back_mixed, high.hop(back_mixed))
    joint_back = attention_back_call(probs, joint, back_mixed)
    if by_hand:
        joint_back = after(joint_back, high.hop(joint_back))
    far_one, near_one, far_two, near_two, rows_c, own_latent, far_latent = input_back_call(
        by_hand, joint_back, normed, start, back_middle, my_latents, choice,
        vectors, embed_w, joint_w, out_lines, head_lines, rows_b, expand_b,
    )
    if by_hand:
        one = Reduction(grid, far_one, near_one, 0)
        two = Reduction(grid, far_two, near_two, 0)
        mark = high.hop(far_one)
        mark = one.hop(mark)
        mark = two.hop(mark)
        mark = high.hop(mark)
        high.last()
        for _ in range(3):
            mark = one.hop(mark)
            mark = two.hop(mark)
        one.last()
        two.last()
        far_out = after(far_out, mark)
        far_latent = after(far_latent, mark)

    def join(own, far):
        other = trade(far).astype(F32)
        return jnp.where(
            side == 0,
            jnp.concatenate([own, other], axis=0),
            jnp.concatenate([other, own], axis=0),
        )

    block_out = join(own_out, far_out)
    latent_out = join(own_latent, far_latent)

    if by_hand:
        grad, notes = finish_call(
            grid.count, high.head, high.across, one.head, one.across, two.head, two.across
        )
        notes = lax.all_to_all(notes, grid.axes, 0, 0, tiled=True)
        lines = [value.reshape(-1, LANES) for value in (flat_first, flat_second, flat_weights)]
        outs = update_call(grad, notes, *lines, vectors, vector_first, vector_second)
        return (
            block_out,
            latent_out,
            *(value.reshape(-1) for value in outs[:3]),
            *outs[3:6],
            outs[6].reshape(-1),
            outs[7][0, 0],
        )

    low = [
        jnp.concatenate([far, near], axis=0).reshape(16, -1, LANES)[:, :PART]
        for far, near in ((far_one, near_one), (far_two, near_two))
    ]
    flat = jnp.concatenate(
        [jnp.concatenate(low, axis=1).reshape(-1), far_high.reshape(-1), near_high.reshape(-1)]
    )
    shard_grad = lax.psum_scatter(flat, grid.axes, scatter_dimension=0, tiled=True)
    shard_grad = shard_grad.astype(F32).reshape(-1, LANES)
    vector_sum = lax.psum(rows_c[: vectors.shape[0]], grid.axes)
    square_sum = lax.psum(jnp.sum(shard_grad * shard_grad), grid.axes)
    grad_norm = jnp.sqrt(square_sum + jnp.sum(vector_sum * vector_sum))
    factor = jnp.minimum(1.0, clip_norm / (grad_norm + 1e-06))
    new_first, new_second, new_weights = adam_update(
        shard_grad.reshape(-1) * factor,
        flat_first,
        flat_second,
        flat_weights,
        learn_rate,
        decay_weight,
    )
    vector_first_new, vector_second_new, vectors_new = adam_update(
        vector_sum * factor, vector_first, vector_second, vectors, vector_rate, 0.0
    )
    reduce_bias_grad = vector_sum[9] * factor
    return (
        block_out,
        latent_out,
        new_first,
        new_second,
        new_weights,
        vector_first_new,
        vector_second_new,
        vectors_new,
        reduce_bias_grad,
        grad_norm,
    )


def solution(mesh):
    grid = Grid(mesh)
    return jax.shard_map(
        lambda *args: local(grid, *args),
        mesh=mesh,
        in_specs=(
            P("dp", "blk", None),
            P("dp", "blk"),
            P("dp"),
            P("dp", "blk", None),
            P(("dp", "blk")),
            P(("dp", "blk")),
            P(("dp", "blk")),
            P(),
            P(),
            P(),
        ),
        out_specs=(
            P("dp", "blk", None),
            P("dp", "blk", None),
            P(("dp", "blk")),
            P(("dp", "blk")),
            P(("dp", "blk")),
            P(),
            P(),
            P(),
            P(),
            P(),
        ),
        check_vma=False,
    )
```

```python
import math

import jax
import jax.numpy as jnp
from jax import lax
from jax.experimental import pallas as pl
from jax.experimental.pallas import tpu as pltpu
from jax.sharding import PartitionSpec as P

DIN = 768
D = 512
HEADS = 16
HD = 32
FF = 2048
SLOTS = 256
KMAX = 64
STEP = 10
NPARAM = 3538944

first_decay = 0.9
second_decay = 0.95
learn_rate = 0.05
vector_rate = 0.5
decay_weight = 0.05
adam_eps = 1e-08
clip_norm = 1.0

BF = jnp.bfloat16
F32 = jnp.float32

LANES = 128
LINES = NPARAM // LANES
EMBED_AT = 0
JOINT_AT = EMBED_AT + DIN * D // LANES
OUTPUT_AT = JOINT_AT + 3 * D * D // LANES
EXPAND_AT = OUTPUT_AT + D * D // LANES
REDUCE_AT = EXPAND_AT + D * FF // LANES
BLOCK = LINES // 32
HALF = 16 * BLOCK
TAIL = 16
ROWS = 16
PART = BLOCK // 2
PARTS = (PART + TAIL, PART)
TILE = 256
TILES = FF // TILE
GROUP = 4
GROUPS = HEADS // GROUP
MINE = 2
TOKENS = MINE * SLOTS
PICKS = KMAX + 16
PACK = SLOTS // 2 + KMAX // 2 + KMAX // 4
VMEM = pl.BlockSpec(memory_space=pltpu.VMEM)
SMEM = pl.BlockSpec(memory_space=pltpu.SMEM)
ANY = pl.BlockSpec(memory_space=pl.ANY)


def position_rows(slot):
    column = jnp.arange(D // 2, dtype=jnp.int32).astype(F32)[None, :]
    angle = slot.astype(F32)[:, None] * jnp.exp(-math.log(10000.0) * column / (D // 2))
    return jnp.concatenate([jnp.sin(angle), jnp.cos(angle)], axis=1)


def adam_update(grad, first, second, weight, rate, shrink):
    first_new = first_decay * first + (1.0 - first_decay) * grad
    second_new = second_decay * second + (1.0 - second_decay) * grad * grad
    first_hat = first_new / (1.0 - first_decay**STEP)
    second_hat = second_new / (1.0 - second_decay**STEP)
    weight_new = weight - rate * (first_hat / (jnp.sqrt(second_hat) + adam_eps) + shrink * weight)
    return (first_new, second_new, weight_new)


def dot(left, right, over=(1, 0)):
    return lax.dot_general(
        left, right, (((over[0],), (over[1],)), ((), ())), preferred_element_type=F32
    )


def place():
    return lax.axis_index("dp") * lax.axis_size("blk") + lax.axis_index("blk")


def collect_call(lines, pieces, places):
    def kernel(*refs):
        out = refs[-1]
        me = place()
        odd = (me >> 1) & 1
        for (bits, even, uneven), piece in zip(places, refs[-1 - len(pieces) : -1], strict=True):
            block = me ^ bits ^ jnp.where(odd == 0, even, uneven)
            out[pl.ds(pl.multiple_of(block * BLOCK, 16), BLOCK), :] = piece[...]

    given = ([] if lines is None else [lines]) + list(pieces)
    return pl.pallas_call(
        kernel,
        in_specs=[VMEM] * len(given),
        out_shape=pltpu.VMEM((LINES, LANES), BF),
        out_specs=VMEM,
        input_output_aliases={} if lines is None else {0: 0},
        compiler_params=pltpu.CompilerParams(vmem_limit_bytes=2 * 2**20),
        cost_estimate=pl.CostEstimate(flops=0, bytes_accessed=2**20, transcendentals=0),
    )(*(in_vmem(value) for value in given))


def lines_to_matrix(lines, stage, matrix, at, rows, wide, batch):
    size = batch * wide

    def body(index, carry):
        for part in range(2):
            row = pl.multiple_of((2 * index + part) * batch, batch)
            source = pl.multiple_of(at + (2 * index + part) * size, 16)
            stage[part, :size, :] = lines[pl.ds(source, size), :].astype(F32)
            for j in range(wide):
                matrix[pl.ds(row, batch), j * LANES : (j + 1) * LANES] = stage[
                    part, pl.ds(j, batch, stride=wide), :
                ].astype(BF)
        return carry

    lax.fori_loop(0, rows // batch // 2, body, 0)


def norm_parts(value):
    centred = value - jnp.mean(value, axis=-1, keepdims=True)
    scale = lax.rsqrt(jnp.mean(centred * centred, axis=-1, keepdims=True) + 1e-06)
    return centred * scale, scale


def norm_back(grad, hat, scale, gain):
    inner = grad * gain
    return scale * (
        inner
        - jnp.mean(inner, axis=-1, keepdims=True)
        - hat * jnp.mean(inner * hat, axis=-1, keepdims=True)
    )


def total(value):
    return jnp.sum(value.astype(F32), axis=0, keepdims=True)


def slot_column(side):
    local = lax.broadcasted_iota(jnp.int32, (SLOTS, 1), 0)
    return (local + side * (SLOTS // 2)) & (SLOTS - 1)


def image_length(bucket, image):
    kind = bucket[image]
    return jnp.where(
        kind == 0, SLOTS * 100 // 256, jnp.where(kind == 1, SLOTS * 196 // 256, SLOTS)
    )


def select_rows(own, far, side):
    half = SLOTS // 2
    row = lax.broadcasted_iota(jnp.int32, (PICKS, half), 0)
    row = jnp.where(row < KMAX, (row + side * (KMAX // 2)) & (KMAX - 1), row)
    parts = [
        (row == names).astype(F32) for names in (own, far)
    ]
    return jnp.concatenate(parts, axis=1).astype(BF)


def three_parts(value):
    high = value.astype(BF)
    rest = value - high.astype(F32)
    mid = rest.astype(BF)
    return high, mid, (rest - mid.astype(F32)).astype(BF)


def head_mask(head):
    lane = lax.broadcasted_iota(jnp.int32, (1, LANES), 1)
    return (lane // HD) == head


def mask_head(value, head):
    return jnp.where(head_mask(head), value, jnp.zeros_like(value))


def pick_kernel(latents, cotangent, restore, far_latents, far_cotangent, far_restore, sem):
    first = (1 - lax.axis_index("blk")) * MINE
    copies = [
        pltpu.make_async_copy(source.at[pl.ds(first, MINE)], target, sem.at[index])
        for index, (source, target) in enumerate(
            ((latents, far_latents), (cotangent, far_cotangent))
        )
    ]
    for copy in copies:
        copy.start()
    for image in range(MINE):
        far_restore[image : image + 1, :] = restore[pl.ds(first + image, 1), :]
    for copy in copies:
        copy.wait()


def pick_call(latents, cotangent, restore):
    outs = tuple(
        pltpu.VMEM((MINE, *value.shape[1:]), value.dtype) for value in (latents, cotangent, restore)
    )
    return pl.pallas_call(
        pick_kernel,
        in_specs=[ANY, ANY, VMEM],
        out_shape=outs,
        out_specs=tuple(VMEM for _ in outs),
        scratch_shapes=[pltpu.SemaphoreType.DMA((2,))],
        compiler_params=pltpu.CompilerParams(vmem_limit_bytes=2 * 2**20),
        cost_estimate=pl.CostEstimate(flops=0, bytes_accessed=2**19, transcendentals=0),
    )(in_hbm(latents), in_hbm(cotangent), restore)


def prepare_kernel(
    latents, far_latents, restore, far_restore, position, my_latents, choice, my_position,
    near_buffer, sem,
):
    side = lax.axis_index("blk")
    copy = pltpu.make_async_copy(latents.at[pl.ds(side * MINE, MINE)], near_buffer, sem)
    copy.start()
    my_position[...] = position[...]
    for image in range(MINE):
        choice[image] = select_rows(
            restore[pl.ds(side * MINE + image, 1), :], far_restore[image : image + 1, :], side
        )
    copy.wait()
    half = KMAX // 2
    for image in range(MINE):
        at = image * KMAX
        my_latents[at : at + half, :] = near_buffer[image]
        my_latents[at + half : at + KMAX, :] = far_latents[image]


def prepare_call(*operands):
    outs = (
        pltpu.VMEM((MINE * KMAX, DIN), BF),
        pltpu.VMEM((MINE, PICKS, SLOTS), BF),
        pltpu.VMEM((SLOTS, D), F32),
    )
    return pl.pallas_call(
        prepare_kernel,
        in_specs=[ANY, VMEM, VMEM, VMEM, VMEM],
        out_shape=outs,
        out_specs=tuple(VMEM for _ in outs),
        scratch_shapes=[
            pltpu.VMEM((MINE, KMAX // 2, DIN), BF),
            pltpu.SemaphoreType.DMA,
        ],
        compiler_params=pltpu.CompilerParams(vmem_limit_bytes=4 * 2**20),
        cost_estimate=pl.CostEstimate(flops=10**6, bytes_accessed=2**20, transcendentals=0),
    )(in_hbm(operands[0]), *operands[1:])


def forward_kernel(bucket, my_latents, choice, position, vectors, lines, *rest):
    (
        probs,
        shares,
        joint,
        normed,
        start,
        middle,
        mixed,
        embed_w,
        joint_w,
        output_w,
        stage,
        query_t,
        value_t,
        mixed_t,
        scores_even,
        scores_odd,
    ) = rest
    side = lax.axis_index("blk")
    lines_to_matrix(lines, stage, embed_w, EMBED_AT, DIN, 4, 128)
    lines_to_matrix(lines, stage, joint_w, JOINT_AT, D, 12, 64)
    lines_to_matrix(lines, stage, output_w, OUTPUT_AT, D, 4, 128)
    embedded = (dot(my_latents[...], embed_w[...]) + vectors[0:1, :]).astype(BF)
    token = list(three_parts(vectors[1:2, :]))
    for image in range(MINE):
        rows = slice(image * SLOTS, (image + 1) * SLOTS)
        picked = choice[image]
        value = dot(picked[:KMAX], embedded[image * KMAX : (image + 1) * KMAX, :], (0, 0))
        masked = jnp.broadcast_to(picked[KMAX : KMAX + 1], (16, SLOTS))
        table = jnp.concatenate(token + [jnp.zeros((13, D), BF)], axis=0)
        value = value + dot(masked, table, (0, 0)) + position[...]
        start[rows, :] = value
        hat, _ = norm_parts(value)
        normed[rows, :] = (hat * vectors[2:3, :] + vectors[3:4, :]).astype(BF)
    for part, bias in enumerate((4, None, 5)):
        columns = slice(part * D, (part + 1) * D)
        out = dot(normed[...], joint_w[:, columns])
        if bias is not None:
            out = out + vectors[bias : bias + 1, :]
        joint[:, columns] = out.astype(BF)
    query_t[...] = joint[:, :D].T
    value_t[...] = joint[:, 2 * D :].T

    rate = HD**-0.5 * math.log2(math.e)

    def score(unit, target):
        image, group = unit // GROUPS, unit % GROUPS
        rows = pl.ds(pl.multiple_of(image * SLOTS, SLOTS), SLOTS)
        keys = joint[rows, pl.ds(pl.multiple_of(D + group * LANES, LANES), LANES)]
        queries = query_t[pl.ds(pl.multiple_of(group * LANES, LANES), LANES), rows]
        for head in range(GROUP):
            target[head] = dot(mask_head(keys, head), queries)

    def mix(unit, source):
        image, group = unit // GROUPS, unit % GROUPS
        rows = pl.ds(pl.multiple_of(image * SLOTS, SLOTS), SLOTS)
        length = image_length(bucket, side * MINE + image)
        hidden_key = jnp.where(slot_column(side) < length, 0.0, -1e30)
        for head in range(GROUP):
            scores = source[head] + hidden_key
            top = jnp.max(scores, axis=0, keepdims=True)
            raised = jnp.exp2((scores - top) * rate)
            share = 1.0 / jnp.sum(raised, axis=0, keepdims=True)
            low = raised.astype(BF)
            probs[unit * GROUP + head] = low
            shares[pl.ds(unit * GROUP + head, 1), :] = share
            features = pl.ds(pl.multiple_of(group * LANES + head * HD, HD), HD)
            mixed_t[features, rows] = (dot(value_t[features, rows], low) * share).astype(BF)

    score(0, scores_even)

    def pair(index, carry):
        unit = 2 * index
        score(unit + 1, scores_odd)
        mix(unit, scores_even)
        score(jnp.minimum(unit + 2, MINE * GROUPS - 1), scores_even)
        mix(unit + 1, scores_odd)
        return carry

    lax.fori_loop(0, MINE * GROUPS // 2, pair, 0)
    mixed[...] = mixed_t[...].T
    middle[...] = start[...] + dot(mixed[...], output_w[...]) + vectors[6:7, :]


def forward_call(*operands):
    outs = (
        pltpu.VMEM((MINE * HEADS, SLOTS, SLOTS), BF),
        pltpu.VMEM((MINE * HEADS, SLOTS), F32),
        pltpu.VMEM((TOKENS, 3 * D), BF),
        pltpu.VMEM((TOKENS, D), BF),
        pltpu.VMEM((TOKENS, D), F32),
        pltpu.VMEM((TOKENS, D), F32),
        pltpu.VMEM((TOKENS, D), BF),
        pltpu.VMEM((DIN, D), BF),
        pltpu.VMEM((D, 3 * D), BF),
        pltpu.VMEM((D, D), BF),
    )
    return pl.pallas_call(
        forward_kernel,
        in_specs=[SMEM] + [VMEM] * (len(operands) - 1),
        out_shape=outs,
        out_specs=tuple(VMEM for _ in outs),
        scratch_shapes=[
            pltpu.VMEM((2, 768, LANES), F32),
            pltpu.VMEM((D, TOKENS), BF),
            pltpu.VMEM((D, TOKENS), BF),
            pltpu.VMEM((D, TOKENS), BF),
            pltpu.VMEM((GROUP, SLOTS, SLOTS), F32),
            pltpu.VMEM((GROUP, SLOTS, SLOTS), F32),
        ],
        compiler_params=pltpu.CompilerParams(vmem_limit_bytes=10 * 2**20),
        cost_estimate=pl.CostEstimate(
            flops=6 * 10**9, bytes_accessed=16 * 2**20, transcendentals=2 * 10**6
        ),
    )(*operands)


def middle_kernel(
    by_hand, bucket, middle, cotangent, far_cotangent, vectors, lines, *rest
):
    (
        own_out,
        far_out,
        hat,
        scale,
        back_out,
        acc_back,
        head_lines,
        far_lines,
        near_lines,
        expand_out,
        stage,
        expand_w,
        reduce_w,
        normed,
        normed_t,
        acc,
        grads,
    ) = rest
    step = pl.program_id(0)
    side = lax.axis_index("blk")

    @pl.when(step == 0)
    def _():
        value, spread = norm_parts(middle[...])
        hat[...] = value
        scale[...] = jnp.broadcast_to(spread, scale.shape)
        normed[...] = (value * vectors[7:8, :] + vectors[8:9, :]).astype(BF)
        normed_t[...] = normed[...].T
        for image in range(MINE):
            valid = slot_column(side) < image_length(bucket, side * MINE + image)
            half = SLOTS // 2
            for part, (ref, at) in enumerate(
                ((cotangent, side * MINE + image), (far_cotangent, image))
            ):
                first = image * SLOTS + part * half
                back_out[first : first + half, :] = jnp.where(
                    valid[part * half : (part + 1) * half, :],
                    ref[at].astype(F32),
                    0.0,
                ).astype(BF)
        acc[...] = jnp.zeros_like(acc)
        acc_back[...] = jnp.zeros_like(acc_back)
        lines_to_matrix(lines, stage, expand_w, EXPAND_AT, D, 16, 32)
        lines_to_matrix(lines, stage, reduce_w, REDUCE_AT, FF, 4, 128)

    columns = pl.ds(pl.multiple_of(step * TILE, TILE), TILE)
    expand = expand_w[:, columns]
    reduce = reduce_w[columns, :]
    bias = vectors[pl.ds(10 + step // 2, 1), pl.ds(pl.multiple_of((step % 2) * TILE, TILE), TILE)]
    hidden = dot(normed[...], expand) + bias
    density = jnp.exp(hidden * hidden * -0.5) * (1.0 / math.sqrt(2.0 * math.pi))
    below = 0.5 + 0.5 * lax.erf(hidden * math.sqrt(0.5))
    active = (hidden * below).astype(BF)
    back_active = dot(back_out[...], reduce, (1, 1))
    back_hidden = (back_active * (below + hidden * density)).astype(BF)
    acc[...] += dot(active, reduce)
    acc_back[...] += dot(back_hidden, expand, (1, 1))
    grad_reduce = dot(active, back_out[...], (0, 0))
    for j in range(4):
        grads[pl.ds(D * 16 + step * (TILE * 4) + j, TILE, stride=4), :] = grad_reduce[
            :, j * LANES : (j + 1) * LANES
        ]
    grad_expand = dot(normed_t[...], back_hidden)
    for j in range(TILE // LANES):
        grads[pl.ds(step * (TILE // LANES) + j, D, stride=16), :] = grad_expand[
            :, j * LANES : (j + 1) * LANES
        ]
    expand_out[pl.ds(step, 1), :] = total(back_hidden)

    @pl.when(step == TILES - 1)
    def _():
        for image in range(MINE):
            near = slice(image * SLOTS, image * SLOTS + SLOTS // 2)
            far = slice(image * SLOTS + SLOTS // 2, (image + 1) * SLOTS)
            own_out[image] = middle[near, :] + acc[near, :] + vectors[9:10, :]
            far_out[image] = (middle[far, :] + acc[far, :] + vectors[9:10, :]).astype(BF)
        cut = HALF - EXPAND_AT
        head_lines[...] = grads[:cut, :].astype(BF)
        put_blocks(
            by_hand,
            far_lines,
            near_lines,
            lambda q: grads[pl.ds(cut + q * BLOCK, BLOCK), :].astype(BF),
        )


def slot_of(index, by_hand):
    if not by_hand:
        return index
    me = place()
    rel = index ^ (me & 15)
    other = (rel >> 1) & 1
    odd = ((me >> 1) & 1) ^ other
    along_y, along_x, along_z = rel & 1, (rel >> 2) & 1, rel >> 3
    first = jnp.where(odd == 0, along_y, along_x)
    second = jnp.where(odd == 0, along_x, along_y)
    slot = (1 - first) * 4 + (1 - second) * 2 + (1 - along_z)
    return slot + jnp.where(other == 1, 0, 8)


def put_blocks(by_hand, far_lines, near_lines, block_of):
    def body(index, carry):
        slot = slot_of(index, by_hand)
        value = block_of(index)

        @pl.when(slot < 8)
        def _():
            far_lines[pl.ds(pl.multiple_of(slot * BLOCK, 16), BLOCK), :] = value

        @pl.when(slot >= 8)
        def _():
            near_lines[pl.ds(pl.multiple_of((slot - 8) * BLOCK, 16), BLOCK), :] = value

        return carry

    lax.fori_loop(0, 16, body, 0)


def middle_call(by_hand, *operands):
    outs = (
        pltpu.VMEM((MINE, SLOTS // 2, D), F32),
        pltpu.VMEM((MINE, SLOTS // 2, D), BF),
        pltpu.VMEM((TOKENS, D), F32),
        pltpu.VMEM((TOKENS, LANES), F32),
        pltpu.VMEM((TOKENS, D), BF),
        pltpu.VMEM((TOKENS, D), F32),
        pltpu.VMEM((HALF - EXPAND_AT, LANES), BF),
        pltpu.VMEM((8 * BLOCK, LANES), BF),
        pltpu.VMEM((8 * BLOCK, LANES), BF),
        pltpu.VMEM((TILES, TILE), F32),
    )
    return pl.pallas_call(
        lambda *refs: middle_kernel(by_hand, *refs),
        grid=(TILES,),
        in_specs=[SMEM] + [VMEM] * (len(operands) - 1),
        out_shape=outs,
        out_specs=tuple(VMEM for _ in outs),
        scratch_shapes=[
            pltpu.VMEM((2, 768, LANES), F32),
            pltpu.VMEM((D, FF), BF),
            pltpu.VMEM((FF, D), BF),
            pltpu.VMEM((TOKENS, D), BF),
            pltpu.VMEM((D, TOKENS), BF),
            pltpu.VMEM((TOKENS, D), F32),
            pltpu.VMEM((2 * D * 16, LANES), F32),
        ],
        compiler_params=pltpu.CompilerParams(vmem_limit_bytes=20 * 2**20),
        cost_estimate=pl.CostEstimate(
            flops=8 * 10**9, bytes_accessed=16 * 2**20, transcendentals=2 * 10**6
        ),
    )(*operands)


def branch_kernel(
    hat, scale, back_out, acc_back, mixed, output_w, vectors,
    back_middle, back_mixed, out_lines, rows_out, out_grads,
):
    grad = acc_back[...]
    rows_out[...] = jnp.zeros_like(rows_out)
    rows_out[1:2, :] = total(grad * hat[...])
    rows_out[2:3, :] = total(grad)
    rows_out[3:4, :] = total(back_out[...])
    back = back_out[...].astype(F32) + norm_back(
        grad, hat[...], scale[:, :1], vectors[7:8, :]
    )
    back_middle[...] = back
    branch = back.astype(BF)
    rows_out[0:1, :] = total(branch)
    back_mixed[...] = dot(branch, output_w[...], (1, 1)).astype(BF)
    grad_output = dot(mixed[...], branch, (0, 0))
    for j in range(4):
        out_grads[pl.ds(j, D, stride=4), :] = grad_output[:, j * LANES : (j + 1) * LANES]
    out_lines[...] = out_grads[...].astype(BF)


def branch_call(hat, scale, back_out, acc_back, mixed, output_w, vectors):
    outs = (
        pltpu.VMEM((TOKENS, D), F32),
        pltpu.VMEM((TOKENS, D), BF),
        pltpu.VMEM((EXPAND_AT - OUTPUT_AT, LANES), BF),
        pltpu.VMEM((8, D), F32),
    )
    return pl.pallas_call(
        branch_kernel,
        in_specs=[VMEM] * 7,
        out_shape=outs,
        out_specs=tuple(VMEM for _ in outs),
        scratch_shapes=[pltpu.VMEM((D * 4, LANES), F32)],
        compiler_params=pltpu.CompilerParams(vmem_limit_bytes=16 * 2**20),
        cost_estimate=pl.CostEstimate(
            flops=2 * 10**9, bytes_accessed=4 * 2**20, transcendentals=0
        ),
    )(hat, scale, back_out, acc_back, mixed, output_w, vectors)


def attention_back_kernel(
    probs, shares, joint, back_mixed, normed, start, back_middle, vectors, joint_w,
    joint_lines, back_start, rows_out,
    joint_back, key_t, back_t, shared_t, shared, query_back_t, even, odd, grads,
):
    key_t[...] = joint[:, D : 2 * D].T
    back_t[...] = back_mixed[...].T
    for image in range(MINE):
        columns = slice(image * SLOTS, (image + 1) * SLOTS)
        for head in range(HEADS):
            features = slice(head * HD, (head + 1) * HD)
            at = image * HEADS + head
            shared_t[features, columns] = (
                back_t[features, columns].astype(F32) * shares[at : at + 1, :]
            ).astype(BF)
    shared[...] = shared_t[...].T

    def pull_back(unit, target):
        image, group = unit // GROUPS, unit % GROUPS
        rows = pl.ds(pl.multiple_of(image * SLOTS, SLOTS), SLOTS)
        values = joint[rows, pl.ds(pl.multiple_of(2 * D + group * LANES, LANES), LANES)]
        back_lanes = back_t[pl.ds(pl.multiple_of(group * LANES, LANES), LANES), rows]
        for head in range(GROUP):
            target[head] = dot(mask_head(values, head), back_lanes)

    def spread(unit, source):
        image, group = unit // GROUPS, unit % GROUPS
        rows = pl.ds(pl.multiple_of(image * SLOTS, SLOTS), SLOTS)
        lanes = pl.ds(pl.multiple_of(group * LANES, LANES), LANES)
        queries = joint[rows, lanes]
        back = shared[rows, lanes]
        key_back = jnp.zeros((SLOTS, LANES), F32)
        value_back = jnp.zeros((SLOTS, LANES), F32)
        for head in range(GROUP):
            low = probs[unit * GROUP + head]
            share = shares[pl.ds(unit * GROUP + head, 1), :]
            wide = low.astype(F32)
            back_probs = source[head]
            pull = jnp.sum(wide * back_probs, axis=0, keepdims=True) * share
            score_back = (wide * ((back_probs - pull) * (share * HD**-0.5))).astype(BF)
            value_back = value_back + dot(low, mask_head(back, head))
            key_back = key_back + dot(score_back, mask_head(queries, head))
            features = pl.ds(pl.multiple_of(group * LANES + head * HD, HD), HD)
            query_back_t[features, rows] = dot(key_t[features, rows], score_back).astype(BF)
        joint_back[rows, pl.ds(pl.multiple_of(D + group * LANES, LANES), LANES)] = (
            key_back.astype(BF)
        )
        joint_back[rows, pl.ds(pl.multiple_of(2 * D + group * LANES, LANES), LANES)] = (
            value_back.astype(BF)
        )

    pull_back(0, even)

    def pair(index, carry):
        unit = 2 * index
        pull_back(unit + 1, odd)
        spread(unit, even)
        pull_back(jnp.minimum(unit + 2, MINE * GROUPS - 1), even)
        spread(unit + 1, odd)
        return carry

    lax.fori_loop(0, MINE * GROUPS // 2, pair, 0)
    joint_back[:, :D] = query_back_t[...].T
    rows_out[...] = jnp.zeros_like(rows_out)
    rows_out[2:3, :] = total(joint_back[:, :D])
    rows_out[3:4, :] = total(joint_back[:, 2 * D :])
    normed_t = normed[...].T
    for part in range(3):
        grad_joint = dot(normed_t, joint_back[:, part * D : (part + 1) * D])
        for j in range(4):
            grads[pl.ds(part * 4 + j, D, stride=12), :] = grad_joint[
                :, j * LANES : (j + 1) * LANES
            ]
    grad = dot(joint_back[...], joint_w[...], (1, 1))
    hat, scale = norm_parts(start[...])
    rows_out[0:1, :] = total(grad * hat)
    rows_out[1:2, :] = total(grad)
    back_start[...] = back_middle[...] + norm_back(grad, hat, scale, vectors[2:3, :])
    joint_lines[...] = grads[...].astype(BF)


def attention_back_call(*operands):
    outs = (
        pltpu.VMEM((OUTPUT_AT - JOINT_AT, LANES), BF),
        pltpu.VMEM((TOKENS, D), F32),
        pltpu.VMEM((8, D), F32),
    )
    return pl.pallas_call(
        attention_back_kernel,
        in_specs=[VMEM] * len(operands),
        out_shape=outs,
        out_specs=tuple(VMEM for _ in outs),
        scratch_shapes=[
            pltpu.VMEM((TOKENS, 3 * D), BF),
            pltpu.VMEM((D, TOKENS), BF),
            pltpu.VMEM((D, TOKENS), BF),
            pltpu.VMEM((D, TOKENS), BF),
            pltpu.VMEM((TOKENS, D), BF),
            pltpu.VMEM((D, TOKENS), BF),
            pltpu.VMEM((GROUP, SLOTS, SLOTS), F32),
            pltpu.VMEM((GROUP, SLOTS, SLOTS), F32),
            pltpu.VMEM((OUTPUT_AT - JOINT_AT, LANES), F32),
        ],
        compiler_params=pltpu.CompilerParams(vmem_limit_bytes=16 * 2**20),
        cost_estimate=pl.CostEstimate(
            flops=8 * 10**9, bytes_accessed=4 * 2**20, transcendentals=0
        ),
    )(*operands)


def input_back_kernel(
    by_hand,
    back_start,
    my_latents,
    choices,
    embed_w,
    joint_lines,
    rows_joint,
    out_lines,
    head_lines,
    rows_in,
    expand_in,
    far_out,
    far_first,
    near_first,
    far_second,
    near_second,
    rows_out,
    own_latent,
    pack,
    grads,
    tails,
):
    rows_out[...] = jnp.zeros_like(rows_out)
    rows_out[2:6, :] = rows_joint[0:4, :]
    low_start = back_start[...].astype(BF)
    low_rest = (back_start[...] - low_start.astype(F32)).astype(BF)
    picked = []
    token_back = jnp.zeros((1, D), F32)
    for image in range(MINE):
        part = slice(image * SLOTS, (image + 1) * SLOTS)
        choice = choices[image]
        chosen = dot(choice, low_start[part, :])
        picked.append(chosen[:KMAX, :].astype(BF))
        token_back = token_back + chosen[KMAX : KMAX + 1, :]
        token_back = token_back + dot(choice[KMAX:, :], low_rest[part, :])[:1, :]
    rows_out[1:2, :] = token_back
    embedded_back = jnp.concatenate(picked, axis=0)
    rows_out[0:1, :] = total(embedded_back)
    grad_embed = dot(my_latents[...], embedded_back, (0, 0))
    for j in range(4):
        grads[pl.ds(EMBED_AT + j, DIN, stride=4), :] = grad_embed[:, j * LANES : (j + 1) * LANES]
    latent_back = dot(embedded_back, embed_w[...], (1, 1))
    for image in range(MINE):
        at = image * KMAX
        own_latent[image] = latent_back[at : at + KMAX // 2, :]
        far = latent_back[at + KMAX // 2 : at + KMAX, :].astype(BF)
        pack[image, : SLOTS // 2, :] = far_out[image]
        pack[image, SLOTS // 2 : SLOTS // 2 + KMAX // 2, :] = far[:, :D]
        pack[image, SLOTS // 2 + KMAX // 2 :, : DIN - D] = far[: KMAX // 4, D:]
        pack[image, SLOTS // 2 + KMAX // 2 :, DIN - D :] = far[KMAX // 4 :, D:]
    rows_out[6:10, :] = rows_in[0:4, :]
    for j in range(4):
        rows_out[10 + j : 11 + j, :TILE] = expand_in[2 * j : 2 * j + 1, :]
        rows_out[10 + j : 11 + j, TILE:] = expand_in[2 * j + 1 : 2 * j + 2, :]
    tails[...] = jnp.zeros_like(tails)
    for row in range(ROWS):
        for j in range(D // LANES):
            tails[row * TAIL + j : row * TAIL + j + 1, :] = rows_out[
                row : row + 1, j * LANES : (j + 1) * LANES
            ]

    def store(index, value):
        slot = slot_of(index, by_hand)
        tail = tails[pl.ds(pl.multiple_of(index * TAIL, TAIL), TAIL), :].astype(BF)

        def put(first, second, at):
            row = pl.multiple_of(at * PARTS[0], 16)
            first[pl.ds(row, PART), :] = value[:PART]
            first[pl.ds(row + PART, TAIL), :] = tail
            second[pl.ds(pl.multiple_of(at * PART, 16), PART), :] = value[PART:]

        @pl.when(slot < 8)
        def _():
            put(far_first, far_second, slot)

        @pl.when(slot >= 8)
        def _():
            put(near_first, near_second, slot - 8)

    ranges = (
        (EMBED_AT, JOINT_AT, lambda low, high: grads[low:high, :].astype(BF)),
        (JOINT_AT, OUTPUT_AT, lambda low, high: joint_lines[low:high, :]),
        (OUTPUT_AT, EXPAND_AT, lambda low, high: out_lines[low:high, :]),
        (EXPAND_AT, HALF, lambda low, high: head_lines[low:high, :]),
    )
    for index in range(16):
        low, high = index * BLOCK, (index + 1) * BLOCK
        parts = [
            take(max(low, begin) - begin, min(high, end) - begin)
            for begin, end, take in ranges
            if max(low, begin) < min(high, end)
        ]
        store(index, jnp.concatenate(parts, axis=0) if len(parts) > 1 else parts[0])


def input_back_call(by_hand, *operands):
    shape = jax.ShapeDtypeStruct
    outs = (
        pltpu.VMEM((8 * PARTS[0], LANES), BF),
        pltpu.VMEM((8 * PARTS[0], LANES), BF),
        pltpu.VMEM((8 * PARTS[1], LANES), BF),
        pltpu.VMEM((8 * PARTS[1], LANES), BF),
        shape((ROWS, D), F32),
        pltpu.VMEM((MINE, KMAX // 2, DIN), F32),
        pltpu.VMEM((MINE, PACK, D), BF),
    )
    return pl.pallas_call(
        lambda *refs: input_back_kernel(by_hand, *refs),
        in_specs=[VMEM] * len(operands),
        out_shape=outs,
        out_specs=tuple(VMEM for _ in outs),
        scratch_shapes=[
            pltpu.VMEM((JOINT_AT, LANES), F32),
            pltpu.VMEM((ROWS * TAIL, LANES), F32),
        ],
        compiler_params=pltpu.CompilerParams(vmem_limit_bytes=24 * 2**20),
        cost_estimate=pl.CostEstimate(
            flops=4 * 10**9, bytes_accessed=8 * 2**20, transcendentals=0
        ),
    )(*operands)


class Grid:
    def __init__(self, mesh):
        self.axes = ("dp", "blk")
        self.count = mesh.shape["dp"] * mesh.shape["blk"]
        self.early = self.late = ()
        self.by_hand = self.count == 32 and mesh.shape["blk"] == 2

    def send(self, value, bits, other=None):
        other = bits if other is None else other
        pairs = [(i, i ^ (other if i & 2 else bits)) for i in range(self.count)]
        return lax.ppermute(value, self.axes, pairs)

    def gather(self, block):
        if not self.by_hand:
            whole = lax.all_gather(block, self.axes, axis=0, tiled=True)
            return whole.reshape(LINES, LANES)
        got = {"held0": block}

        def send(name, value, bits, other=None, behind=()):
            got[name] = self.send(after(got[value], *(got[b] for b in behind)), bits, other)

        def put(lines, *names):
            pieces, places = [], []
            for name in names:
                even, uneven = {"held": (0, 0), "near": (4, 1), "side": (1, 4), "far": (5, 5)}[
                    name.rstrip("0123456789")
                ]
                bits = int(name.lstrip("abcdefghijklmnopqrstuvwxyz"))
                pieces += [got[name], self.send(got[name], 2)]
                places += [(bits, even, uneven), (bits ^ 2, uneven, even)]
            return collect_call(lines, pieces, places)

        send("held16", "held0", 16)
        send("near0", "held0", 4, 1)
        send("held8", "held0", 8)
        send("side0", "held0", 1, 4)
        send("far0", "near0", 1, 4)
        send("near16", "held16", 4, 1)
        send("side16", "held16", 1, 4)
        send("held24", "held16", 8)
        send("near8", "held8", 4, 1)
        send("side8", "held8", 1, 4)
        send("far8", "far0", 8)
        send("far16", "near16", 1, 4)
        send("near24", "held24", 4, 1, behind=("near8",))
        send("side24", "held24", 1, 4, behind=("side8",))
        send("far24", "far16", 8, behind=("far8",))
        lines = put(
            None, "held0", "near0", "side0", "far0", "held8", "near8", "side8", "far8", "held16",
            "near16", "side16", "far16", "held24", "near24", "side24", "far24",
        )
        self.late = (got["side24"], got["far24"])
        self.early = (got["near24"],)
        return lines


def add_call(rows, *terms):
    def kernel(*refs):
        out = refs[-1]
        value = None
        for ref, (_, at) in zip(refs[:-1], terms, strict=True):
            part = ref[at : at + rows, :].astype(F32)
            value = part if value is None else value + part
        out[...] = value.astype(BF)

    return pl.pallas_call(
        kernel,
        in_specs=[VMEM] * len(terms),
        out_shape=pltpu.VMEM((rows, LANES), BF),
        out_specs=VMEM,
        compiler_params=pltpu.CompilerParams(vmem_limit_bytes=4 * 2**20),
        cost_estimate=pl.CostEstimate(flops=10**5, bytes_accessed=2**20, transcendentals=0),
    )(*(in_vmem(array) for array, _ in terms))


def in_hbm(value):
    return pltpu.with_memory_space_constraint(value, pltpu.HBM)


def in_vmem(value):
    return pltpu.with_memory_space_constraint(value, pltpu.VMEM)


class Reduction:
    HOPS = ((2, 2), (1, 4), (4, 1), (8, 8))

    def __init__(self, grid, far_lines, near_lines, half):
        self.grid = grid
        self.near = near_lines
        self.half = half
        self.rows = far_lines.shape[0] // 8
        self.head = far_lines
        self.came = []

    def hop(self, *behind):
        step = len(self.came)
        self.came.append(self.grid.send(self.head, *self.HOPS[step]))
        left = 8 >> (step + 1)
        count = max(left, 1) if step < 3 else 1
        begin = 8 - 2 * left if step < 3 else 7
        terms = [(after(self.near, *behind), begin * self.rows)]
        for level, value in enumerate(self.came):
            terms.append((value, (begin - (8 - (8 >> level))) * self.rows))
        self.head = add_call(count * self.rows, *terms)
        return self.head


def cross_call(low, high, at):
    rows = low.shape[0]
    lines = min(rows, PART)

    def kernel(low, high, out):
        lower = (place() & 16) == 0
        out[:lines, :] = jnp.where(lower, high[at : at + lines, :], low[:lines, :])
        if lines < rows:
            out[lines:, :] = low[lines:, :]

    return pl.pallas_call(
        kernel,
        in_specs=[VMEM] * 2,
        out_shape=pltpu.VMEM((rows, LANES), BF),
        out_specs=VMEM,
        compiler_params=pltpu.CompilerParams(vmem_limit_bytes=2**20),
        cost_estimate=pl.CostEstimate(flops=0, bytes_accessed=2**17, transcendentals=0),
    )(in_vmem(low), in_vmem(high))


def finish_kernel(high, one, one_far, two, two_far, grad, notes):
    lower = (place() & 16) == 0

    for begin, near, far in ((0, one, one_far), (PART, two, two_far)):
        upper = high[begin : begin + PART, :].astype(F32)
        mine = jnp.where(lower, near[:PART, :].astype(F32), upper)
        grad[begin : begin + PART, :] = mine + far[:PART, :].astype(F32)
    tail = one[PART:, :].astype(F32) + one_far[PART:, :].astype(F32)
    row = jnp.where(lower, tail, 0.0)
    value = grad[...]
    square = jnp.sum(jnp.sum(value * value, axis=0, keepdims=True), axis=1, keepdims=True)
    square = square + jnp.sum(jnp.sum(row * row, axis=0, keepdims=True), axis=1, keepdims=True)
    line = lax.broadcasted_iota(jnp.int32, (8, LANES), 0)
    note = jnp.where(line < 4, row[:8], square)
    for device in range(notes.shape[0]):
        notes[device] = note


def finish_call(count, *operands):
    outs = (pltpu.VMEM((BLOCK, LANES), F32), pltpu.VMEM((count, 8, LANES), F32))
    return pl.pallas_call(
        finish_kernel,
        in_specs=[VMEM] * len(operands),
        out_shape=outs,
        out_specs=tuple(VMEM for _ in outs),
        compiler_params=pltpu.CompilerParams(vmem_limit_bytes=8 * 2**20),
        cost_estimate=pl.CostEstimate(flops=10**6, bytes_accessed=2**20, transcendentals=0),
    )(*(in_vmem(value) for value in operands))


def update_kernel(
    grad, notes, first, second, weights, vectors, vector_first, vector_second,
    first_out, second_out, weights_out, vectors_first_out, vectors_second_out, vectors_out,
    bias_out, norm_out, sums,
):
    square = jnp.sum(notes[:, 4, :], axis=0, keepdims=True)
    norm = jnp.sqrt(square)
    factor = jnp.minimum(1.0, clip_norm / (norm + 1e-06))
    norm_out[...] = norm
    for row in range(sums.shape[0]):
        for j in range(D // LANES):
            sums[row : row + 1, j * LANES : (j + 1) * LANES] = notes[row, j : j + 1, :]
    first_out[...], second_out[...], weights_out[...] = adam_update(
        grad[...] * factor, first[...], second[...], weights[...], learn_rate, decay_weight
    )
    clipped = sums[...] * jnp.concatenate([factor] * (D // LANES), axis=1)
    bias_out[...] = clipped[9:10, :]
    vectors_first_out[...], vectors_second_out[...], vectors_out[...] = adam_update(
        clipped, vector_first[...], vector_second[...], vectors[...], vector_rate, 0.0
    )


def update_call(*operands):
    shape = jax.ShapeDtypeStruct
    lines, rows = operands[2].shape, operands[5].shape
    outs = (
        [shape(lines, F32)] * 3
        + [shape(rows, F32)] * 3
        + [shape((1, rows[1]), F32), shape((1, LANES), F32)]
    )
    return pl.pallas_call(
        update_kernel,
        in_specs=[VMEM] * len(operands),
        out_shape=outs,
        out_specs=[VMEM for _ in outs],
        scratch_shapes=[pltpu.VMEM(rows, F32)],
        compiler_params=pltpu.CompilerParams(vmem_limit_bytes=12 * 2**20),
        cost_estimate=pl.CostEstimate(flops=10**7, bytes_accessed=2**22, transcendentals=10**6),
    )(*operands)


def join_kernel(own_out, own_latent, pack, block_out, latent_out, out_wide, latent_wide, sem):
    side = lax.axis_index("blk")
    mine = pl.ds(side * MINE, MINE)
    other = pl.ds((1 - side) * MINE, MINE)
    half = SLOTS // 2
    copies = [
        pltpu.make_async_copy(own_out, block_out.at[mine], sem.at[0]),
        pltpu.make_async_copy(own_latent, latent_out.at[mine], sem.at[1]),
        pltpu.make_async_copy(out_wide, block_out.at[other], sem.at[2]),
        pltpu.make_async_copy(latent_wide, latent_out.at[other], sem.at[3]),
    ]
    copies[0].start()
    copies[1].start()
    for image in range(MINE):
        out_wide[image] = pack[image, :half, :].astype(F32)
        latent_wide[image, :, :D] = pack[image, half : half + KMAX // 2, :].astype(F32)
        last = pack[image, half + KMAX // 2 :, :].astype(F32)
        latent_wide[image, : KMAX // 4, D:] = last[:, : DIN - D]
        latent_wide[image, KMAX // 4 :, D:] = last[:, DIN - D :]
    copies[2].start()
    copies[3].start()
    for copy in copies:
        copy.wait()


def join_call(own_out, own_latent, pack, images):
    shape = jax.ShapeDtypeStruct
    return pl.pallas_call(
        join_kernel,
        in_specs=[VMEM] * 3,
        out_shape=(
            shape((images, *own_out.shape[1:]), F32),
            shape((images, *own_latent.shape[1:]), F32),
        ),
        out_specs=(ANY, ANY),
        scratch_shapes=[
            pltpu.VMEM(own_out.shape, F32),
            pltpu.VMEM(own_latent.shape, F32),
            pltpu.SemaphoreType.DMA((4,)),
        ],
        compiler_params=pltpu.CompilerParams(vmem_limit_bytes=4 * 2**20),
        cost_estimate=pl.CostEstimate(flops=0, bytes_accessed=2**21, transcendentals=0),
    )(own_out, own_latent, pack)


def after(value, *others):
    if not others:
        return value
    return lax.optimization_barrier((value, *others))[0]


def local(
    grid,
    latents,
    restore,
    bucket,
    cotangent,
    flat_weights,
    flat_first,
    flat_second,
    vectors,
    vector_first,
    vector_second,
):
    side = lax.axis_index("blk").astype(jnp.int32)
    by_hand = grid.by_hand

    def trade(value):
        return lax.ppermute(value, "blk", [(0, 1), (1, 0)])

    out_latents, out_cotangent, out_restore = pick_call(latents, cotangent, restore)
    lines = grid.gather(flat_weights.reshape(-1, LANES).astype(BF))
    slot = (jnp.arange(SLOTS, dtype=jnp.int32) + side * (SLOTS // 2)) & (SLOTS - 1)
    position = position_rows(slot)
    my_latents, choice, my_position = prepare_call(
        latents, trade(after(out_latents, *grid.early)), restore,
        trade(after(out_restore, *grid.early)), position,
    )
    far_cotangent = trade(after(out_cotangent, *grid.late))
    (
        probs, shares, joint, normed, start, middle, mixed, embed_w, joint_w, output_w,
    ) = forward_call(bucket, my_latents, choice, my_position, vectors, lines)
    (
        own_out, far_out, hat, scale, back_out, acc_back, head_lines, far_high, near_high, expand_b,
    ) = middle_call(by_hand, bucket, middle, cotangent, far_cotangent, vectors, lines)
    if by_hand:
        high = Reduction(grid, far_high, near_high, 1)
    back_middle, back_mixed, out_lines, rows_b = branch_call(
        hat, scale, back_out, acc_back, mixed, output_w, vectors
    )
    if by_hand:
        back_mixed = after(back_mixed, high.hop(back_mixed))
    joint_lines, back_start, rows_joint = attention_back_call(
        probs, shares, joint, back_mixed, normed, start, back_middle, vectors, joint_w
    )
    if by_hand:
        back_start = after(back_start, high.hop(back_start))
    far_one, near_one, far_two, near_two, rows_c, own_latent, pack = input_back_call(
        by_hand, back_start, my_latents, choice, embed_w, joint_lines, rows_joint, out_lines,
        head_lines, rows_b, expand_b,
        far_out,
    )
    if by_hand:
        one = Reduction(grid, far_one, near_one, 0)
        two = Reduction(grid, far_two, near_two, 0)
        mark = far_one
        for stream in (one, two, high, one, two, high, one, two, one, two):
            mark = stream.hop(mark)
            if stream is two:
                pack_mark = mark
        across = [
            grid.send(cross_call(stream.head, high.head, at), 16)
            for stream, at in ((one, 0), (two, PART))
        ]
        pack = after(pack, pack_mark)
    block_out, latent_out = join_call(own_out, own_latent, trade(pack), latents.shape[0])

    if by_hand:
        grad, notes = finish_call(
            grid.count, high.head, one.head, across[0], two.head, across[1]
        )
        notes = lax.all_to_all(notes, grid.axes, 0, 0, tiled=True)
        lines = [value.reshape(-1, LANES) for value in (flat_first, flat_second, flat_weights)]
        outs = update_call(grad, notes, *lines, vectors, vector_first, vector_second)
        return (
            block_out,
            latent_out,
            *(value.reshape(-1) for value in outs[:3]),
            *outs[3:6],
            outs[6].reshape(-1),
            outs[7][0, 0],
        )

    low = [
        jnp.concatenate([far, near], axis=0).reshape(16, -1, LANES)[:, :PART]
        for far, near in ((far_one, near_one), (far_two, near_two))
    ]
    flat = jnp.concatenate(
        [jnp.concatenate(low, axis=1).reshape(-1), far_high.reshape(-1), near_high.reshape(-1)]
    )
    shard_grad = lax.psum_scatter(flat, grid.axes, scatter_dimension=0, tiled=True)
    shard_grad = shard_grad.astype(F32).reshape(-1, LANES)
    vector_sum = lax.psum(rows_c[: vectors.shape[0]], grid.axes)
    square_sum = lax.psum(jnp.sum(shard_grad * shard_grad), grid.axes)
    grad_norm = jnp.sqrt(square_sum + jnp.sum(vector_sum * vector_sum))
    factor = jnp.minimum(1.0, clip_norm / (grad_norm + 1e-06))
    new_first, new_second, new_weights = adam_update(
        shard_grad.reshape(-1) * factor,
        flat_first,
        flat_second,
        flat_weights,
        learn_rate,
        decay_weight,
    )
    vector_first_new, vector_second_new, vectors_new = adam_update(
        vector_sum * factor, vector_first, vector_second, vectors, vector_rate, 0.0
    )
    reduce_bias_grad = vector_sum[9] * factor
    return (
        block_out,
        latent_out,
        new_first,
        new_second,
        new_weights,
        vector_first_new,
        vector_second_new,
        vectors_new,
        reduce_bias_grad,
        grad_norm,
    )


def solution(mesh):
    grid = Grid(mesh)
    return jax.shard_map(
        lambda *args: local(grid, *args),
        mesh=mesh,
        in_specs=(
            P("dp", "blk", None),
            P("dp", "blk"),
            P("dp"),
            P("dp", "blk", None),
            P(("dp", "blk")),
            P(("dp", "blk")),
            P(("dp", "blk")),
            P(),
            P(),
            P(),
        ),
        out_specs=(
            P("dp", "blk", None),
            P("dp", "blk", None),
            P(("dp", "blk")),
            P(("dp", "blk")),
            P(("dp", "blk")),
            P(),
            P(),
            P(),
            P(),
            P(),
        ),
        check_vma=False,
    )
```

```python
import math

import jax
import jax.numpy as jnp
from jax import lax
from jax.experimental import pallas as pl
from jax.experimental.pallas import tpu as pltpu
from jax.sharding import PartitionSpec as P

DIN = 768
D = 512
HEADS = 16
HD = 32
FF = 2048
SLOTS = 256
KMAX = 64
STEP = 10
NPARAM = 3538944

first_decay = 0.9
second_decay = 0.95
learn_rate = 0.05
vector_rate = 0.5
decay_weight = 0.05
adam_eps = 1e-08
clip_norm = 1.0

BF = jnp.bfloat16
F32 = jnp.float32

LANES = 128
LINES = NPARAM // LANES
EMBED_AT = 0
JOINT_AT = EMBED_AT + DIN * D // LANES
OUTPUT_AT = JOINT_AT + 3 * D * D // LANES
EXPAND_AT = OUTPUT_AT + D * D // LANES
REDUCE_AT = EXPAND_AT + D * FF // LANES
BLOCK = LINES // 32
HALF = 16 * BLOCK
TAIL = 16
ROWS = 16
PART = BLOCK // 2
PARTS = (PART + TAIL, PART)
TILE = 256
TILES = FF // TILE
GROUP = 4
GROUPS = HEADS // GROUP
MINE = 2
TOKENS = MINE * SLOTS
PICKS = KMAX + 16
PACK = SLOTS // 2 + KMAX // 2 + KMAX // 4
VMEM = pl.BlockSpec(memory_space=pltpu.VMEM)
SMEM = pl.BlockSpec(memory_space=pltpu.SMEM)
ANY = pl.BlockSpec(memory_space=pl.ANY)


def position_rows(slot):
    column = jnp.arange(D // 2, dtype=jnp.int32).astype(F32)[None, :]
    angle = slot.astype(F32)[:, None] * jnp.exp(-math.log(10000.0) * column / (D // 2))
    return jnp.concatenate([jnp.sin(angle), jnp.cos(angle)], axis=1)


def adam_update(grad, first, second, weight, rate, shrink):
    first_new = first_decay * first + (1.0 - first_decay) * grad
    second_new = second_decay * second + (1.0 - second_decay) * grad * grad
    first_hat = first_new / (1.0 - first_decay**STEP)
    second_hat = second_new / (1.0 - second_decay**STEP)
    weight_new = weight - rate * (first_hat / (jnp.sqrt(second_hat) + adam_eps) + shrink * weight)
    return (first_new, second_new, weight_new)


def dot(left, right, over=(1, 0)):
    return lax.dot_general(
        left, right, (((over[0],), (over[1],)), ((), ())), preferred_element_type=F32
    )


def place():
    return lax.axis_index("dp") * lax.axis_size("blk") + lax.axis_index("blk")


def collect_call(lines, pieces, places):
    def kernel(*refs):
        out = refs[-1]
        me = place()
        odd = (me >> 1) & 1
        for (bits, even, uneven), piece in zip(places, refs[-1 - len(pieces) : -1], strict=True):
            block = me ^ bits ^ jnp.where(odd == 0, even, uneven)
            out[pl.ds(pl.multiple_of(block * BLOCK, 16), BLOCK), :] = piece[...]

    given = ([] if lines is None else [lines]) + list(pieces)
    return pl.pallas_call(
        kernel,
        in_specs=[VMEM] * len(given),
        out_shape=pltpu.VMEM((LINES, LANES), BF),
        out_specs=VMEM,
        input_output_aliases={} if lines is None else {0: 0},
        compiler_params=pltpu.CompilerParams(vmem_limit_bytes=2 * 2**20),
        cost_estimate=pl.CostEstimate(flops=0, bytes_accessed=2**20, transcendentals=0),
    )(*(in_vmem(value) for value in given))


def lines_to_matrix(lines, stage, matrix, at, rows, wide, batch):
    size = batch * wide

    def body(index, carry):
        for part in range(2):
            row = pl.multiple_of((2 * index + part) * batch, batch)
            source = pl.multiple_of(at + (2 * index + part) * size, 16)
            stage[part, :size, :] = lines[pl.ds(source, size), :].astype(F32)
            for j in range(wide):
                matrix[pl.ds(row, batch), j * LANES : (j + 1) * LANES] = stage[
                    part, pl.ds(j, batch, stride=wide), :
                ].astype(BF)
        return carry

    lax.fori_loop(0, rows // batch // 2, body, 0)


def norm_parts(value):
    centred = value - jnp.mean(value, axis=-1, keepdims=True)
    scale = lax.rsqrt(jnp.mean(centred * centred, axis=-1, keepdims=True) + 1e-06)
    return centred * scale, scale


def norm_back(grad, hat, scale, gain):
    inner = grad * gain
    return scale * (
        inner
        - jnp.mean(inner, axis=-1, keepdims=True)
        - hat * jnp.mean(inner * hat, axis=-1, keepdims=True)
    )


def total(value):
    return jnp.sum(value.astype(F32), axis=0, keepdims=True)


def slot_column(side):
    local = lax.broadcasted_iota(jnp.int32, (SLOTS, 1), 0)
    return (local + side * (SLOTS // 2)) & (SLOTS - 1)


def image_length(bucket, image):
    kind = bucket[image]
    return jnp.where(
        kind == 0, SLOTS * 100 // 256, jnp.where(kind == 1, SLOTS * 196 // 256, SLOTS)
    )


def select_rows(own, far, side):
    half = SLOTS // 2
    row = lax.broadcasted_iota(jnp.int32, (PICKS, half), 0)
    row = jnp.where(row < KMAX, (row + side * (KMAX // 2)) & (KMAX - 1), row)
    parts = [
        (row == names).astype(F32) for names in (own, far)
    ]
    return jnp.concatenate(parts, axis=1).astype(BF)


def three_parts(value):
    high = value.astype(BF)
    rest = value - high.astype(F32)
    mid = rest.astype(BF)
    return high, mid, (rest - mid.astype(F32)).astype(BF)


def head_mask(head):
    lane = lax.broadcasted_iota(jnp.int32, (1, LANES), 1)
    return (lane // HD) == head


def mask_head(value, head):
    return jnp.where(head_mask(head), value, jnp.zeros_like(value))


def pick_kernel(latents, cotangent, restore, far_latents, far_cotangent, far_restore, sem):
    first = (1 - lax.axis_index("blk")) * MINE
    copies = [
        pltpu.make_async_copy(source.at[pl.ds(first, MINE)], target, sem.at[index])
        for index, (source, target) in enumerate(
            ((latents, far_latents), (cotangent, far_cotangent))
        )
    ]
    for copy in copies:
        copy.start()
    for image in range(MINE):
        far_restore[image : image + 1, :] = restore[pl.ds(first + image, 1), :]
    for copy in copies:
        copy.wait()


def pick_call(latents, cotangent, restore):
    outs = tuple(
        pltpu.VMEM((MINE, *value.shape[1:]), value.dtype) for value in (latents, cotangent, restore)
    )
    return pl.pallas_call(
        pick_kernel,
        in_specs=[ANY, ANY, VMEM],
        out_shape=outs,
        out_specs=tuple(VMEM for _ in outs),
        scratch_shapes=[pltpu.SemaphoreType.DMA((2,))],
        compiler_params=pltpu.CompilerParams(vmem_limit_bytes=2 * 2**20),
        cost_estimate=pl.CostEstimate(flops=0, bytes_accessed=2**19, transcendentals=0),
    )(in_hbm(latents), in_hbm(cotangent), restore)


def prepare_kernel(
    latents, far_latents, restore, far_restore, position, my_latents, choice, my_position,
    near_buffer, sem,
):
    side = lax.axis_index("blk")
    copy = pltpu.make_async_copy(latents.at[pl.ds(side * MINE, MINE)], near_buffer, sem)
    copy.start()
    my_position[...] = position[...]
    for image in range(MINE):
        choice[image] = select_rows(
            restore[pl.ds(side * MINE + image, 1), :], far_restore[image : image + 1, :], side
        )
    copy.wait()
    half = KMAX // 2
    for image in range(MINE):
        at = image * KMAX
        my_latents[at : at + half, :] = near_buffer[image]
        my_latents[at + half : at + KMAX, :] = far_latents[image]


def prepare_call(*operands):
    outs = (
        pltpu.VMEM((MINE * KMAX, DIN), BF),
        pltpu.VMEM((MINE, PICKS, SLOTS), BF),
        pltpu.VMEM((SLOTS, D), F32),
    )
    return pl.pallas_call(
        prepare_kernel,
        in_specs=[ANY, VMEM, VMEM, VMEM, VMEM],
        out_shape=outs,
        out_specs=tuple(VMEM for _ in outs),
        scratch_shapes=[
            pltpu.VMEM((MINE, KMAX // 2, DIN), BF),
            pltpu.SemaphoreType.DMA,
        ],
        compiler_params=pltpu.CompilerParams(vmem_limit_bytes=4 * 2**20),
        cost_estimate=pl.CostEstimate(flops=10**6, bytes_accessed=2**20, transcendentals=0),
    )(in_hbm(operands[0]), *operands[1:])


def forward_kernel(bucket, my_latents, choice, position, vectors, lines, *rest):
    (
        probs,
        shares,
        joint,
        normed,
        start,
        middle,
        mixed,
        embed_w,
        joint_w,
        output_w,
        stage,
        query_t,
        value_t,
        mixed_t,
        scores_even,
        scores_odd,
    ) = rest
    side = lax.axis_index("blk")
    lines_to_matrix(lines, stage, embed_w, EMBED_AT, DIN, 4, 128)
    lines_to_matrix(lines, stage, joint_w, JOINT_AT, D, 12, 64)
    lines_to_matrix(lines, stage, output_w, OUTPUT_AT, D, 4, 128)
    embedded = (dot(my_latents[...], embed_w[...]) + vectors[0:1, :]).astype(BF)
    token = list(three_parts(vectors[1:2, :]))
    for image in range(MINE):
        rows = slice(image * SLOTS, (image + 1) * SLOTS)
        picked = choice[image]
        value = dot(picked[:KMAX], embedded[image * KMAX : (image + 1) * KMAX, :], (0, 0))
        masked = jnp.broadcast_to(picked[KMAX : KMAX + 1], (16, SLOTS))
        table = jnp.concatenate(token + [jnp.zeros((13, D), BF)], axis=0)
        value = value + dot(masked, table, (0, 0)) + position[...]
        start[rows, :] = value
        hat, _ = norm_parts(value)
        normed[rows, :] = (hat * vectors[2:3, :] + vectors[3:4, :]).astype(BF)
    for part, bias in enumerate((4, None, 5)):
        columns = slice(part * D, (part + 1) * D)
        out = dot(normed[...], joint_w[:, columns])
        if bias is not None:
            out = out + vectors[bias : bias + 1, :]
        joint[:, columns] = out.astype(BF)
    query_t[...] = joint[:, :D].T
    value_t[...] = joint[:, 2 * D :].T

    rate = HD**-0.5 * math.log2(math.e)

    def score(unit, target):
        image, group = unit // GROUPS, unit % GROUPS
        rows = pl.ds(pl.multiple_of(image * SLOTS, SLOTS), SLOTS)
        keys = joint[rows, pl.ds(pl.multiple_of(D + group * LANES, LANES), LANES)]
        queries = query_t[pl.ds(pl.multiple_of(group * LANES, LANES), LANES), rows]
        for head in range(GROUP):
            target[head] = dot(mask_head(keys, head), queries)

    def mix(unit, source):
        image, group = unit // GROUPS, unit % GROUPS
        rows = pl.ds(pl.multiple_of(image * SLOTS, SLOTS), SLOTS)
        length = image_length(bucket, side * MINE + image)
        hidden_key = jnp.where(slot_column(side) < length, 0.0, -1e30)
        for head in range(GROUP):
            scores = source[head] + hidden_key
            top = jnp.max(scores, axis=0, keepdims=True)
            raised = jnp.exp2((scores - top) * rate)
            share = 1.0 / jnp.sum(raised, axis=0, keepdims=True)
            low = raised.astype(BF)
            probs[unit * GROUP + head] = low
            shares[pl.ds(unit * GROUP + head, 1), :] = share
            features = pl.ds(pl.multiple_of(group * LANES + head * HD, HD), HD)
            mixed_t[features, rows] = (dot(value_t[features, rows], low) * share).astype(BF)

    score(0, scores_even)

    def pair(index, carry):
        unit = 2 * index
        score(unit + 1, scores_odd)
        mix(unit, scores_even)
        score(jnp.minimum(unit + 2, MINE * GROUPS - 1), scores_even)
        mix(unit + 1, scores_odd)
        return carry

    lax.fori_loop(0, MINE * GROUPS // 2, pair, 0)
    mixed[...] = mixed_t[...].T
    middle[...] = start[...] + dot(mixed[...], output_w[...]) + vectors[6:7, :]


def forward_call(*operands):
    outs = (
        pltpu.VMEM((MINE * HEADS, SLOTS, SLOTS), BF),
        pltpu.VMEM((MINE * HEADS, SLOTS), F32),
        pltpu.VMEM((TOKENS, 3 * D), BF),
        pltpu.VMEM((TOKENS, D), BF),
        pltpu.VMEM((TOKENS, D), F32),
        pltpu.VMEM((TOKENS, D), F32),
        pltpu.VMEM((TOKENS, D), BF),
        pltpu.VMEM((DIN, D), BF),
        pltpu.VMEM((D, 3 * D), BF),
        pltpu.VMEM((D, D), BF),
    )
    return pl.pallas_call(
        forward_kernel,
        in_specs=[SMEM] + [VMEM] * (len(operands) - 1),
        out_shape=outs,
        out_specs=tuple(VMEM for _ in outs),
        scratch_shapes=[
            pltpu.VMEM((2, 768, LANES), F32),
            pltpu.VMEM((D, TOKENS), BF),
            pltpu.VMEM((D, TOKENS), BF),
            pltpu.VMEM((D, TOKENS), BF),
            pltpu.VMEM((GROUP, SLOTS, SLOTS), F32),
            pltpu.VMEM((GROUP, SLOTS, SLOTS), F32),
        ],
        compiler_params=pltpu.CompilerParams(vmem_limit_bytes=10 * 2**20),
        cost_estimate=pl.CostEstimate(
            flops=6 * 10**9, bytes_accessed=16 * 2**20, transcendentals=2 * 10**6
        ),
    )(*operands)


def middle_kernel(
    by_hand, bucket, middle, cotangent, far_cotangent, vectors, lines, *rest
):
    (
        own_out,
        far_out,
        hat,
        scale,
        back_out,
        acc_back,
        head_lines,
        far_lines,
        near_lines,
        expand_out,
        stage,
        expand_w,
        reduce_w,
        normed,
        normed_t,
        acc,
        grads,
    ) = rest
    step = pl.program_id(0)
    side = lax.axis_index("blk")

    @pl.when(step == 0)
    def _():
        value, spread = norm_parts(middle[...])
        hat[...] = value
        scale[...] = jnp.broadcast_to(spread, scale.shape)
        normed[...] = (value * vectors[7:8, :] + vectors[8:9, :]).astype(BF)
        normed_t[...] = normed[...].T
        for image in range(MINE):
            valid = slot_column(side) < image_length(bucket, side * MINE + image)
            half = SLOTS // 2
            for part, (ref, at) in enumerate(
                ((cotangent, side * MINE + image), (far_cotangent, image))
            ):
                first = image * SLOTS + part * half
                back_out[first : first + half, :] = jnp.where(
                    valid[part * half : (part + 1) * half, :],
                    ref[at].astype(F32),
                    0.0,
                ).astype(BF)
        acc[...] = jnp.zeros_like(acc)
        acc_back[...] = jnp.zeros_like(acc_back)
        lines_to_matrix(lines, stage, expand_w, EXPAND_AT, D, 16, 32)
        lines_to_matrix(lines, stage, reduce_w, REDUCE_AT, FF, 4, 128)

    columns = pl.ds(pl.multiple_of(step * TILE, TILE), TILE)
    expand = expand_w[:, columns]
    reduce = reduce_w[columns, :]
    bias = vectors[pl.ds(10 + step // 2, 1), pl.ds(pl.multiple_of((step % 2) * TILE, TILE), TILE)]
    hidden = dot(normed[...], expand) + bias
    density = jnp.exp(hidden * hidden * -0.5) * (1.0 / math.sqrt(2.0 * math.pi))
    below = 0.5 + 0.5 * lax.erf(hidden * math.sqrt(0.5))
    active = (hidden * below).astype(BF)
    back_active = dot(back_out[...], reduce, (1, 1))
    back_hidden = (back_active * (below + hidden * density)).astype(BF)
    acc[...] += dot(active, reduce)
    acc_back[...] += dot(back_hidden, expand, (1, 1))
    grad_reduce = dot(active, back_out[...], (0, 0))
    for j in range(4):
        grads[pl.ds(D * 16 + step * (TILE * 4) + j, TILE, stride=4), :] = grad_reduce[
            :, j * LANES : (j + 1) * LANES
        ]
    grad_expand = dot(normed_t[...], back_hidden)
    for j in range(TILE // LANES):
        grads[pl.ds(step * (TILE // LANES) + j, D, stride=16), :] = grad_expand[
            :, j * LANES : (j + 1) * LANES
        ]
    expand_out[pl.ds(step, 1), :] = total(back_hidden)

    @pl.when(step == TILES - 1)
    def _():
        for image in range(MINE):
            near = slice(image * SLOTS, image * SLOTS + SLOTS // 2)
            far = slice(image * SLOTS + SLOTS // 2, (image + 1) * SLOTS)
            own_out[image] = middle[near, :] + acc[near, :] + vectors[9:10, :]
            far_out[image] = (middle[far, :] + acc[far, :] + vectors[9:10, :]).astype(BF)
        cut = HALF - EXPAND_AT
        head_lines[...] = grads[:cut, :].astype(BF)
        put_blocks(
            by_hand,
            far_lines,
            near_lines,
            lambda q: grads[pl.ds(cut + q * BLOCK, BLOCK), :].astype(BF),
        )


def slot_of(index, by_hand):
    if not by_hand:
        return index
    me = place()
    rel = index ^ (me & 15)
    other = (rel >> 1) & 1
    odd = ((me >> 1) & 1) ^ other
    along_y, along_x, along_z = rel & 1, (rel >> 2) & 1, rel >> 3
    first = jnp.where(odd == 0, along_y, along_x)
    second = jnp.where(odd == 0, along_x, along_y)
    slot = (1 - first) * 4 + (1 - second) * 2 + (1 - along_z)
    return slot + jnp.where(other == 1, 0, 8)


def put_blocks(by_hand, far_lines, near_lines, block_of):
    def body(index, carry):
        slot = slot_of(index, by_hand)
        value = block_of(index)

        @pl.when(slot < 8)
        def _():
            far_lines[pl.ds(pl.multiple_of(slot * BLOCK, 16), BLOCK), :] = value

        @pl.when(slot >= 8)
        def _():
            near_lines[pl.ds(pl.multiple_of((slot - 8) * BLOCK, 16), BLOCK), :] = value

        return carry

    lax.fori_loop(0, 16, body, 0)


def middle_call(by_hand, *operands):
    outs = (
        pltpu.VMEM((MINE, SLOTS // 2, D), F32),
        pltpu.VMEM((MINE, SLOTS // 2, D), BF),
        pltpu.VMEM((TOKENS, D), F32),
        pltpu.VMEM((TOKENS, LANES), F32),
        pltpu.VMEM((TOKENS, D), BF),
        pltpu.VMEM((TOKENS, D), F32),
        pltpu.VMEM((HALF - EXPAND_AT, LANES), BF),
        pltpu.VMEM((8 * BLOCK, LANES), BF),
        pltpu.VMEM((8 * BLOCK, LANES), BF),
        pltpu.VMEM((TILES, TILE), F32),
    )
    return pl.pallas_call(
        lambda *refs: middle_kernel(by_hand, *refs),
        grid=(TILES,),
        in_specs=[SMEM] + [VMEM] * (len(operands) - 1),
        out_shape=outs,
        out_specs=tuple(VMEM for _ in outs),
        scratch_shapes=[
            pltpu.VMEM((2, 768, LANES), F32),
            pltpu.VMEM((D, FF), BF),
            pltpu.VMEM((FF, D), BF),
            pltpu.VMEM((TOKENS, D), BF),
            pltpu.VMEM((D, TOKENS), BF),
            pltpu.VMEM((TOKENS, D), F32),
            pltpu.VMEM((2 * D * 16, LANES), F32),
        ],
        compiler_params=pltpu.CompilerParams(vmem_limit_bytes=20 * 2**20),
        cost_estimate=pl.CostEstimate(
            flops=8 * 10**9, bytes_accessed=16 * 2**20, transcendentals=2 * 10**6
        ),
    )(*operands)


def branch_kernel(
    hat, scale, back_out, acc_back, mixed, output_w, vectors,
    back_middle, back_mixed, out_lines, rows_out, out_grads,
):
    grad = acc_back[...]
    rows_out[...] = jnp.zeros_like(rows_out)
    rows_out[1:2, :] = total(grad * hat[...])
    rows_out[2:3, :] = total(grad)
    rows_out[3:4, :] = total(back_out[...])
    back = back_out[...].astype(F32) + norm_back(
        grad, hat[...], scale[:, :1], vectors[7:8, :]
    )
    back_middle[...] = back
    branch = back.astype(BF)
    rows_out[0:1, :] = total(branch)
    back_mixed[...] = dot(branch, output_w[...], (1, 1)).astype(BF)
    grad_output = dot(mixed[...], branch, (0, 0))
    for j in range(4):
        out_grads[pl.ds(j, D, stride=4), :] = grad_output[:, j * LANES : (j + 1) * LANES]
    out_lines[...] = out_grads[...].astype(BF)


def branch_call(hat, scale, back_out, acc_back, mixed, output_w, vectors):
    outs = (
        pltpu.VMEM((TOKENS, D), F32),
        pltpu.VMEM((TOKENS, D), BF),
        pltpu.VMEM((EXPAND_AT - OUTPUT_AT, LANES), BF),
        pltpu.VMEM((8, D), F32),
    )
    return pl.pallas_call(
        branch_kernel,
        in_specs=[VMEM] * 7,
        out_shape=outs,
        out_specs=tuple(VMEM for _ in outs),
        scratch_shapes=[pltpu.VMEM((D * 4, LANES), F32)],
        compiler_params=pltpu.CompilerParams(vmem_limit_bytes=16 * 2**20),
        cost_estimate=pl.CostEstimate(
            flops=2 * 10**9, bytes_accessed=4 * 2**20, transcendentals=0
        ),
    )(hat, scale, back_out, acc_back, mixed, output_w, vectors)


def attention_back_kernel(
    probs, shares, joint, back_mixed, normed, start, back_middle, vectors, joint_w,
    joint_lines, back_start, rows_out,
    joint_back, key_t, back_t, shared_t, shared, query_back_t, even, odd, grads,
):
    key_t[...] = joint[:, D : 2 * D].T
    back_t[...] = back_mixed[...].T
    for image in range(MINE):
        columns = slice(image * SLOTS, (image + 1) * SLOTS)
        for head in range(HEADS):
            features = slice(head * HD, (head + 1) * HD)
            at = image * HEADS + head
            shared_t[features, columns] = (
                back_t[features, columns].astype(F32) * shares[at : at + 1, :]
            ).astype(BF)
    shared[...] = shared_t[...].T

    def pull_back(unit, target):
        image, group = unit // GROUPS, unit % GROUPS
        rows = pl.ds(pl.multiple_of(image * SLOTS, SLOTS), SLOTS)
        values = joint[rows, pl.ds(pl.multiple_of(2 * D + group * LANES, LANES), LANES)]
        back_lanes = back_t[pl.ds(pl.multiple_of(group * LANES, LANES), LANES), rows]
        for head in range(GROUP):
            target[head] = dot(mask_head(values, head), back_lanes)

    def spread(unit, source):
        image, group = unit // GROUPS, unit % GROUPS
        rows = pl.ds(pl.multiple_of(image * SLOTS, SLOTS), SLOTS)
        lanes = pl.ds(pl.multiple_of(group * LANES, LANES), LANES)
        queries = joint[rows, lanes]
        back = shared[rows, lanes]
        key_back = jnp.zeros((SLOTS, LANES), F32)
        value_back = jnp.zeros((SLOTS, LANES), F32)
        for head in range(GROUP):
            low = probs[unit * GROUP + head]
            share = shares[pl.ds(unit * GROUP + head, 1), :]
            wide = low.astype(F32)
            back_probs = source[head]
            pull = jnp.sum(wide * back_probs, axis=0, keepdims=True) * share
            score_back = (wide * ((back_probs - pull) * (share * HD**-0.5))).astype(BF)
            value_back = value_back + dot(low, mask_head(back, head))
            key_back = key_back + dot(score_back, mask_head(queries, head))
            features = pl.ds(pl.multiple_of(group * LANES + head * HD, HD), HD)
            query_back_t[features, rows] = dot(key_t[features, rows], score_back).astype(BF)
        joint_back[rows, pl.ds(pl.multiple_of(D + group * LANES, LANES), LANES)] = (
            key_back.astype(BF)
        )
        joint_back[rows, pl.ds(pl.multiple_of(2 * D + group * LANES, LANES), LANES)] = (
            value_back.astype(BF)
        )

    pull_back(0, even)

    def pair(index, carry):
        unit = 2 * index
        pull_back(unit + 1, odd)
        spread(unit, even)
        pull_back(jnp.minimum(unit + 2, MINE * GROUPS - 1), even)
        spread(unit + 1, odd)
        return carry

    lax.fori_loop(0, MINE * GROUPS // 2, pair, 0)
    joint_back[:, :D] = query_back_t[...].T
    rows_out[...] = jnp.zeros_like(rows_out)
    rows_out[2:3, :] = total(joint_back[:, :D])
    rows_out[3:4, :] = total(joint_back[:, 2 * D :])
    normed_t = normed[...].T
    for part in range(3):
        grad_joint = dot(normed_t, joint_back[:, part * D : (part + 1) * D])
        for j in range(4):
            grads[pl.ds(part * 4 + j, D, stride=12), :] = grad_joint[
                :, j * LANES : (j + 1) * LANES
            ]
    grad = dot(joint_back[...], joint_w[...], (1, 1))
    hat, scale = norm_parts(start[...])
    rows_out[0:1, :] = total(grad * hat)
    rows_out[1:2, :] = total(grad)
    back_start[...] = back_middle[...] + norm_back(grad, hat, scale, vectors[2:3, :])
    joint_lines[...] = grads[...].astype(BF)


def input_back_kernel(
    by_hand,
    back_start,
    my_latents,
    choices,
    embed_w,
    joint_lines,
    rows_joint,
    out_lines,
    head_lines,
    rows_in,
    expand_in,
    far_out,
    far_first,
    near_first,
    far_second,
    near_second,
    rows_out,
    own_latent,
    pack,
    grads,
    tails,
):
    rows_out[...] = jnp.zeros_like(rows_out)
    rows_out[2:6, :] = rows_joint[0:4, :]
    low_start = back_start[...].astype(BF)
    low_rest = (back_start[...] - low_start.astype(F32)).astype(BF)
    picked = []
    token_back = jnp.zeros((1, D), F32)
    for image in range(MINE):
        part = slice(image * SLOTS, (image + 1) * SLOTS)
        choice = choices[image]
        chosen = dot(choice, low_start[part, :])
        picked.append(chosen[:KMAX, :].astype(BF))
        token_back = token_back + chosen[KMAX : KMAX + 1, :]
        token_back = token_back + dot(choice[KMAX:, :], low_rest[part, :])[:1, :]
    rows_out[1:2, :] = token_back
    embedded_back = jnp.concatenate(picked, axis=0)
    rows_out[0:1, :] = total(embedded_back)
    grad_embed = dot(my_latents[...], embedded_back, (0, 0))
    for j in range(4):
        grads[pl.ds(EMBED_AT + j, DIN, stride=4), :] = grad_embed[:, j * LANES : (j + 1) * LANES]
    latent_back = dot(embedded_back, embed_w[...], (1, 1))
    for image in range(MINE):
        at = image * KMAX
        own_latent[image] = latent_back[at : at + KMAX // 2, :]
        far = latent_back[at + KMAX // 2 : at + KMAX, :].astype(BF)
        pack[image, : SLOTS // 2, :] = far_out[image]
        pack[image, SLOTS // 2 : SLOTS // 2 + KMAX // 2, :] = far[:, :D]
        pack[image, SLOTS // 2 + KMAX // 2 :, : DIN - D] = far[: KMAX // 4, D:]
        pack[image, SLOTS // 2 + KMAX // 2 :, DIN - D :] = far[KMAX // 4 :, D:]
    rows_out[6:10, :] = rows_in[0:4, :]
    for j in range(4):
        rows_out[10 + j : 11 + j, :TILE] = expand_in[2 * j : 2 * j + 1, :]
        rows_out[10 + j : 11 + j, TILE:] = expand_in[2 * j + 1 : 2 * j + 2, :]
    tails[...] = jnp.zeros_like(tails)
    for row in range(ROWS):
        for j in range(D // LANES):
            tails[row * TAIL + j : row * TAIL + j + 1, :] = rows_out[
                row : row + 1, j * LANES : (j + 1) * LANES
            ]

    def store(index, value):
        slot = slot_of(index, by_hand)
        tail = tails[pl.ds(pl.multiple_of(index * TAIL, TAIL), TAIL), :].astype(BF)

        def put(first, second, at):
            row = pl.multiple_of(at * PARTS[0], 16)
            first[pl.ds(row, PART), :] = value[:PART]
            first[pl.ds(row + PART, TAIL), :] = tail
            second[pl.ds(pl.multiple_of(at * PART, 16), PART), :] = value[PART:]

        @pl.when(slot < 8)
        def _():
            put(far_first, far_second, slot)

        @pl.when(slot >= 8)
        def _():
            put(near_first, near_second, slot - 8)

    ranges = (
        (EMBED_AT, JOINT_AT, lambda low, high: grads[low:high, :].astype(BF)),
        (JOINT_AT, OUTPUT_AT, lambda low, high: joint_lines[low:high, :]),
        (OUTPUT_AT, EXPAND_AT, lambda low, high: out_lines[low:high, :]),
        (EXPAND_AT, HALF, lambda low, high: head_lines[low:high, :]),
    )
    for index in range(16):
        low, high = index * BLOCK, (index + 1) * BLOCK
        parts = [
            take(max(low, begin) - begin, min(high, end) - begin)
            for begin, end, take in ranges
            if max(low, begin) < min(high, end)
        ]
        store(index, jnp.concatenate(parts, axis=0) if len(parts) > 1 else parts[0])


def back_kernel(by_hand, *refs):
    attention, (my_latents, choices, embed_w, out_lines, head_lines, rows_in, expand_in, far_out) = (
        refs[:9], refs[9:17],
    )
    outs, scratch = refs[17:24], refs[24:]
    joint_lines, back_start, rows_joint = scratch[:3]
    attention_back_kernel(*attention, joint_lines, back_start, rows_joint, *scratch[3:12])
    input_back_kernel(
        by_hand, back_start, my_latents, choices, embed_w, joint_lines, rows_joint, out_lines,
        head_lines, rows_in, expand_in, far_out, *outs, *scratch[12:],
    )


def back_call(by_hand, *operands):
    shape = jax.ShapeDtypeStruct
    outs = (
        pltpu.VMEM((8 * PARTS[0], LANES), BF),
        pltpu.VMEM((8 * PARTS[0], LANES), BF),
        pltpu.VMEM((8 * PARTS[1], LANES), BF),
        pltpu.VMEM((8 * PARTS[1], LANES), BF),
        shape((ROWS, D), F32),
        pltpu.VMEM((MINE, KMAX // 2, DIN), F32),
        pltpu.VMEM((MINE, PACK, D), BF),
    )
    return pl.pallas_call(
        lambda *refs: back_kernel(by_hand, *refs),
        in_specs=[VMEM] * len(operands),
        out_shape=outs,
        out_specs=tuple(VMEM for _ in outs),
        scratch_shapes=[
            pltpu.VMEM((OUTPUT_AT - JOINT_AT, LANES), BF),
            pltpu.VMEM((TOKENS, D), F32),
            pltpu.VMEM((8, D), F32),
            pltpu.VMEM((TOKENS, 3 * D), BF),
            pltpu.VMEM((D, TOKENS), BF),
            pltpu.VMEM((D, TOKENS), BF),
            pltpu.VMEM((D, TOKENS), BF),
            pltpu.VMEM((TOKENS, D), BF),
            pltpu.VMEM((D, TOKENS), BF),
            pltpu.VMEM((GROUP, SLOTS, SLOTS), F32),
            pltpu.VMEM((GROUP, SLOTS, SLOTS), F32),
            pltpu.VMEM((OUTPUT_AT - JOINT_AT, LANES), F32),
            pltpu.VMEM((JOINT_AT, LANES), F32),
            pltpu.VMEM((ROWS * TAIL, LANES), F32),
        ],
        compiler_params=pltpu.CompilerParams(vmem_limit_bytes=24 * 2**20),
        cost_estimate=pl.CostEstimate(
            flops=4 * 10**9, bytes_accessed=8 * 2**20, transcendentals=0
        ),
    )(*operands)


class Grid:
    def __init__(self, mesh):
        self.axes = ("dp", "blk")
        self.count = mesh.shape["dp"] * mesh.shape["blk"]
        self.early = self.late = ()
        self.by_hand = self.count == 32 and mesh.shape["blk"] == 2

    def send(self, value, bits, other=None):
        other = bits if other is None else other
        pairs = [(i, i ^ (other if i & 2 else bits)) for i in range(self.count)]
        return lax.ppermute(value, self.axes, pairs)

    def gather(self, block):
        if not self.by_hand:
            whole = lax.all_gather(block, self.axes, axis=0, tiled=True)
            return whole.reshape(LINES, LANES)
        got = {"held0": block}

        def send(name, value, bits, other=None, behind=()):
            got[name] = self.send(after(got[value], *(got[b] for b in behind)), bits, other)

        def put(lines, *names):
            pieces, places = [], []
            for name in names:
                even, uneven = {"held": (0, 0), "near": (4, 1), "side": (1, 4), "far": (5, 5)}[
                    name.rstrip("0123456789")
                ]
                bits = int(name.lstrip("abcdefghijklmnopqrstuvwxyz"))
                pieces += [got[name], self.send(got[name], 2)]
                places += [(bits, even, uneven), (bits ^ 2, uneven, even)]
            return collect_call(lines, pieces, places)

        send("held16", "held0", 16)
        send("near0", "held0", 4, 1)
        send("held8", "held0", 8)
        send("side0", "held0", 1, 4)
        send("far0", "near0", 1, 4)
        send("near16", "held16", 4, 1)
        send("side16", "held16", 1, 4)
        send("held24", "held16", 8)
        send("near8", "held8", 4, 1)
        send("side8", "held8", 1, 4)
        send("far8", "far0", 8)
        send("far16", "near16", 1, 4, behind=("far0",))
        send("near24", "held24", 4, 1)
        send("side24", "held24", 1, 4, behind=("near16",))
        send("far24", "far16", 8)
        lines = put(
            None, "held0", "near0", "side0", "far0", "held8", "near8", "side8", "far8", "held16",
            "near16", "side16", "far16", "held24", "near24", "side24", "far24",
        )
        self.late = (got["side24"], got["far24"])
        self.early = (got["far8"], got["side24"])
        return lines


def add_call(rows, *terms):
    def kernel(*refs):
        out = refs[-1]
        value = None
        for ref, (_, at) in zip(refs[:-1], terms, strict=True):
            part = ref[at : at + rows, :].astype(F32)
            value = part if value is None else value + part
        out[...] = value.astype(BF)

    return pl.pallas_call(
        kernel,
        in_specs=[VMEM] * len(terms),
        out_shape=pltpu.VMEM((rows, LANES), BF),
        out_specs=VMEM,
        compiler_params=pltpu.CompilerParams(vmem_limit_bytes=4 * 2**20),
        cost_estimate=pl.CostEstimate(flops=10**5, bytes_accessed=2**20, transcendentals=0),
    )(*(in_vmem(array) for array, _ in terms))


def in_hbm(value):
    return pltpu.with_memory_space_constraint(value, pltpu.HBM)


def in_vmem(value):
    return pltpu.with_memory_space_constraint(value, pltpu.VMEM)


class Reduction:
    HOPS = ((2, 2), (1, 4), (4, 1), (8, 8))

    def __init__(self, grid, far_lines, near_lines, half):
        self.grid = grid
        self.near = near_lines
        self.half = half
        self.rows = far_lines.shape[0] // 8
        self.head = far_lines
        self.came = []

    def hop(self, *behind):
        step = len(self.came)
        self.came.append(self.grid.send(self.head, *self.HOPS[step]))
        left = 8 >> (step + 1)
        count = max(left, 1) if step < 3 else 1
        begin = 8 - 2 * left if step < 3 else 7
        terms = [(after(self.near, *behind), begin * self.rows)]
        for level, value in enumerate(self.came):
            terms.append((value, (begin - (8 - (8 >> level))) * self.rows))
        self.head = add_call(count * self.rows, *terms)
        return self.head


def cross_call(low, high, at):
    rows = low.shape[0]
    lines = min(rows, PART)

    def kernel(low, high, out):
        lower = (place() & 16) == 0
        out[:lines, :] = jnp.where(lower, high[at : at + lines, :], low[:lines, :])
        if lines < rows:
            out[lines:, :] = low[lines:, :]

    return pl.pallas_call(
        kernel,
        in_specs=[VMEM] * 2,
        out_shape=pltpu.VMEM((rows, LANES), BF),
        out_specs=VMEM,
        compiler_params=pltpu.CompilerParams(vmem_limit_bytes=2**20),
        cost_estimate=pl.CostEstimate(flops=0, bytes_accessed=2**17, transcendentals=0),
    )(in_vmem(low), in_vmem(high))


def finish_kernel(high, one, one_far, two, two_far, grad, notes):
    lower = (place() & 16) == 0

    for begin, near, far in ((0, one, one_far), (PART, two, two_far)):
        upper = high[begin : begin + PART, :].astype(F32)
        mine = jnp.where(lower, near[:PART, :].astype(F32), upper)
        grad[begin : begin + PART, :] = mine + far[:PART, :].astype(F32)
    tail = one[PART:, :].astype(F32) + one_far[PART:, :].astype(F32)
    row = jnp.where(lower, tail, 0.0)
    value = grad[...]
    square = jnp.sum(jnp.sum(value * value, axis=0, keepdims=True), axis=1, keepdims=True)
    square = square + jnp.sum(jnp.sum(row * row, axis=0, keepdims=True), axis=1, keepdims=True)
    line = lax.broadcasted_iota(jnp.int32, (8, LANES), 0)
    note = jnp.where(line < 4, row[:8], square)
    for device in range(notes.shape[0]):
        notes[device] = note


def finish_call(count, *operands):
    outs = (pltpu.VMEM((BLOCK, LANES), F32), pltpu.VMEM((count, 8, LANES), F32))
    return pl.pallas_call(
        finish_kernel,
        in_specs=[VMEM] * len(operands),
        out_shape=outs,
        out_specs=tuple(VMEM for _ in outs),
        compiler_params=pltpu.CompilerParams(vmem_limit_bytes=8 * 2**20),
        cost_estimate=pl.CostEstimate(flops=10**6, bytes_accessed=2**20, transcendentals=0),
    )(*(in_vmem(value) for value in operands))


def update_kernel(
    grad, notes, first, second, weights, vectors, vector_first, vector_second,
    first_out, second_out, weights_out, vectors_first_out, vectors_second_out, vectors_out,
    bias_out, norm_out, sums,
):
    square = jnp.sum(notes[:, 4, :], axis=0, keepdims=True)
    norm = jnp.sqrt(square)
    factor = jnp.minimum(1.0, clip_norm / (norm + 1e-06))
    norm_out[...] = norm
    for row in range(sums.shape[0]):
        for j in range(D // LANES):
            sums[row : row + 1, j * LANES : (j + 1) * LANES] = notes[row, j : j + 1, :]
    first_out[...], second_out[...], weights_out[...] = adam_update(
        grad[...] * factor, first[...], second[...], weights[...], learn_rate, decay_weight
    )
    clipped = sums[...] * jnp.concatenate([factor] * (D // LANES), axis=1)
    bias_out[...] = clipped[9:10, :]
    vectors_first_out[...], vectors_second_out[...], vectors_out[...] = adam_update(
        clipped, vector_first[...], vector_second[...], vectors[...], vector_rate, 0.0
    )


def update_call(*operands):
    shape = jax.ShapeDtypeStruct
    lines, rows = operands[2].shape, operands[5].shape
    outs = (
        [shape(lines, F32)] * 3
        + [shape(rows, F32)] * 3
        + [shape((1, rows[1]), F32), shape((1, LANES), F32)]
    )
    return pl.pallas_call(
        update_kernel,
        in_specs=[VMEM] * len(operands),
        out_shape=outs,
        out_specs=[VMEM for _ in outs],
        scratch_shapes=[pltpu.VMEM(rows, F32)],
        compiler_params=pltpu.CompilerParams(vmem_limit_bytes=12 * 2**20),
        cost_estimate=pl.CostEstimate(flops=10**7, bytes_accessed=2**22, transcendentals=10**6),
    )(*operands)


def join_kernel(own_out, own_latent, pack, block_out, latent_out, out_wide, latent_wide, sem):
    side = lax.axis_index("blk")
    mine = pl.ds(side * MINE, MINE)
    other = pl.ds((1 - side) * MINE, MINE)
    half = SLOTS // 2
    copies = [
        pltpu.make_async_copy(own_out, block_out.at[mine], sem.at[0]),
        pltpu.make_async_copy(own_latent, latent_out.at[mine], sem.at[1]),
        pltpu.make_async_copy(out_wide, block_out.at[other], sem.at[2]),
        pltpu.make_async_copy(latent_wide, latent_out.at[other], sem.at[3]),
    ]
    copies[0].start()
    copies[1].start()
    for image in range(MINE):
        out_wide[image] = pack[image, :half, :].astype(F32)
        latent_wide[image, :, :D] = pack[image, half : half + KMAX // 2, :].astype(F32)
        last = pack[image, half + KMAX // 2 :, :].astype(F32)
        latent_wide[image, : KMAX // 4, D:] = last[:, : DIN - D]
        latent_wide[image, KMAX // 4 :, D:] = last[:, DIN - D :]
    copies[2].start()
    copies[3].start()
    for copy in copies:
        copy.wait()


def join_call(own_out, own_latent, pack, images):
    shape = jax.ShapeDtypeStruct
    return pl.pallas_call(
        join_kernel,
        in_specs=[VMEM] * 3,
        out_shape=(
            shape((images, *own_out.shape[1:]), F32),
            shape((images, *own_latent.shape[1:]), F32),
        ),
        out_specs=(ANY, ANY),
        scratch_shapes=[
            pltpu.VMEM(own_out.shape, F32),
            pltpu.VMEM(own_latent.shape, F32),
            pltpu.SemaphoreType.DMA((4,)),
        ],
        compiler_params=pltpu.CompilerParams(vmem_limit_bytes=4 * 2**20),
        cost_estimate=pl.CostEstimate(flops=0, bytes_accessed=2**21, transcendentals=0),
    )(own_out, own_latent, pack)


def after(value, *others):
    if not others:
        return value
    return lax.optimization_barrier((value, *others))[0]


def local(
    grid,
    latents,
    restore,
    bucket,
    cotangent,
    flat_weights,
    flat_first,
    flat_second,
    vectors,
    vector_first,
    vector_second,
):
    side = lax.axis_index("blk").astype(jnp.int32)
    by_hand = grid.by_hand

    def trade(value):
        return lax.ppermute(value, "blk", [(0, 1), (1, 0)])

    out_latents, out_cotangent, out_restore = pick_call(latents, cotangent, restore)
    lines = grid.gather(flat_weights.reshape(-1, LANES).astype(BF))
    slot = (jnp.arange(SLOTS, dtype=jnp.int32) + side * (SLOTS // 2)) & (SLOTS - 1)
    position = position_rows(slot)
    my_latents, choice, my_position = prepare_call(
        latents, trade(after(out_latents, *grid.early)), restore,
        trade(after(out_restore, *grid.early)), position,
    )
    far_cotangent = trade(after(out_cotangent, *grid.late))
    (
        probs, shares, joint, normed, start, middle, mixed, embed_w, joint_w, output_w,
    ) = forward_call(bucket, my_latents, choice, my_position, vectors, lines)
    (
        own_out, far_out, hat, scale, back_out, acc_back, head_lines, far_high, near_high, expand_b,
    ) = middle_call(by_hand, bucket, middle, cotangent, far_cotangent, vectors, lines)
    if by_hand:
        high = Reduction(grid, far_high, near_high, 1)
    back_middle, back_mixed, out_lines, rows_b = branch_call(
        hat, scale, back_out, acc_back, mixed, output_w, vectors
    )
    if by_hand:
        back_mixed = after(back_mixed, high.hop(back_mixed))
    far_one, near_one, far_two, near_two, rows_c, own_latent, pack = back_call(
        by_hand, probs, shares, joint, back_mixed, normed, start, back_middle, vectors, joint_w,
        my_latents, choice, embed_w, out_lines, head_lines, rows_b, expand_b, far_out,
    )
    if by_hand:
        mark = high.hop(far_one)
        one = Reduction(grid, after(far_one, mark), near_one, 0)
        two = Reduction(grid, after(far_two, mark), near_two, 0)
        for stream in (one, two, high, one, high, two, one, two, one, two):
            mark = stream.hop(mark)
            if stream is two:
                pack_mark = mark
        across = [
            grid.send(cross_call(stream.head, high.head, at), 16)
            for stream, at in ((one, 0), (two, PART))
        ]
        pack = after(pack, pack_mark)
    block_out, latent_out = join_call(own_out, own_latent, trade(pack), latents.shape[0])

    if by_hand:
        grad, notes = finish_call(
            grid.count, high.head, one.head, across[0], two.head, across[1]
        )
        notes = lax.all_to_all(notes, grid.axes, 0, 0, tiled=True)
        lines = [value.reshape(-1, LANES) for value in (flat_first, flat_second, flat_weights)]
        outs = update_call(grad, notes, *lines, vectors, vector_first, vector_second)
        return (
            block_out,
            latent_out,
            *(value.reshape(-1) for value in outs[:3]),
            *outs[3:6],
            outs[6].reshape(-1),
            outs[7][0, 0],
        )

    low = [
        jnp.concatenate([far, near], axis=0).reshape(16, -1, LANES)[:, :PART]
        for far, near in ((far_one, near_one), (far_two, near_two))
    ]
    flat = jnp.concatenate(
        [jnp.concatenate(low, axis=1).reshape(-1), far_high.reshape(-1), near_high.reshape(-1)]
    )
    shard_grad = lax.psum_scatter(flat, grid.axes, scatter_dimension=0, tiled=True)
    shard_grad = shard_grad.astype(F32).reshape(-1, LANES)
    vector_sum = lax.psum(rows_c[: vectors.shape[0]], grid.axes)
    square_sum = lax.psum(jnp.sum(shard_grad * shard_grad), grid.axes)
    grad_norm = jnp.sqrt(square_sum + jnp.sum(vector_sum * vector_sum))
    factor = jnp.minimum(1.0, clip_norm / (grad_norm + 1e-06))
    new_first, new_second, new_weights = adam_update(
        shard_grad.reshape(-1) * factor,
        flat_first,
        flat_second,
        flat_weights,
        learn_rate,
        decay_weight,
    )
    vector_first_new, vector_second_new, vectors_new = adam_update(
        vector_sum * factor, vector_first, vector_second, vectors, vector_rate, 0.0
    )
    reduce_bias_grad = vector_sum[9] * factor
    return (
        block_out,
        latent_out,
        new_first,
        new_second,
        new_weights,
        vector_first_new,
        vector_second_new,
        vectors_new,
        reduce_bias_grad,
        grad_norm,
    )


def solution(mesh):
    grid = Grid(mesh)
    return jax.shard_map(
        lambda *args: local(grid, *args),
        mesh=mesh,
        in_specs=(
            P("dp", "blk", None),
            P("dp", "blk"),
            P("dp"),
            P("dp", "blk", None),
            P(("dp", "blk")),
            P(("dp", "blk")),
            P(("dp", "blk")),
            P(),
            P(),
            P(),
        ),
        out_specs=(
            P("dp", "blk", None),
            P("dp", "blk", None),
            P(("dp", "blk")),
            P(("dp", "blk")),
            P(("dp", "blk")),
            P(),
            P(),
            P(),
            P(),
            P(),
        ),
        check_vma=False,
    )
```

```python
import math

import jax
import jax.numpy as jnp
from jax import lax
from jax.experimental import pallas as pl
from jax.experimental.pallas import tpu as pltpu
from jax.sharding import PartitionSpec as P

DIN = 768
D = 512
HEADS = 16
HD = 32
FF = 2048
SLOTS = 256
KMAX = 64
STEP = 10
NPARAM = 3538944

first_decay = 0.9
second_decay = 0.95
learn_rate = 0.05
vector_rate = 0.5
decay_weight = 0.05
adam_eps = 1e-08
clip_norm = 1.0

BF = jnp.bfloat16
F32 = jnp.float32

LANES = 128
LINES = NPARAM // LANES
EMBED_AT = 0
JOINT_AT = EMBED_AT + DIN * D // LANES
OUTPUT_AT = JOINT_AT + 3 * D * D // LANES
EXPAND_AT = OUTPUT_AT + D * D // LANES
REDUCE_AT = EXPAND_AT + D * FF // LANES
BLOCK = LINES // 32
HALF = 16 * BLOCK
TAIL = 16
ROWS = 16
PART = BLOCK // 2
PARTS = (PART + TAIL, PART)
TILE = 256
TILES = FF // TILE
GROUP = 4
GROUPS = HEADS // GROUP
MINE = 2
TOKENS = MINE * SLOTS
PICKS = KMAX + 16
PACK = SLOTS // 2 + KMAX // 2 + KMAX // 4
VMEM = pl.BlockSpec(memory_space=pltpu.VMEM)
SMEM = pl.BlockSpec(memory_space=pltpu.SMEM)
ANY = pl.BlockSpec(memory_space=pl.ANY)


def position_rows(slot):
    column = jnp.arange(D // 2, dtype=jnp.int32).astype(F32)[None, :]
    angle = slot.astype(F32)[:, None] * jnp.exp(-math.log(10000.0) * column / (D // 2))
    return jnp.concatenate([jnp.sin(angle), jnp.cos(angle)], axis=1)


def adam_update(grad, first, second, weight, rate, shrink):
    first_new = first_decay * first + (1.0 - first_decay) * grad
    second_new = second_decay * second + (1.0 - second_decay) * grad * grad
    first_hat = first_new / (1.0 - first_decay**STEP)
    second_hat = second_new / (1.0 - second_decay**STEP)
    weight_new = weight - rate * (first_hat / (jnp.sqrt(second_hat) + adam_eps) + shrink * weight)
    return (first_new, second_new, weight_new)


def dot(left, right, over=(1, 0)):
    return lax.dot_general(
        left, right, (((over[0],), (over[1],)), ((), ())), preferred_element_type=F32
    )


def place():
    return lax.axis_index("dp") * lax.axis_size("blk") + lax.axis_index("blk")


def collect_call(lines, pieces, places):
    def kernel(*refs):
        out = refs[-1]
        me = place()
        odd = (me >> 1) & 1
        for (bits, even, uneven), piece in zip(places, refs[-1 - len(pieces) : -1], strict=True):
            block = me ^ bits ^ jnp.where(odd == 0, even, uneven)
            out[pl.ds(pl.multiple_of(block * BLOCK, 16), BLOCK), :] = piece[...]

    given = ([] if lines is None else [lines]) + list(pieces)
    return pl.pallas_call(
        kernel,
        in_specs=[VMEM] * len(given),
        out_shape=pltpu.VMEM((LINES, LANES), BF),
        out_specs=VMEM,
        input_output_aliases={} if lines is None else {0: 0},
        compiler_params=pltpu.CompilerParams(vmem_limit_bytes=2 * 2**20),
        cost_estimate=pl.CostEstimate(flops=0, bytes_accessed=2**20, transcendentals=0),
    )(*(in_vmem(value) for value in given))


def lines_to_matrix(lines, stage, matrix, at, rows, wide, batch):
    size = batch * wide

    def body(index, carry):
        for part in range(2):
            row = pl.multiple_of((2 * index + part) * batch, batch)
            source = pl.multiple_of(at + (2 * index + part) * size, 16)
            stage[part, :size, :] = lines[pl.ds(source, size), :].astype(F32)
            for j in range(wide):
                matrix[pl.ds(row, batch), j * LANES : (j + 1) * LANES] = stage[
                    part, pl.ds(j, batch, stride=wide), :
                ].astype(BF)
        return carry

    lax.fori_loop(0, rows // batch // 2, body, 0)


def norm_parts(value):
    centred = value - jnp.mean(value, axis=-1, keepdims=True)
    scale = lax.rsqrt(jnp.mean(centred * centred, axis=-1, keepdims=True) + 1e-06)
    return centred * scale, scale


def norm_back(grad, hat, scale, gain):
    inner = grad * gain
    return scale * (
        inner
        - jnp.mean(inner, axis=-1, keepdims=True)
        - hat * jnp.mean(inner * hat, axis=-1, keepdims=True)
    )


def total(value):
    return jnp.sum(value.astype(F32), axis=0, keepdims=True)


def slot_column(side):
    local = lax.broadcasted_iota(jnp.int32, (SLOTS, 1), 0)
    return (local + side * (SLOTS // 2)) & (SLOTS - 1)


def image_length(bucket, image):
    kind = bucket[image]
    return jnp.where(
        kind == 0, SLOTS * 100 // 256, jnp.where(kind == 1, SLOTS * 196 // 256, SLOTS)
    )


def select_rows(own, far, side):
    half = SLOTS // 2
    row = lax.broadcasted_iota(jnp.int32, (PICKS, half), 0)
    row = jnp.where(row < KMAX, (row + side * (KMAX // 2)) & (KMAX - 1), row)
    parts = [
        (row == names).astype(F32) for names in (own, far)
    ]
    return jnp.concatenate(parts, axis=1).astype(BF)


def three_parts(value):
    high = value.astype(BF)
    rest = value - high.astype(F32)
    mid = rest.astype(BF)
    return high, mid, (rest - mid.astype(F32)).astype(BF)


def head_mask(head):
    lane = lax.broadcasted_iota(jnp.int32, (1, LANES), 1)
    return (lane // HD) == head


def mask_head(value, head):
    return jnp.where(head_mask(head), value, jnp.zeros_like(value))


def pick_kernel(latents, cotangent, restore, far_latents, far_cotangent, far_restore, sem):
    first = (1 - lax.axis_index("blk")) * MINE
    copies = [
        pltpu.make_async_copy(source.at[pl.ds(first, MINE)], target, sem.at[index])
        for index, (source, target) in enumerate(
            ((latents, far_latents), (cotangent, far_cotangent))
        )
    ]
    for copy in copies:
        copy.start()
    for image in range(MINE):
        far_restore[image : image + 1, :] = restore[pl.ds(first + image, 1), :]
    for copy in copies:
        copy.wait()


def pick_call(latents, cotangent, restore):
    outs = tuple(
        pltpu.VMEM((MINE, *value.shape[1:]), value.dtype) for value in (latents, cotangent, restore)
    )
    return pl.pallas_call(
        pick_kernel,
        in_specs=[ANY, ANY, VMEM],
        out_shape=outs,
        out_specs=tuple(VMEM for _ in outs),
        scratch_shapes=[pltpu.SemaphoreType.DMA((2,))],
        compiler_params=pltpu.CompilerParams(vmem_limit_bytes=2 * 2**20),
        cost_estimate=pl.CostEstimate(flops=0, bytes_accessed=2**19, transcendentals=0),
    )(in_hbm(latents), in_hbm(cotangent), restore)


def prepare_kernel(
    latents, far_latents, restore, far_restore, position, my_latents, choice, my_position,
    near_buffer, sem,
):
    side = lax.axis_index("blk")
    copy = pltpu.make_async_copy(latents.at[pl.ds(side * MINE, MINE)], near_buffer, sem)
    copy.start()
    my_position[...] = position[...]
    for image in range(MINE):
        choice[image] = select_rows(
            restore[pl.ds(side * MINE + image, 1), :], far_restore[image : image + 1, :], side
        )
    copy.wait()
    half = KMAX // 2
    for image in range(MINE):
        at = image * KMAX
        my_latents[at : at + half, :] = near_buffer[image]
        my_latents[at + half : at + KMAX, :] = far_latents[image]


def prepare_call(*operands):
    outs = (
        pltpu.VMEM((MINE * KMAX, DIN), BF),
        pltpu.VMEM((MINE, PICKS, SLOTS), BF),
        pltpu.VMEM((SLOTS, D), F32),
    )
    return pl.pallas_call(
        prepare_kernel,
        in_specs=[ANY, VMEM, VMEM, VMEM, VMEM],
        out_shape=outs,
        out_specs=tuple(VMEM for _ in outs),
        scratch_shapes=[
            pltpu.VMEM((MINE, KMAX // 2, DIN), BF),
            pltpu.SemaphoreType.DMA,
        ],
        compiler_params=pltpu.CompilerParams(vmem_limit_bytes=4 * 2**20),
        cost_estimate=pl.CostEstimate(flops=10**6, bytes_accessed=2**20, transcendentals=0),
    )(in_hbm(operands[0]), *operands[1:])


def forward_kernel(bucket, my_latents, choice, position, vectors, lines, *rest):
    (
        probs,
        shares,
        joint,
        normed,
        start,
        middle,
        mixed,
        embed_w,
        joint_w,
        output_w,
        stage,
        query_t,
        value_t,
        mixed_t,
        scores_even,
        scores_odd,
    ) = rest
    side = lax.axis_index("blk")
    lines_to_matrix(lines, stage, embed_w, EMBED_AT, DIN, 4, 128)
    lines_to_matrix(lines, stage, joint_w, JOINT_AT, D, 12, 64)
    lines_to_matrix(lines, stage, output_w, OUTPUT_AT, D, 4, 128)
    embedded = (dot(my_latents[...], embed_w[...]) + vectors[0:1, :]).astype(BF)
    token = list(three_parts(vectors[1:2, :]))
    for image in range(MINE):
        rows = slice(image * SLOTS, (image + 1) * SLOTS)
        picked = choice[image]
        value = dot(picked[:KMAX], embedded[image * KMAX : (image + 1) * KMAX, :], (0, 0))
        masked = jnp.broadcast_to(picked[KMAX : KMAX + 1], (16, SLOTS))
        table = jnp.concatenate(token + [jnp.zeros((13, D), BF)], axis=0)
        value = value + dot(masked, table, (0, 0)) + position[...]
        start[rows, :] = value
        hat, _ = norm_parts(value)
        normed[rows, :] = (hat * vectors[2:3, :] + vectors[3:4, :]).astype(BF)
    for part, bias in enumerate((4, None, 5)):
        columns = slice(part * D, (part + 1) * D)
        out = dot(normed[...], joint_w[:, columns])
        if bias is not None:
            out = out + vectors[bias : bias + 1, :]
        joint[:, columns] = out.astype(BF)
    query_t[...] = joint[:, :D].T
    value_t[...] = joint[:, 2 * D :].T

    rate = HD**-0.5 * math.log2(math.e)

    def score(unit, target):
        image, group = unit // GROUPS, unit % GROUPS
        rows = pl.ds(pl.multiple_of(image * SLOTS, SLOTS), SLOTS)
        keys = joint[rows, pl.ds(pl.multiple_of(D + group * LANES, LANES), LANES)]
        queries = query_t[pl.ds(pl.multiple_of(group * LANES, LANES), LANES), rows]
        for head in range(GROUP):
            target[head] = dot(mask_head(keys, head), queries)

    def mix(unit, source):
        image, group = unit // GROUPS, unit % GROUPS
        rows = pl.ds(pl.multiple_of(image * SLOTS, SLOTS), SLOTS)
        length = image_length(bucket, side * MINE + image)
        hidden_key = jnp.where(slot_column(side) < length, 0.0, -1e30)
        for head in range(GROUP):
            scores = source[head] + hidden_key
            top = jnp.max(scores, axis=0, keepdims=True)
            raised = jnp.exp2((scores - top) * rate)
            share = 1.0 / jnp.sum(raised, axis=0, keepdims=True)
            low = raised.astype(BF)
            probs[unit * GROUP + head] = low
            shares[pl.ds(unit * GROUP + head, 1), :] = share
            features = pl.ds(pl.multiple_of(group * LANES + head * HD, HD), HD)
            mixed_t[features, rows] = (dot(value_t[features, rows], low) * share).astype(BF)

    score(0, scores_even)

    def pair(index, carry):
        unit = 2 * index
        score(unit + 1, scores_odd)
        mix(unit, scores_even)
        score(jnp.minimum(unit + 2, MINE * GROUPS - 1), scores_even)
        mix(unit + 1, scores_odd)
        return carry

    lax.fori_loop(0, MINE * GROUPS // 2, pair, 0)
    mixed[...] = mixed_t[...].T
    middle[...] = start[...] + dot(mixed[...], output_w[...]) + vectors[6:7, :]


def forward_call(*operands):
    outs = (
        pltpu.VMEM((MINE * HEADS, SLOTS, SLOTS), BF),
        pltpu.VMEM((MINE * HEADS, SLOTS), F32),
        pltpu.VMEM((TOKENS, 3 * D), BF),
        pltpu.VMEM((TOKENS, D), BF),
        pltpu.VMEM((TOKENS, D), F32),
        pltpu.VMEM((TOKENS, D), F32),
        pltpu.VMEM((TOKENS, D), BF),
        pltpu.VMEM((DIN, D), BF),
        pltpu.VMEM((D, 3 * D), BF),
        pltpu.VMEM((D, D), BF),
    )
    return pl.pallas_call(
        forward_kernel,
        in_specs=[SMEM] + [VMEM] * (len(operands) - 1),
        out_shape=outs,
        out_specs=tuple(VMEM for _ in outs),
        scratch_shapes=[
            pltpu.VMEM((2, 768, LANES), F32),
            pltpu.VMEM((D, TOKENS), BF),
            pltpu.VMEM((D, TOKENS), BF),
            pltpu.VMEM((D, TOKENS), BF),
            pltpu.VMEM((GROUP, SLOTS, SLOTS), F32),
            pltpu.VMEM((GROUP, SLOTS, SLOTS), F32),
        ],
        compiler_params=pltpu.CompilerParams(vmem_limit_bytes=10 * 2**20),
        cost_estimate=pl.CostEstimate(
            flops=6 * 10**9, bytes_accessed=16 * 2**20, transcendentals=2 * 10**6
        ),
    )(*operands)


def middle_kernel(
    by_hand, bucket, middle, cotangent, far_cotangent, vectors, lines, *rest
):
    (
        own_out,
        far_out,
        hat,
        scale,
        back_out,
        acc_back,
        head_lines,
        far_lines,
        near_lines,
        expand_out,
        stage,
        expand_w,
        reduce_w,
        normed,
        normed_t,
        acc,
        grads,
    ) = rest
    step = pl.program_id(0)
    side = lax.axis_index("blk")

    @pl.when(step == 0)
    def _():
        value, spread = norm_parts(middle[...])
        hat[...] = value
        scale[...] = jnp.broadcast_to(spread, scale.shape)
        normed[...] = (value * vectors[7:8, :] + vectors[8:9, :]).astype(BF)
        normed_t[...] = normed[...].T
        for image in range(MINE):
            valid = slot_column(side) < image_length(bucket, side * MINE + image)
            half = SLOTS // 2
            for part, (ref, at) in enumerate(
                ((cotangent, side * MINE + image), (far_cotangent, image))
            ):
                first = image * SLOTS + part * half
                back_out[first : first + half, :] = jnp.where(
                    valid[part * half : (part + 1) * half, :],
                    ref[at].astype(F32),
                    0.0,
                ).astype(BF)
        acc[...] = jnp.zeros_like(acc)
        acc_back[...] = jnp.zeros_like(acc_back)
        lines_to_matrix(lines, stage, expand_w, EXPAND_AT, D, 16, 32)
        lines_to_matrix(lines, stage, reduce_w, REDUCE_AT, FF, 4, 128)

    columns = pl.ds(pl.multiple_of(step * TILE, TILE), TILE)
    expand = expand_w[:, columns]
    reduce = reduce_w[columns, :]
    bias = vectors[pl.ds(10 + step // 2, 1), pl.ds(pl.multiple_of((step % 2) * TILE, TILE), TILE)]
    hidden = dot(normed[...], expand) + bias
    density = jnp.exp(hidden * hidden * -0.5) * (1.0 / math.sqrt(2.0 * math.pi))
    below = 0.5 + 0.5 * lax.erf(hidden * math.sqrt(0.5))
    active = (hidden * below).astype(BF)
    back_active = dot(back_out[...], reduce, (1, 1))
    back_hidden = (back_active * (below + hidden * density)).astype(BF)
    acc[...] += dot(active, reduce)
    acc_back[...] += dot(back_hidden, expand, (1, 1))
    grad_reduce = dot(active, back_out[...], (0, 0))
    for j in range(4):
        grads[pl.ds(D * 16 + step * (TILE * 4) + j, TILE, stride=4), :] = grad_reduce[
            :, j * LANES : (j + 1) * LANES
        ]
    grad_expand = dot(normed_t[...], back_hidden)
    for j in range(TILE // LANES):
        grads[pl.ds(step * (TILE // LANES) + j, D, stride=16), :] = grad_expand[
            :, j * LANES : (j + 1) * LANES
        ]
    expand_out[pl.ds(step, 1), :] = total(back_hidden)

    @pl.when(step == TILES - 1)
    def _():
        for image in range(MINE):
            near = slice(image * SLOTS, image * SLOTS + SLOTS // 2)
            far = slice(image * SLOTS + SLOTS // 2, (image + 1) * SLOTS)
            own_out[image] = middle[near, :] + acc[near, :] + vectors[9:10, :]
            far_out[image] = (middle[far, :] + acc[far, :] + vectors[9:10, :]).astype(BF)
        cut = HALF - EXPAND_AT
        head_lines[...] = grads[:cut, :].astype(BF)
        put_blocks(
            by_hand,
            far_lines,
            near_lines,
            lambda q: grads[pl.ds(cut + q * BLOCK, BLOCK), :].astype(BF),
        )


FIRST, SECOND, ALONG_Z = 0, 1, 2
HOP_BITS = ((1, 4), (4, 1), (8, 8))
HIGH_ORDER = (FIRST, ALONG_Z, SECOND)
ONE_ORDER = (FIRST, SECOND, ALONG_Z)
TWO_ORDER = (FIRST, SECOND, ALONG_Z)


def slot_of(index, by_hand, order):
    if not by_hand:
        return index
    me = place()
    rel = index ^ (me & 15)
    other = (rel >> 1) & 1
    odd = ((me >> 1) & 1) ^ other
    along_y, along_x, along_z = rel & 1, (rel >> 2) & 1, rel >> 3
    first = jnp.where(odd == 0, along_y, along_x)
    second = jnp.where(odd == 0, along_x, along_y)
    bits = (first, second, along_z)
    slot = (1 - bits[order[0]]) * 4 + (1 - bits[order[1]]) * 2 + (1 - bits[order[2]])
    return slot + jnp.where(other == 1, 0, 8)


def put_blocks(by_hand, far_lines, near_lines, block_of):
    def body(index, carry):
        slot = slot_of(index, by_hand, HIGH_ORDER)
        value = block_of(index)

        @pl.when(slot < 8)
        def _():
            far_lines[pl.ds(pl.multiple_of(slot * BLOCK, 16), BLOCK), :] = value

        @pl.when(slot >= 8)
        def _():
            near_lines[pl.ds(pl.multiple_of((slot - 8) * BLOCK, 16), BLOCK), :] = value

        return carry

    lax.fori_loop(0, 16, body, 0)


def middle_call(by_hand, *operands):
    outs = (
        pltpu.VMEM((MINE, SLOTS // 2, D), F32),
        pltpu.VMEM((MINE, SLOTS // 2, D), BF),
        pltpu.VMEM((TOKENS, D), F32),
        pltpu.VMEM((TOKENS, LANES), F32),
        pltpu.VMEM((TOKENS, D), BF),
        pltpu.VMEM((TOKENS, D), F32),
        pltpu.VMEM((HALF - EXPAND_AT, LANES), BF),
        pltpu.VMEM((8 * BLOCK, LANES), BF),
        pltpu.VMEM((8 * BLOCK, LANES), BF),
        pltpu.VMEM((TILES, TILE), F32),
    )
    return pl.pallas_call(
        lambda *refs: middle_kernel(by_hand, *refs),
        grid=(TILES,),
        in_specs=[SMEM] + [VMEM] * (len(operands) - 1),
        out_shape=outs,
        out_specs=tuple(VMEM for _ in outs),
        scratch_shapes=[
            pltpu.VMEM((2, 768, LANES), F32),
            pltpu.VMEM((D, FF), BF),
            pltpu.VMEM((FF, D), BF),
            pltpu.VMEM((TOKENS, D), BF),
            pltpu.VMEM((D, TOKENS), BF),
            pltpu.VMEM((TOKENS, D), F32),
            pltpu.VMEM((2 * D * 16, LANES), F32),
        ],
        compiler_params=pltpu.CompilerParams(vmem_limit_bytes=20 * 2**20),
        cost_estimate=pl.CostEstimate(
            flops=8 * 10**9, bytes_accessed=16 * 2**20, transcendentals=2 * 10**6
        ),
    )(*operands)


def branch_kernel(
    hat, scale, back_out, acc_back, mixed, output_w, vectors,
    back_middle, back_mixed, out_lines, rows_out, out_grads,
):
    grad = acc_back[...]
    rows_out[...] = jnp.zeros_like(rows_out)
    rows_out[1:2, :] = total(grad * hat[...])
    rows_out[2:3, :] = total(grad)
    rows_out[3:4, :] = total(back_out[...])
    back = back_out[...].astype(F32) + norm_back(
        grad, hat[...], scale[:, :1], vectors[7:8, :]
    )
    back_middle[...] = back
    branch = back.astype(BF)
    rows_out[0:1, :] = total(branch)
    back_mixed[...] = dot(branch, output_w[...], (1, 1)).astype(BF)
    grad_output = dot(mixed[...], branch, (0, 0))
    for j in range(4):
        out_grads[pl.ds(j, D, stride=4), :] = grad_output[:, j * LANES : (j + 1) * LANES]
    out_lines[...] = out_grads[...].astype(BF)


def branch_call(hat, scale, back_out, acc_back, mixed, output_w, vectors):
    outs = (
        pltpu.VMEM((TOKENS, D), F32),
        pltpu.VMEM((TOKENS, D), BF),
        pltpu.VMEM((EXPAND_AT - OUTPUT_AT, LANES), BF),
        pltpu.VMEM((8, D), F32),
    )
    return pl.pallas_call(
        branch_kernel,
        in_specs=[VMEM] * 7,
        out_shape=outs,
        out_specs=tuple(VMEM for _ in outs),
        scratch_shapes=[pltpu.VMEM((D * 4, LANES), F32)],
        compiler_params=pltpu.CompilerParams(vmem_limit_bytes=16 * 2**20),
        cost_estimate=pl.CostEstimate(
            flops=2 * 10**9, bytes_accessed=4 * 2**20, transcendentals=0
        ),
    )(hat, scale, back_out, acc_back, mixed, output_w, vectors)


def attention_back_kernel(
    probs, shares, joint, back_mixed, normed, start, back_middle, vectors, joint_w,
    joint_lines, back_start, rows_out,
    joint_back, key_t, back_t, shared_t, shared, query_back_t, even, odd, grads,
):
    key_t[...] = joint[:, D : 2 * D].T
    back_t[...] = back_mixed[...].T
    for image in range(MINE):
        columns = slice(image * SLOTS, (image + 1) * SLOTS)
        for head in range(HEADS):
            features = slice(head * HD, (head + 1) * HD)
            at = image * HEADS + head
            shared_t[features, columns] = (
                back_t[features, columns].astype(F32) * shares[at : at + 1, :]
            ).astype(BF)
    shared[...] = shared_t[...].T

    def pull_back(unit, target):
        image, group = unit // GROUPS, unit % GROUPS
        rows = pl.ds(pl.multiple_of(image * SLOTS, SLOTS), SLOTS)
        values = joint[rows, pl.ds(pl.multiple_of(2 * D + group * LANES, LANES), LANES)]
        back_lanes = back_t[pl.ds(pl.multiple_of(group * LANES, LANES), LANES), rows]
        for head in range(GROUP):
            target[head] = dot(mask_head(values, head), back_lanes)

    def spread(unit, source):
        image, group = unit // GROUPS, unit % GROUPS
        rows = pl.ds(pl.multiple_of(image * SLOTS, SLOTS), SLOTS)
        lanes = pl.ds(pl.multiple_of(group * LANES, LANES), LANES)
        queries = joint[rows, lanes]
        back = shared[rows, lanes]
        key_back = jnp.zeros((SLOTS, LANES), F32)
        value_back = jnp.zeros((SLOTS, LANES), F32)
        for head in range(GROUP):
            low = probs[unit * GROUP + head]
            share = shares[pl.ds(unit * GROUP + head, 1), :]
            wide = low.astype(F32)
            back_probs = source[head]
            pull = jnp.sum(wide * back_probs, axis=0, keepdims=True) * share
            score_back = (wide * ((back_probs - pull) * (share * HD**-0.5))).astype(BF)
            value_back = value_back + dot(low, mask_head(back, head))
            key_back = key_back + dot(score_back, mask_head(queries, head))
            features = pl.ds(pl.multiple_of(group * LANES + head * HD, HD), HD)
            query_back_t[features, rows] = dot(key_t[features, rows], score_back).astype(BF)
        joint_back[rows, pl.ds(pl.multiple_of(D + group * LANES, LANES), LANES)] = (
            key_back.astype(BF)
        )
        joint_back[rows, pl.ds(pl.multiple_of(2 * D + group * LANES, LANES), LANES)] = (
            value_back.astype(BF)
        )

    pull_back(0, even)

    def pair(index, carry):
        unit = 2 * index
        pull_back(unit + 1, odd)
        spread(unit, even)
        pull_back(jnp.minimum(unit + 2, MINE * GROUPS - 1), even)
        spread(unit + 1, odd)
        return carry

    lax.fori_loop(0, MINE * GROUPS // 2, pair, 0)
    joint_back[:, :D] = query_back_t[...].T
    rows_out[...] = jnp.zeros_like(rows_out)
    rows_out[2:3, :] = total(joint_back[:, :D])
    rows_out[3:4, :] = total(joint_back[:, 2 * D :])
    normed_t = normed[...].T
    for part in range(3):
        grad_joint = dot(normed_t, joint_back[:, part * D : (part + 1) * D])
        for j in range(4):
            grads[pl.ds(part * 4 + j, D, stride=12), :] = grad_joint[
                :, j * LANES : (j + 1) * LANES
            ]
    grad = dot(joint_back[...], joint_w[...], (1, 1))
    hat, scale = norm_parts(start[...])
    rows_out[0:1, :] = total(grad * hat)
    rows_out[1:2, :] = total(grad)
    back_start[...] = back_middle[...] + norm_back(grad, hat, scale, vectors[2:3, :])
    joint_lines[...] = grads[...].astype(BF)


def input_back_kernel(
    by_hand,
    back_start,
    my_latents,
    choices,
    embed_w,
    joint_lines,
    rows_joint,
    out_lines,
    head_lines,
    rows_in,
    expand_in,
    far_out,
    far_first,
    near_first,
    far_second,
    near_second,
    rows_out,
    own_latent,
    pack,
    grads,
    tails,
):
    rows_out[...] = jnp.zeros_like(rows_out)
    rows_out[2:6, :] = rows_joint[0:4, :]
    low_start = back_start[...].astype(BF)
    low_rest = (back_start[...] - low_start.astype(F32)).astype(BF)
    picked = []
    token_back = jnp.zeros((1, D), F32)
    for image in range(MINE):
        part = slice(image * SLOTS, (image + 1) * SLOTS)
        choice = choices[image]
        chosen = dot(choice, low_start[part, :])
        picked.append(chosen[:KMAX, :].astype(BF))
        token_back = token_back + chosen[KMAX : KMAX + 1, :]
        token_back = token_back + dot(choice[KMAX:, :], low_rest[part, :])[:1, :]
    rows_out[1:2, :] = token_back
    embedded_back = jnp.concatenate(picked, axis=0)
    rows_out[0:1, :] = total(embedded_back)
    grad_embed = dot(my_latents[...], embedded_back, (0, 0))
    for j in range(4):
        grads[pl.ds(EMBED_AT + j, DIN, stride=4), :] = grad_embed[:, j * LANES : (j + 1) * LANES]
    latent_back = dot(embedded_back, embed_w[...], (1, 1))
    for image in range(MINE):
        at = image * KMAX
        own_latent[image] = latent_back[at : at + KMAX // 2, :]
        far = latent_back[at + KMAX // 2 : at + KMAX, :].astype(BF)
        pack[image, : SLOTS // 2, :] = far_out[image]
        pack[image, SLOTS // 2 : SLOTS // 2 + KMAX // 2, :] = far[:, :D]
        pack[image, SLOTS // 2 + KMAX // 2 :, : DIN - D] = far[: KMAX // 4, D:]
        pack[image, SLOTS // 2 + KMAX // 2 :, DIN - D :] = far[KMAX // 4 :, D:]
    rows_out[6:10, :] = rows_in[0:4, :]
    for j in range(4):
        rows_out[10 + j : 11 + j, :TILE] = expand_in[2 * j : 2 * j + 1, :]
        rows_out[10 + j : 11 + j, TILE:] = expand_in[2 * j + 1 : 2 * j + 2, :]
    tails[...] = jnp.zeros_like(tails)
    for row in range(ROWS):
        for j in range(D // LANES):
            tails[row * TAIL + j : row * TAIL + j + 1, :] = rows_out[
                row : row + 1, j * LANES : (j + 1) * LANES
            ]

    def store(index, value):
        slot = slot_of(index, by_hand, ONE_ORDER)
        late = slot_of(index, by_hand, TWO_ORDER)
        tail = tails[pl.ds(pl.multiple_of(index * TAIL, TAIL), TAIL), :].astype(BF)

        def put(first, second, at, late_at):
            row = pl.multiple_of(at * PARTS[0], 16)
            first[pl.ds(row, PART), :] = value[:PART]
            first[pl.ds(row + PART, TAIL), :] = tail
            second[pl.ds(pl.multiple_of(late_at * PART, 16), PART), :] = value[PART:]

        @pl.when(slot < 8)
        def _():
            put(far_first, far_second, slot, late)

        @pl.when(slot >= 8)
        def _():
            put(near_first, near_second, slot - 8, late - 8)

    ranges = (
        (EMBED_AT, JOINT_AT, lambda low, high: grads[low:high, :].astype(BF)),
        (JOINT_AT, OUTPUT_AT, lambda low, high: joint_lines[low:high, :]),
        (OUTPUT_AT, EXPAND_AT, lambda low, high: out_lines[low:high, :]),
        (EXPAND_AT, HALF, lambda low, high: head_lines[low:high, :]),
    )
    for index in range(16):
        low, high = index * BLOCK, (index + 1) * BLOCK
        parts = [
            take(max(low, begin) - begin, min(high, end) - begin)
            for begin, end, take in ranges
            if max(low, begin) < min(high, end)
        ]
        store(index, jnp.concatenate(parts, axis=0) if len(parts) > 1 else parts[0])


def back_kernel(by_hand, *refs):
    attention, (my_latents, choices, embed_w, out_lines, head_lines, rows_in, expand_in, far_out) = (
        refs[:9], refs[9:17],
    )
    outs, scratch = refs[17:24], refs[24:]
    joint_lines, back_start, rows_joint = scratch[:3]
    attention_back_kernel(*attention, joint_lines, back_start, rows_joint, *scratch[3:12])
    input_back_kernel(
        by_hand, back_start, my_latents, choices, embed_w, joint_lines, rows_joint, out_lines,
        head_lines, rows_in, expand_in, far_out, *outs, *scratch[12:],
    )


def back_call(by_hand, *operands):
    shape = jax.ShapeDtypeStruct
    outs = (
        pltpu.VMEM((8 * PARTS[0], LANES), BF),
        pltpu.VMEM((8 * PARTS[0], LANES), BF),
        pltpu.VMEM((8 * PARTS[1], LANES), BF),
        pltpu.VMEM((8 * PARTS[1], LANES), BF),
        shape((ROWS, D), F32),
        pltpu.VMEM((MINE, KMAX // 2, DIN), F32),
        pltpu.VMEM((MINE, PACK, D), BF),
    )
    return pl.pallas_call(
        lambda *refs: back_kernel(by_hand, *refs),
        in_specs=[VMEM] * len(operands),
        out_shape=outs,
        out_specs=tuple(VMEM for _ in outs),
        scratch_shapes=[
            pltpu.VMEM((OUTPUT_AT - JOINT_AT, LANES), BF),
            pltpu.VMEM((TOKENS, D), F32),
            pltpu.VMEM((8, D), F32),
            pltpu.VMEM((TOKENS, 3 * D), BF),
            pltpu.VMEM((D, TOKENS), BF),
            pltpu.VMEM((D, TOKENS), BF),
            pltpu.VMEM((D, TOKENS), BF),
            pltpu.VMEM((TOKENS, D), BF),
            pltpu.VMEM((D, TOKENS), BF),
            pltpu.VMEM((GROUP, SLOTS, SLOTS), F32),
            pltpu.VMEM((GROUP, SLOTS, SLOTS), F32),
            pltpu.VMEM((OUTPUT_AT - JOINT_AT, LANES), F32),
            pltpu.VMEM((JOINT_AT, LANES), F32),
            pltpu.VMEM((ROWS * TAIL, LANES), F32),
        ],
        compiler_params=pltpu.CompilerParams(vmem_limit_bytes=24 * 2**20),
        cost_estimate=pl.CostEstimate(
            flops=4 * 10**9, bytes_accessed=8 * 2**20, transcendentals=0
        ),
    )(*operands)


class Grid:
    def __init__(self, mesh):
        self.axes = ("dp", "blk")
        self.count = mesh.shape["dp"] * mesh.shape["blk"]
        self.early = self.late = ()
        self.by_hand = self.count == 32 and mesh.shape["blk"] == 2

    def send(self, value, bits, other=None):
        other = bits if other is None else other
        pairs = [(i, i ^ (other if i & 2 else bits)) for i in range(self.count)]
        return lax.ppermute(value, self.axes, pairs)

    def gather(self, block):
        if not self.by_hand:
            whole = lax.all_gather(block, self.axes, axis=0, tiled=True)
            return whole.reshape(LINES, LANES)
        got = {"held0": block}

        def send(name, value, bits, other=None, behind=()):
            got[name] = self.send(after(got[value], *(got[b] for b in behind)), bits, other)

        def put(lines, *names):
            pieces, places = [], []
            for name in names:
                even, uneven = {"held": (0, 0), "near": (4, 1), "side": (1, 4), "far": (5, 5)}[
                    name.rstrip("0123456789")
                ]
                bits = int(name.lstrip("abcdefghijklmnopqrstuvwxyz"))
                pieces += [got[name], self.send(got[name], 2)]
                places += [(bits, even, uneven), (bits ^ 2, uneven, even)]
            return collect_call(lines, pieces, places)

        send("held16", "held0", 16)
        send("near0", "held0", 4, 1)
        send("held8", "held0", 8)
        send("side0", "held0", 1, 4)
        send("far0", "near0", 1, 4)
        send("near16", "held16", 4, 1)
        send("side16", "held16", 1, 4)
        send("held24", "held16", 8)
        send("near8", "held8", 4, 1)
        send("side8", "held8", 1, 4)
        send("far8", "far0", 8)
        send("far16", "near16", 1, 4, behind=("far0",))
        send("near24", "held24", 4, 1)
        send("side24", "held24", 1, 4, behind=("near16",))
        send("far24", "far16", 8)
        lines = put(
            None, "held0", "near0", "side0", "far0", "held8", "near8", "side8", "far8", "held16",
            "near16", "side16", "far16", "held24", "near24", "side24", "far24",
        )
        self.late = (got["side24"], got["far24"])
        self.early = (got["far8"], got["side24"])
        return lines


def add_call(rows, *terms):
    def kernel(*refs):
        out = refs[-1]
        value = None
        for ref, (_, at) in zip(refs[:-1], terms, strict=True):
            part = ref[at : at + rows, :].astype(F32)
            value = part if value is None else value + part
        out[...] = value.astype(BF)

    return pl.pallas_call(
        kernel,
        in_specs=[VMEM] * len(terms),
        out_shape=pltpu.VMEM((rows, LANES), BF),
        out_specs=VMEM,
        compiler_params=pltpu.CompilerParams(vmem_limit_bytes=4 * 2**20),
        cost_estimate=pl.CostEstimate(flops=10**5, bytes_accessed=2**20, transcendentals=0),
    )(*(in_vmem(array) for array, _ in terms))


def in_hbm(value):
    return pltpu.with_memory_space_constraint(value, pltpu.HBM)


def in_vmem(value):
    return pltpu.with_memory_space_constraint(value, pltpu.VMEM)


class Reduction:
    def __init__(self, grid, far_lines, near_lines, order):
        self.grid = grid
        self.near = near_lines
        self.hops = ((2, 2), *(HOP_BITS[hop] for hop in order))
        self.rows = far_lines.shape[0] // 8
        self.head = far_lines
        self.came = []

    def hop(self, *behind):
        step = len(self.came)
        self.came.append(self.grid.send(self.head, *self.hops[step]))
        left = 8 >> (step + 1)
        count = max(left, 1) if step < 3 else 1
        begin = 8 - 2 * left if step < 3 else 7
        terms = [(after(self.near, *behind), begin * self.rows)]
        for level, value in enumerate(self.came):
            terms.append((value, (begin - (8 - (8 >> level))) * self.rows))
        self.head = add_call(count * self.rows, *terms)
        return self.head


def cross_call(low, high, at):
    rows = low.shape[0]
    lines = min(rows, PART)

    def kernel(low, high, out):
        lower = (place() & 16) == 0
        out[:lines, :] = jnp.where(lower, high[at : at + lines, :], low[:lines, :])
        if lines < rows:
            out[lines:, :] = low[lines:, :]

    return pl.pallas_call(
        kernel,
        in_specs=[VMEM] * 2,
        out_shape=pltpu.VMEM((rows, LANES), BF),
        out_specs=VMEM,
        compiler_params=pltpu.CompilerParams(vmem_limit_bytes=2**20),
        cost_estimate=pl.CostEstimate(flops=0, bytes_accessed=2**17, transcendentals=0),
    )(in_vmem(low), in_vmem(high))


def finish_kernel(high, one, one_far, two, two_far, grad, notes):
    lower = (place() & 16) == 0

    for begin, near, far in ((0, one, one_far), (PART, two, two_far)):
        upper = high[begin : begin + PART, :].astype(F32)
        mine = jnp.where(lower, near[:PART, :].astype(F32), upper)
        grad[begin : begin + PART, :] = mine + far[:PART, :].astype(F32)
    tail = one[PART:, :].astype(F32) + one_far[PART:, :].astype(F32)
    row = jnp.where(lower, tail, 0.0)
    value = grad[...]
    square = jnp.sum(jnp.sum(value * value, axis=0, keepdims=True), axis=1, keepdims=True)
    square = square + jnp.sum(jnp.sum(row * row, axis=0, keepdims=True), axis=1, keepdims=True)
    line = lax.broadcasted_iota(jnp.int32, (8, LANES), 0)
    note = jnp.where(line < 4, row[:8], square)
    for device in range(notes.shape[0]):
        notes[device] = note


def finish_call(count, *operands):
    outs = (pltpu.VMEM((BLOCK, LANES), F32), pltpu.VMEM((count, 8, LANES), F32))
    return pl.pallas_call(
        finish_kernel,
        in_specs=[VMEM] * len(operands),
        out_shape=outs,
        out_specs=tuple(VMEM for _ in outs),
        compiler_params=pltpu.CompilerParams(vmem_limit_bytes=8 * 2**20),
        cost_estimate=pl.CostEstimate(flops=10**6, bytes_accessed=2**20, transcendentals=0),
    )(*(in_vmem(value) for value in operands))


def update_kernel(
    grad, notes, first, second, weights, vectors, vector_first, vector_second,
    first_out, second_out, weights_out, vectors_first_out, vectors_second_out, vectors_out,
    bias_out, norm_out, sums,
):
    square = jnp.sum(notes[:, 4, :], axis=0, keepdims=True)
    norm = jnp.sqrt(square)
    factor = jnp.minimum(1.0, clip_norm / (norm + 1e-06))
    norm_out[...] = norm
    for row in range(sums.shape[0]):
        for j in range(D // LANES):
            sums[row : row + 1, j * LANES : (j + 1) * LANES] = notes[row, j : j + 1, :]
    first_out[...], second_out[...], weights_out[...] = adam_update(
        grad[...] * factor, first[...], second[...], weights[...], learn_rate, decay_weight
    )
    clipped = sums[...] * jnp.concatenate([factor] * (D // LANES), axis=1)
    bias_out[...] = clipped[9:10, :]
    vectors_first_out[...], vectors_second_out[...], vectors_out[...] = adam_update(
        clipped, vector_first[...], vector_second[...], vectors[...], vector_rate, 0.0
    )


def update_call(*operands):
    shape = jax.ShapeDtypeStruct
    lines, rows = operands[2].shape, operands[5].shape
    outs = (
        [shape(lines, F32)] * 3
        + [shape(rows, F32)] * 3
        + [shape((1, rows[1]), F32), shape((1, LANES), F32)]
    )
    return pl.pallas_call(
        update_kernel,
        in_specs=[VMEM] * len(operands),
        out_shape=outs,
        out_specs=[VMEM for _ in outs],
        scratch_shapes=[pltpu.VMEM(rows, F32)],
        compiler_params=pltpu.CompilerParams(vmem_limit_bytes=12 * 2**20),
        cost_estimate=pl.CostEstimate(flops=10**7, bytes_accessed=2**22, transcendentals=10**6),
    )(*operands)


def join_kernel(own_out, own_latent, pack, block_out, latent_out, out_wide, latent_wide, sem):
    side = lax.axis_index("blk")
    mine = pl.ds(side * MINE, MINE)
    other = pl.ds((1 - side) * MINE, MINE)
    half = SLOTS // 2
    copies = [
        pltpu.make_async_copy(own_out, block_out.at[mine], sem.at[0]),
        pltpu.make_async_copy(own_latent, latent_out.at[mine], sem.at[1]),
        pltpu.make_async_copy(out_wide, block_out.at[other], sem.at[2]),
        pltpu.make_async_copy(latent_wide, latent_out.at[other], sem.at[3]),
    ]
    copies[0].start()
    copies[1].start()
    for image in range(MINE):
        out_wide[image] = pack[image, :half, :].astype(F32)
        latent_wide[image, :, :D] = pack[image, half : half + KMAX // 2, :].astype(F32)
        last = pack[image, half + KMAX // 2 :, :].astype(F32)
        latent_wide[image, : KMAX // 4, D:] = last[:, : DIN - D]
        latent_wide[image, KMAX // 4 :, D:] = last[:, DIN - D :]
    copies[2].start()
    copies[3].start()
    for copy in copies:
        copy.wait()


def join_call(own_out, own_latent, pack, images):
    shape = jax.ShapeDtypeStruct
    return pl.pallas_call(
        join_kernel,
        in_specs=[VMEM] * 3,
        out_shape=(
            shape((images, *own_out.shape[1:]), F32),
            shape((images, *own_latent.shape[1:]), F32),
        ),
        out_specs=(ANY, ANY),
        scratch_shapes=[
            pltpu.VMEM(own_out.shape, F32),
            pltpu.VMEM(own_latent.shape, F32),
            pltpu.SemaphoreType.DMA((4,)),
        ],
        compiler_params=pltpu.CompilerParams(vmem_limit_bytes=4 * 2**20),
        cost_estimate=pl.CostEstimate(flops=0, bytes_accessed=2**21, transcendentals=0),
    )(own_out, own_latent, pack)


def after(value, *others):
    if not others:
        return value
    return lax.optimization_barrier((value, *others))[0]


def local(
    grid,
    latents,
    restore,
    bucket,
    cotangent,
    flat_weights,
    flat_first,
    flat_second,
    vectors,
    vector_first,
    vector_second,
):
    side = lax.axis_index("blk").astype(jnp.int32)
    by_hand = grid.by_hand

    def trade(value):
        return lax.ppermute(value, "blk", [(0, 1), (1, 0)])

    out_latents, out_cotangent, out_restore = pick_call(latents, cotangent, restore)
    lines = grid.gather(flat_weights.reshape(-1, LANES).astype(BF))
    slot = (jnp.arange(SLOTS, dtype=jnp.int32) + side * (SLOTS // 2)) & (SLOTS - 1)
    position = position_rows(slot)
    my_latents, choice, my_position = prepare_call(
        latents, trade(after(out_latents, *grid.early)), restore,
        trade(after(out_restore, *grid.early)), position,
    )
    far_cotangent = trade(after(out_cotangent, *grid.late))
    (
        probs, shares, joint, normed, start, middle, mixed, embed_w, joint_w, output_w,
    ) = forward_call(bucket, my_latents, choice, my_position, vectors, lines)
    (
        own_out, far_out, hat, scale, back_out, acc_back, head_lines, far_high, near_high, expand_b,
    ) = middle_call(by_hand, bucket, middle, cotangent, far_cotangent, vectors, lines)
    if by_hand:
        high = Reduction(grid, far_high, near_high, HIGH_ORDER)
    back_middle, back_mixed, out_lines, rows_b = branch_call(
        hat, scale, back_out, acc_back, mixed, output_w, vectors
    )
    if by_hand:
        back_mixed = after(back_mixed, high.hop(back_mixed))
    far_one, near_one, far_two, near_two, rows_c, own_latent, pack = back_call(
        by_hand, probs, shares, joint, back_mixed, normed, start, back_middle, vectors, joint_w,
        my_latents, choice, embed_w, out_lines, head_lines, rows_b, expand_b, far_out,
    )
    if by_hand:
        mark = high.hop(far_one)
        one = Reduction(grid, after(far_one, mark), near_one, ONE_ORDER)
        two = Reduction(grid, after(far_two, mark), near_two, TWO_ORDER)
        for stream in (one, two, one, high, two, one, high, two, one, two):
            mark = stream.hop(mark)
            if stream is two:
                pack_mark = mark
        across = [
            grid.send(cross_call(stream.head, high.head, at), 16)
            for stream, at in ((one, 0), (two, PART))
        ]
        pack = after(pack, pack_mark)
    block_out, latent_out = join_call(own_out, own_latent, trade(pack), latents.shape[0])

    if by_hand:
        grad, notes = finish_call(
            grid.count, high.head, one.head, across[0], two.head, across[1]
        )
        notes = lax.all_to_all(notes, grid.axes, 0, 0, tiled=True)
        lines = [value.reshape(-1, LANES) for value in (flat_first, flat_second, flat_weights)]
        outs = update_call(grad, notes, *lines, vectors, vector_first, vector_second)
        return (
            block_out,
            latent_out,
            *(value.reshape(-1) for value in outs[:3]),
            *outs[3:6],
            outs[6].reshape(-1),
            outs[7][0, 0],
        )

    low = [
        jnp.concatenate([far, near], axis=0).reshape(16, -1, LANES)[:, :PART]
        for far, near in ((far_one, near_one), (far_two, near_two))
    ]
    flat = jnp.concatenate(
        [jnp.concatenate(low, axis=1).reshape(-1), far_high.reshape(-1), near_high.reshape(-1)]
    )
    shard_grad = lax.psum_scatter(flat, grid.axes, scatter_dimension=0, tiled=True)
    shard_grad = shard_grad.astype(F32).reshape(-1, LANES)
    vector_sum = lax.psum(rows_c[: vectors.shape[0]], grid.axes)
    square_sum = lax.psum(jnp.sum(shard_grad * shard_grad), grid.axes)
    grad_norm = jnp.sqrt(square_sum + jnp.sum(vector_sum * vector_sum))
    factor = jnp.minimum(1.0, clip_norm / (grad_norm + 1e-06))
    new_first, new_second, new_weights = adam_update(
        shard_grad.reshape(-1) * factor,
        flat_first,
        flat_second,
        flat_weights,
        learn_rate,
        decay_weight,
    )
    vector_first_new, vector_second_new, vectors_new = adam_update(
        vector_sum * factor, vector_first, vector_second, vectors, vector_rate, 0.0
    )
    reduce_bias_grad = vector_sum[9] * factor
    return (
        block_out,
        latent_out,
        new_first,
        new_second,
        new_weights,
        vector_first_new,
        vector_second_new,
        vectors_new,
        reduce_bias_grad,
        grad_norm,
    )


def solution(mesh):
    grid = Grid(mesh)
    return jax.shard_map(
        lambda *args: local(grid, *args),
        mesh=mesh,
        in_specs=(
            P("dp", "blk", None),
            P("dp", "blk"),
            P("dp"),
            P("dp", "blk", None),
            P(("dp", "blk")),
            P(("dp", "blk")),
            P(("dp", "blk")),
            P(),
            P(),
            P(),
        ),
        out_specs=(
            P("dp", "blk", None),
            P("dp", "blk", None),
            P(("dp", "blk")),
            P(("dp", "blk")),
            P(("dp", "blk")),
            P(),
            P(),
            P(),
            P(),
            P(),
        ),
        check_vma=False,
    )
```

```python
import math

import jax
import jax.numpy as jnp
from jax import lax
from jax.experimental import pallas as pl
from jax.experimental.pallas import tpu as pltpu
from jax.sharding import PartitionSpec as P

DIN = 768
D = 512
HEADS = 16
HD = 32
FF = 2048
SLOTS = 256
KMAX = 64
STEP = 10
NPARAM = 3538944

first_decay = 0.9
second_decay = 0.95
learn_rate = 0.05
vector_rate = 0.5
decay_weight = 0.05
adam_eps = 1e-08
clip_norm = 1.0

BF = jnp.bfloat16
F32 = jnp.float32

LANES = 128
LINES = NPARAM // LANES
EMBED_AT = 0
JOINT_AT = EMBED_AT + DIN * D // LANES
OUTPUT_AT = JOINT_AT + 3 * D * D // LANES
EXPAND_AT = OUTPUT_AT + D * D // LANES
REDUCE_AT = EXPAND_AT + D * FF // LANES
BLOCK = LINES // 32
HALF = 16 * BLOCK
TAIL = 16
ROWS = 16
PART = BLOCK // 2
PARTS = (PART + TAIL, PART)
TILE = 512
TILES = FF // TILE
GROUP = 4
GROUPS = HEADS // GROUP
MINE = 2
TOKENS = MINE * SLOTS
PICKS = KMAX + 16
PACK = SLOTS // 2 + KMAX // 2 + KMAX // 4
VMEM = pl.BlockSpec(memory_space=pltpu.VMEM)
SMEM = pl.BlockSpec(memory_space=pltpu.SMEM)
ANY = pl.BlockSpec(memory_space=pl.ANY)


def position_rows(slot):
    column = jnp.arange(D // 2, dtype=jnp.int32).astype(F32)[None, :]
    angle = slot.astype(F32)[:, None] * jnp.exp(-math.log(10000.0) * column / (D // 2))
    return jnp.concatenate([jnp.sin(angle), jnp.cos(angle)], axis=1)


def adam_update(grad, first, second, weight, rate, shrink):
    first_new = first_decay * first + (1.0 - first_decay) * grad
    second_new = second_decay * second + (1.0 - second_decay) * grad * grad
    first_hat = first_new / (1.0 - first_decay**STEP)
    second_hat = second_new / (1.0 - second_decay**STEP)
    weight_new = weight - rate * (first_hat / (jnp.sqrt(second_hat) + adam_eps) + shrink * weight)
    return (first_new, second_new, weight_new)


def dot(left, right, over=(1, 0)):
    return lax.dot_general(
        left, right, (((over[0],), (over[1],)), ((), ())), preferred_element_type=F32
    )


def place():
    return lax.axis_index("dp") * lax.axis_size("blk") + lax.axis_index("blk")


def collect_call(lines, pieces, places):
    def kernel(*refs):
        out = refs[-1]
        me = place()
        odd = (me >> 1) & 1
        for (bits, even, uneven), piece in zip(places, refs[-1 - len(pieces) : -1], strict=True):
            block = me ^ bits ^ jnp.where(odd == 0, even, uneven)
            out[pl.ds(pl.multiple_of(block * BLOCK, 16), BLOCK), :] = piece[...]

    given = ([] if lines is None else [lines]) + list(pieces)
    return pl.pallas_call(
        kernel,
        in_specs=[VMEM] * len(given),
        out_shape=pltpu.VMEM((LINES, LANES), BF),
        out_specs=VMEM,
        input_output_aliases={} if lines is None else {0: 0},
        compiler_params=pltpu.CompilerParams(vmem_limit_bytes=2 * 2**20),
        cost_estimate=pl.CostEstimate(flops=0, bytes_accessed=2**20, transcendentals=0),
    )(*(in_vmem(value) for value in given))


def lines_to_matrix(lines, stage, matrix, at, rows, wide, batch):
    size = batch * wide

    def body(index, carry):
        for part in range(2):
            row = pl.multiple_of((2 * index + part) * batch, batch)
            source = pl.multiple_of(at + (2 * index + part) * size, 16)
            stage[part, :size, :] = lines[pl.ds(source, size), :].astype(F32)
            for j in range(wide):
                matrix[pl.ds(row, batch), j * LANES : (j + 1) * LANES] = stage[
                    part, pl.ds(j, batch, stride=wide), :
                ].astype(BF)
        return carry

    lax.fori_loop(0, rows // batch // 2, body, 0)


def norm_parts(value):
    centred = value - jnp.mean(value, axis=-1, keepdims=True)
    scale = lax.rsqrt(jnp.mean(centred * centred, axis=-1, keepdims=True) + 1e-06)
    return centred * scale, scale


def norm_back(grad, hat, scale, gain):
    inner = grad * gain
    return scale * (
        inner
        - jnp.mean(inner, axis=-1, keepdims=True)
        - hat * jnp.mean(inner * hat, axis=-1, keepdims=True)
    )


def total(value):
    return jnp.sum(value.astype(F32), axis=0, keepdims=True)


def slot_column(side):
    local = lax.broadcasted_iota(jnp.int32, (SLOTS, 1), 0)
    return (local + side * (SLOTS // 2)) & (SLOTS - 1)


def image_length(bucket, image):
    kind = bucket[image]
    return jnp.where(
        kind == 0, SLOTS * 100 // 256, jnp.where(kind == 1, SLOTS * 196 // 256, SLOTS)
    )


def select_rows(own, far, side):
    half = SLOTS // 2
    row = lax.broadcasted_iota(jnp.int32, (PICKS, half), 0)
    row = jnp.where(row < KMAX, (row + side * (KMAX // 2)) & (KMAX - 1), row)
    parts = [
        (row == names).astype(F32) for names in (own, far)
    ]
    return jnp.concatenate(parts, axis=1).astype(BF)


def three_parts(value):
    high = value.astype(BF)
    rest = value - high.astype(F32)
    mid = rest.astype(BF)
    return high, mid, (rest - mid.astype(F32)).astype(BF)


def head_mask(head):
    lane = lax.broadcasted_iota(jnp.int32, (1, LANES), 1)
    return (lane // HD) == head


def mask_head(value, head):
    return jnp.where(head_mask(head), value, jnp.zeros_like(value))


def pick_kernel(latents, cotangent, restore, far_latents, far_cotangent, far_restore, sem):
    first = (1 - lax.axis_index("blk")) * MINE
    copies = [
        pltpu.make_async_copy(source.at[pl.ds(first, MINE)], target, sem.at[index])
        for index, (source, target) in enumerate(
            ((latents, far_latents), (cotangent, far_cotangent))
        )
    ]
    for copy in copies:
        copy.start()
    for image in range(MINE):
        far_restore[image : image + 1, :] = restore[pl.ds(first + image, 1), :]
    for copy in copies:
        copy.wait()


def pick_call(latents, cotangent, restore):
    outs = tuple(
        pltpu.VMEM((MINE, *value.shape[1:]), value.dtype) for value in (latents, cotangent, restore)
    )
    return pl.pallas_call(
        pick_kernel,
        in_specs=[ANY, ANY, VMEM],
        out_shape=outs,
        out_specs=tuple(VMEM for _ in outs),
        scratch_shapes=[pltpu.SemaphoreType.DMA((2,))],
        compiler_params=pltpu.CompilerParams(vmem_limit_bytes=2 * 2**20),
        cost_estimate=pl.CostEstimate(flops=0, bytes_accessed=2**19, transcendentals=0),
    )(in_hbm(latents), in_hbm(cotangent), restore)


def prepare_kernel(
    latents, far_latents, restore, far_restore, position, my_latents, choice, my_position,
    near_buffer, sem,
):
    side = lax.axis_index("blk")
    copy = pltpu.make_async_copy(latents.at[pl.ds(side * MINE, MINE)], near_buffer, sem)
    copy.start()
    my_position[...] = position[...]
    for image in range(MINE):
        choice[image] = select_rows(
            restore[pl.ds(side * MINE + image, 1), :], far_restore[image : image + 1, :], side
        )
    copy.wait()
    half = KMAX // 2
    for image in range(MINE):
        at = image * KMAX
        my_latents[at : at + half, :] = near_buffer[image]
        my_latents[at + half : at + KMAX, :] = far_latents[image]


def prepare_call(*operands):
    outs = (
        pltpu.VMEM((MINE * KMAX, DIN), BF),
        pltpu.VMEM((MINE, PICKS, SLOTS), BF),
        pltpu.VMEM((SLOTS, D), F32),
    )
    return pl.pallas_call(
        prepare_kernel,
        in_specs=[ANY, VMEM, VMEM, VMEM, VMEM],
        out_shape=outs,
        out_specs=tuple(VMEM for _ in outs),
        scratch_shapes=[
            pltpu.VMEM((MINE, KMAX // 2, DIN), BF),
            pltpu.SemaphoreType.DMA,
        ],
        compiler_params=pltpu.CompilerParams(vmem_limit_bytes=4 * 2**20),
        cost_estimate=pl.CostEstimate(flops=10**6, bytes_accessed=2**20, transcendentals=0),
    )(in_hbm(operands[0]), *operands[1:])


def forward_kernel(bucket, my_latents, choice, position, vectors, lines, *rest):
    (
        probs,
        shares,
        joint,
        normed,
        start,
        middle,
        mixed,
        embed_w,
        joint_w,
        output_w,
        stage,
        query_t,
        value_t,
        mixed_t,
        scores_even,
        scores_odd,
    ) = rest
    side = lax.axis_index("blk")
    lines_to_matrix(lines, stage, embed_w, EMBED_AT, DIN, 4, 128)
    lines_to_matrix(lines, stage, joint_w, JOINT_AT, D, 12, 64)
    lines_to_matrix(lines, stage, output_w, OUTPUT_AT, D, 4, 128)
    embedded = (dot(my_latents[...], embed_w[...]) + vectors[0:1, :]).astype(BF)
    token = list(three_parts(vectors[1:2, :]))
    for image in range(MINE):
        rows = slice(image * SLOTS, (image + 1) * SLOTS)
        picked = choice[image]
        value = dot(picked[:KMAX], embedded[image * KMAX : (image + 1) * KMAX, :], (0, 0))
        masked = jnp.broadcast_to(picked[KMAX : KMAX + 1], (16, SLOTS))
        table = jnp.concatenate(token + [jnp.zeros((13, D), BF)], axis=0)
        value = value + dot(masked, table, (0, 0)) + position[...]
        start[rows, :] = value
        hat, _ = norm_parts(value)
        normed[rows, :] = (hat * vectors[2:3, :] + vectors[3:4, :]).astype(BF)
    for part, bias in enumerate((4, None, 5)):
        columns = slice(part * D, (part + 1) * D)
        out = dot(normed[...], joint_w[:, columns])
        if bias is not None:
            out = out + vectors[bias : bias + 1, :]
        joint[:, columns] = out.astype(BF)
    query_t[...] = joint[:, :D].T
    value_t[...] = joint[:, 2 * D :].T

    rate = HD**-0.5 * math.log2(math.e)

    def score(unit, target):
        image, group = unit // GROUPS, unit % GROUPS
        rows = pl.ds(pl.multiple_of(image * SLOTS, SLOTS), SLOTS)
        keys = joint[rows, pl.ds(pl.multiple_of(D + group * LANES, LANES), LANES)]
        queries = query_t[pl.ds(pl.multiple_of(group * LANES, LANES), LANES), rows]
        for head in range(GROUP):
            target[head] = dot(mask_head(keys, head), queries)

    def mix(unit, source):
        image, group = unit // GROUPS, unit % GROUPS
        rows = pl.ds(pl.multiple_of(image * SLOTS, SLOTS), SLOTS)
        length = image_length(bucket, side * MINE + image)
        hidden_key = jnp.where(slot_column(side) < length, 0.0, -1e30)
        for head in range(GROUP):
            scores = source[head] + hidden_key
            top = jnp.max(scores, axis=0, keepdims=True)
            raised = jnp.exp2((scores - top) * rate)
            share = 1.0 / jnp.sum(raised, axis=0, keepdims=True)
            low = raised.astype(BF)
            probs[unit * GROUP + head] = low
            shares[pl.ds(unit * GROUP + head, 1), :] = share
            features = pl.ds(pl.multiple_of(group * LANES + head * HD, HD), HD)
            mixed_t[features, rows] = (dot(value_t[features, rows], low) * share).astype(BF)

    score(0, scores_even)

    def pair(index, carry):
        unit = 2 * index
        score(unit + 1, scores_odd)
        mix(unit, scores_even)
        score(jnp.minimum(unit + 2, MINE * GROUPS - 1), scores_even)
        mix(unit + 1, scores_odd)
        return carry

    lax.fori_loop(0, MINE * GROUPS // 2, pair, 0)
    mixed[...] = mixed_t[...].T
    middle[...] = start[...] + dot(mixed[...], output_w[...]) + vectors[6:7, :]


def forward_call(*operands):
    outs = (
        pltpu.VMEM((MINE * HEADS, SLOTS, SLOTS), BF),
        pltpu.VMEM((MINE * HEADS, SLOTS), F32),
        pltpu.VMEM((TOKENS, 3 * D), BF),
        pltpu.VMEM((TOKENS, D), BF),
        pltpu.VMEM((TOKENS, D), F32),
        pltpu.VMEM((TOKENS, D), F32),
        pltpu.VMEM((TOKENS, D), BF),
        pltpu.VMEM((DIN, D), BF),
        pltpu.VMEM((D, 3 * D), BF),
        pltpu.VMEM((D, D), BF),
    )
    return pl.pallas_call(
        forward_kernel,
        in_specs=[SMEM] + [VMEM] * (len(operands) - 1),
        out_shape=outs,
        out_specs=tuple(VMEM for _ in outs),
        scratch_shapes=[
            pltpu.VMEM((2, 768, LANES), F32),
            pltpu.VMEM((D, TOKENS), BF),
            pltpu.VMEM((D, TOKENS), BF),
            pltpu.VMEM((D, TOKENS), BF),
            pltpu.VMEM((GROUP, SLOTS, SLOTS), F32),
            pltpu.VMEM((GROUP, SLOTS, SLOTS), F32),
        ],
        compiler_params=pltpu.CompilerParams(vmem_limit_bytes=10 * 2**20),
        cost_estimate=pl.CostEstimate(
            flops=6 * 10**9, bytes_accessed=16 * 2**20, transcendentals=2 * 10**6
        ),
    )(*operands)


def middle_kernel(
    by_hand, bucket, middle, cotangent, far_cotangent, vectors, lines, *rest
):
    (
        acc,
        hat,
        scale,
        back_out,
        acc_back,
        head_lines,
        far_lines,
        near_lines,
        expand_out,
        stage,
        expand_w,
        reduce_w,
        normed,
        normed_t,
        grads,
    ) = rest
    step = pl.program_id(0)
    side = lax.axis_index("blk")

    @pl.when(step == 0)
    def _():
        value, spread = norm_parts(middle[...])
        hat[...] = value
        scale[...] = jnp.broadcast_to(spread, scale.shape)
        normed[...] = (value * vectors[7:8, :] + vectors[8:9, :]).astype(BF)
        normed_t[...] = normed[...].T
        for image in range(MINE):
            valid = slot_column(side) < image_length(bucket, side * MINE + image)
            half = SLOTS // 2
            for part, (ref, at) in enumerate(
                ((cotangent, side * MINE + image), (far_cotangent, image))
            ):
                first = image * SLOTS + part * half
                back_out[first : first + half, :] = jnp.where(
                    valid[part * half : (part + 1) * half, :],
                    ref[at].astype(F32),
                    0.0,
                ).astype(BF)
        acc[...] = jnp.zeros_like(acc)
        acc_back[...] = jnp.zeros_like(acc_back)
        lines_to_matrix(lines, stage, expand_w, EXPAND_AT, D, 16, 32)
        lines_to_matrix(lines, stage, reduce_w, REDUCE_AT, FF, 4, 128)

    columns = pl.ds(pl.multiple_of(step * TILE, TILE), TILE)
    expand = expand_w[:, columns]
    reduce = reduce_w[columns, :]
    bias = vectors[pl.ds(10 + step, 1), :]
    hidden = dot(normed[...], expand) + bias
    density = jnp.exp(hidden * hidden * -0.5) * (1.0 / math.sqrt(2.0 * math.pi))
    below = 0.5 + 0.5 * lax.erf(hidden * math.sqrt(0.5))
    active = (hidden * below).astype(BF)
    back_active = dot(back_out[...], reduce, (1, 1))
    back_hidden = (back_active * (below + hidden * density)).astype(BF)
    acc[...] += dot(active, reduce)
    acc_back[...] += dot(back_hidden, expand, (1, 1))
    grad_reduce = dot(active, back_out[...], (0, 0))
    for j in range(4):
        grads[pl.ds(D * 16 + step * (TILE * 4) + j, TILE, stride=4), :] = grad_reduce[
            :, j * LANES : (j + 1) * LANES
        ]
    grad_expand = dot(normed_t[...], back_hidden)
    for j in range(TILE // LANES):
        grads[pl.ds(step * (TILE // LANES) + j, D, stride=16), :] = grad_expand[
            :, j * LANES : (j + 1) * LANES
        ]
    expand_out[pl.ds(step, 1), :] = total(back_hidden)

    @pl.when(step == TILES - 1)
    def _():
        cut = HALF - EXPAND_AT
        head_lines[...] = grads[:cut, :].astype(BF)
        put_blocks(
            by_hand,
            far_lines,
            near_lines,
            lambda q: grads[pl.ds(cut + q * BLOCK, BLOCK), :].astype(BF),
        )


FIRST, SECOND, ALONG_Z = 0, 1, 2
HOP_BITS = ((1, 4), (4, 1), (8, 8))
HIGH_ORDER = (FIRST, ALONG_Z, SECOND)
ONE_ORDER = (FIRST, SECOND, ALONG_Z)
TWO_ORDER = (FIRST, SECOND, ALONG_Z)


def slot_of(index, by_hand, order):
    if not by_hand:
        return index
    me = place()
    rel = index ^ (me & 15)
    other = (rel >> 1) & 1
    odd = ((me >> 1) & 1) ^ other
    along_y, along_x, along_z = rel & 1, (rel >> 2) & 1, rel >> 3
    first = jnp.where(odd == 0, along_y, along_x)
    second = jnp.where(odd == 0, along_x, along_y)
    bits = (first, second, along_z)
    slot = (1 - bits[order[0]]) * 4 + (1 - bits[order[1]]) * 2 + (1 - bits[order[2]])
    return slot + jnp.where(other == 1, 0, 8)


def put_blocks(by_hand, far_lines, near_lines, block_of):
    def body(index, carry):
        slot = slot_of(index, by_hand, HIGH_ORDER)
        value = block_of(index)

        @pl.when(slot < 8)
        def _():
            far_lines[pl.ds(pl.multiple_of(slot * BLOCK, 16), BLOCK), :] = value

        @pl.when(slot >= 8)
        def _():
            near_lines[pl.ds(pl.multiple_of((slot - 8) * BLOCK, 16), BLOCK), :] = value

        return carry

    lax.fori_loop(0, 16, body, 0)


def middle_call(by_hand, *operands):
    outs = (
        pltpu.VMEM((TOKENS, D), F32),
        pltpu.VMEM((TOKENS, D), F32),
        pltpu.VMEM((TOKENS, LANES), F32),
        pltpu.VMEM((TOKENS, D), BF),
        pltpu.VMEM((TOKENS, D), F32),
        pltpu.VMEM((HALF - EXPAND_AT, LANES), BF),
        pltpu.VMEM((8 * BLOCK, LANES), BF),
        pltpu.VMEM((8 * BLOCK, LANES), BF),
        pltpu.VMEM((TILES, TILE), F32),
    )
    return pl.pallas_call(
        lambda *refs: middle_kernel(by_hand, *refs),
        grid=(TILES,),
        in_specs=[SMEM] + [VMEM] * (len(operands) - 1),
        out_shape=outs,
        out_specs=tuple(VMEM for _ in outs),
        scratch_shapes=[
            pltpu.VMEM((2, 768, LANES), F32),
            pltpu.VMEM((D, FF), BF),
            pltpu.VMEM((FF, D), BF),
            pltpu.VMEM((TOKENS, D), BF),
            pltpu.VMEM((D, TOKENS), BF),
            pltpu.VMEM((2 * D * 16, LANES), F32),
        ],
        compiler_params=pltpu.CompilerParams(vmem_limit_bytes=26 * 2**20),
        cost_estimate=pl.CostEstimate(
            flops=8 * 10**9, bytes_accessed=16 * 2**20, transcendentals=2 * 10**6
        ),
    )(*operands)


def branch_kernel(
    middle, acc, hat, scale, back_out, acc_back, mixed, output_w, vectors,
    own_out, far_out, back_middle, back_mixed, out_lines, rows_out, out_grads,
):
    for image in range(MINE):
        near = slice(image * SLOTS, image * SLOTS + SLOTS // 2)
        far = slice(image * SLOTS + SLOTS // 2, (image + 1) * SLOTS)
        own_out[image] = middle[near, :] + acc[near, :] + vectors[9:10, :]
        far_out[image] = (middle[far, :] + acc[far, :] + vectors[9:10, :]).astype(BF)
    grad = acc_back[...]
    rows_out[...] = jnp.zeros_like(rows_out)
    rows_out[1:2, :] = total(grad * hat[...])
    rows_out[2:3, :] = total(grad)
    rows_out[3:4, :] = total(back_out[...])
    back = back_out[...].astype(F32) + norm_back(
        grad, hat[...], scale[:, :1], vectors[7:8, :]
    )
    back_middle[...] = back
    branch = back.astype(BF)
    rows_out[0:1, :] = total(branch)
    back_mixed[...] = dot(branch, output_w[...], (1, 1)).astype(BF)
    grad_output = dot(mixed[...], branch, (0, 0))
    for j in range(4):
        out_grads[pl.ds(j, D, stride=4), :] = grad_output[:, j * LANES : (j + 1) * LANES]
    out_lines[...] = out_grads[...].astype(BF)


def branch_call(*operands):
    outs = (
        pltpu.VMEM((MINE, SLOTS // 2, D), F32),
        pltpu.VMEM((MINE, SLOTS // 2, D), BF),
        pltpu.VMEM((TOKENS, D), F32),
        pltpu.VMEM((TOKENS, D), BF),
        pltpu.VMEM((EXPAND_AT - OUTPUT_AT, LANES), BF),
        pltpu.VMEM((8, D), F32),
    )
    return pl.pallas_call(
        branch_kernel,
        in_specs=[VMEM] * len(operands),
        out_shape=outs,
        out_specs=tuple(VMEM for _ in outs),
        scratch_shapes=[pltpu.VMEM((D * 4, LANES), F32)],
        compiler_params=pltpu.CompilerParams(vmem_limit_bytes=16 * 2**20),
        cost_estimate=pl.CostEstimate(
            flops=2 * 10**9, bytes_accessed=4 * 2**20, transcendentals=0
        ),
    )(*operands)


def attention_back_kernel(
    probs, shares, joint, back_mixed, normed, start, back_middle, vectors, joint_w,
    back_start, rows_out,
    joint_back, key_t, back_t, shared_t, shared, query_back_t, even, odd, grads,
):
    key_t[...] = joint[:, D : 2 * D].T
    back_t[...] = back_mixed[...].T
    for image in range(MINE):
        columns = slice(image * SLOTS, (image + 1) * SLOTS)
        for head in range(HEADS):
            features = slice(head * HD, (head + 1) * HD)
            at = image * HEADS + head
            shared_t[features, columns] = (
                back_t[features, columns].astype(F32) * shares[at : at + 1, :]
            ).astype(BF)
    shared[...] = shared_t[...].T

    def pull_back(unit, target):
        image, group = unit // GROUPS, unit % GROUPS
        rows = pl.ds(pl.multiple_of(image * SLOTS, SLOTS), SLOTS)
        values = joint[rows, pl.ds(pl.multiple_of(2 * D + group * LANES, LANES), LANES)]
        back_lanes = back_t[pl.ds(pl.multiple_of(group * LANES, LANES), LANES), rows]
        for head in range(GROUP):
            target[head] = dot(mask_head(values, head), back_lanes)

    def spread(unit, source):
        image, group = unit // GROUPS, unit % GROUPS
        rows = pl.ds(pl.multiple_of(image * SLOTS, SLOTS), SLOTS)
        lanes = pl.ds(pl.multiple_of(group * LANES, LANES), LANES)
        queries = joint[rows, lanes]
        back = shared[rows, lanes]
        key_back = jnp.zeros((SLOTS, LANES), F32)
        value_back = jnp.zeros((SLOTS, LANES), F32)
        for head in range(GROUP):
            low = probs[unit * GROUP + head]
            share = shares[pl.ds(unit * GROUP + head, 1), :]
            wide = low.astype(F32)
            back_probs = source[head]
            pull = jnp.sum(wide * back_probs, axis=0, keepdims=True) * share
            score_back = (wide * ((back_probs - pull) * (share * HD**-0.5))).astype(BF)
            value_back = value_back + dot(low, mask_head(back, head))
            key_back = key_back + dot(score_back, mask_head(queries, head))
            features = pl.ds(pl.multiple_of(group * LANES + head * HD, HD), HD)
            query_back_t[features, rows] = dot(key_t[features, rows], score_back).astype(BF)
        joint_back[rows, pl.ds(pl.multiple_of(D + group * LANES, LANES), LANES)] = (
            key_back.astype(BF)
        )
        joint_back[rows, pl.ds(pl.multiple_of(2 * D + group * LANES, LANES), LANES)] = (
            value_back.astype(BF)
        )

    pull_back(0, even)

    def pair(index, carry):
        unit = 2 * index
        pull_back(unit + 1, odd)
        spread(unit, even)
        pull_back(jnp.minimum(unit + 2, MINE * GROUPS - 1), even)
        spread(unit + 1, odd)
        return carry

    lax.fori_loop(0, MINE * GROUPS // 2, pair, 0)
    joint_back[:, :D] = query_back_t[...].T
    rows_out[...] = jnp.zeros_like(rows_out)
    rows_out[2:3, :] = total(joint_back[:, :D])
    rows_out[3:4, :] = total(joint_back[:, 2 * D :])
    normed_t = normed[...].T
    for part in range(3):
        grad_joint = dot(normed_t, joint_back[:, part * D : (part + 1) * D])
        for j in range(4):
            grads[pl.ds(part * 4 + j, D, stride=12), :] = grad_joint[
                :, j * LANES : (j + 1) * LANES
            ]
    grad = dot(joint_back[...], joint_w[...], (1, 1))
    hat, scale = norm_parts(start[...])
    rows_out[0:1, :] = total(grad * hat)
    rows_out[1:2, :] = total(grad)
    back_start[...] = back_middle[...] + norm_back(grad, hat, scale, vectors[2:3, :])


def input_back_kernel(
    by_hand,
    back_start,
    my_latents,
    choices,
    embed_w,
    joint_lines,
    rows_joint,
    out_lines,
    head_lines,
    rows_in,
    expand_in,
    far_out,
    far_first,
    near_first,
    far_second,
    near_second,
    rows_out,
    own_latent,
    pack,
    grads,
    tails,
):
    rows_out[...] = jnp.zeros_like(rows_out)
    rows_out[2:6, :] = rows_joint[0:4, :]
    low_start = back_start[...].astype(BF)
    low_rest = (back_start[...] - low_start.astype(F32)).astype(BF)
    picked = []
    token_back = jnp.zeros((1, D), F32)
    for image in range(MINE):
        part = slice(image * SLOTS, (image + 1) * SLOTS)
        choice = choices[image]
        chosen = dot(choice, low_start[part, :])
        picked.append(chosen[:KMAX, :].astype(BF))
        token_back = token_back + chosen[KMAX : KMAX + 1, :]
        token_back = token_back + dot(choice[KMAX:, :], low_rest[part, :])[:1, :]
    rows_out[1:2, :] = token_back
    embedded_back = jnp.concatenate(picked, axis=0)
    rows_out[0:1, :] = total(embedded_back)
    grad_embed = dot(my_latents[...], embedded_back, (0, 0))
    for j in range(4):
        grads[pl.ds(EMBED_AT + j, DIN, stride=4), :] = grad_embed[:, j * LANES : (j + 1) * LANES]
    latent_back = dot(embedded_back, embed_w[...], (1, 1))
    for image in range(MINE):
        at = image * KMAX
        own_latent[image] = latent_back[at : at + KMAX // 2, :]
        far = latent_back[at + KMAX // 2 : at + KMAX, :].astype(BF)
        pack[image, : SLOTS // 2, :] = far_out[image]
        pack[image, SLOTS // 2 : SLOTS // 2 + KMAX // 2, :] = far[:, :D]
        pack[image, SLOTS // 2 + KMAX // 2 :, : DIN - D] = far[: KMAX // 4, D:]
        pack[image, SLOTS // 2 + KMAX // 2 :, DIN - D :] = far[KMAX // 4 :, D:]
    rows_out[6:10, :] = rows_in[0:4, :]
    for j in range(4):
        rows_out[10 + j : 11 + j, :] = expand_in[j : j + 1, :]
    tails[...] = jnp.zeros_like(tails)
    for row in range(ROWS):
        for j in range(D // LANES):
            tails[row * TAIL + j : row * TAIL + j + 1, :] = rows_out[
                row : row + 1, j * LANES : (j + 1) * LANES
            ]

    def store(index, value):
        slot = slot_of(index, by_hand, ONE_ORDER)
        late = slot_of(index, by_hand, TWO_ORDER)
        tail = tails[pl.ds(pl.multiple_of(index * TAIL, TAIL), TAIL), :].astype(BF)

        def put(first, second, at, late_at):
            row = pl.multiple_of(at * PARTS[0], 16)
            first[pl.ds(row, PART), :] = value[:PART]
            first[pl.ds(row + PART, TAIL), :] = tail
            second[pl.ds(pl.multiple_of(late_at * PART, 16), PART), :] = value[PART:]

        @pl.when(slot < 8)
        def _():
            put(far_first, far_second, slot, late)

        @pl.when(slot >= 8)
        def _():
            put(near_first, near_second, slot - 8, late - 8)

    ranges = (
        (EMBED_AT, JOINT_AT, lambda low, high: grads[low:high, :].astype(BF)),
        (JOINT_AT, OUTPUT_AT, lambda low, high: joint_lines[low:high, :].astype(BF)),
        (OUTPUT_AT, EXPAND_AT, lambda low, high: out_lines[low:high, :]),
        (EXPAND_AT, HALF, lambda low, high: head_lines[low:high, :]),
    )
    for index in range(16):
        low, high = index * BLOCK, (index + 1) * BLOCK
        parts = [
            take(max(low, begin) - begin, min(high, end) - begin)
            for begin, end, take in ranges
            if max(low, begin) < min(high, end)
        ]
        store(index, jnp.concatenate(parts, axis=0) if len(parts) > 1 else parts[0])


def back_kernel(by_hand, *refs):
    attention, (my_latents, choices, embed_w, out_lines, head_lines, rows_in, expand_in, far_out) = (
        refs[:9], refs[9:17],
    )
    outs, scratch = refs[17:24], refs[24:]
    back_start, rows_joint = scratch[:2]
    attention_back_kernel(*attention, back_start, rows_joint, *scratch[2:11])
    joint_lines = scratch[10]
    input_back_kernel(
        by_hand, back_start, my_latents, choices, embed_w, joint_lines, rows_joint, out_lines,
        head_lines, rows_in, expand_in, far_out, *outs, *scratch[11:],
    )


def back_call(by_hand, *operands):
    shape = jax.ShapeDtypeStruct
    outs = (
        pltpu.VMEM((8 * PARTS[0], LANES), BF),
        pltpu.VMEM((8 * PARTS[0], LANES), BF),
        pltpu.VMEM((8 * PARTS[1], LANES), BF),
        pltpu.VMEM((8 * PARTS[1], LANES), BF),
        shape((ROWS, D), F32),
        pltpu.VMEM((MINE, KMAX // 2, DIN), F32),
        pltpu.VMEM((MINE, PACK, D), BF),
    )
    return pl.pallas_call(
        lambda *refs: back_kernel(by_hand, *refs),
        in_specs=[VMEM] * len(operands),
        out_shape=outs,
        out_specs=tuple(VMEM for _ in outs),
        scratch_shapes=[
            pltpu.VMEM((TOKENS, D), F32),
            pltpu.VMEM((8, D), F32),
            pltpu.VMEM((TOKENS, 3 * D), BF),
            pltpu.VMEM((D, TOKENS), BF),
            pltpu.VMEM((D, TOKENS), BF),
            pltpu.VMEM((D, TOKENS), BF),
            pltpu.VMEM((TOKENS, D), BF),
            pltpu.VMEM((D, TOKENS), BF),
            pltpu.VMEM((GROUP, SLOTS, SLOTS), F32),
            pltpu.VMEM((GROUP, SLOTS, SLOTS), F32),
            pltpu.VMEM((OUTPUT_AT - JOINT_AT, LANES), F32),
            pltpu.VMEM((JOINT_AT, LANES), F32),
            pltpu.VMEM((ROWS * TAIL, LANES), F32),
        ],
        compiler_params=pltpu.CompilerParams(vmem_limit_bytes=24 * 2**20),
        cost_estimate=pl.CostEstimate(
            flops=4 * 10**9, bytes_accessed=8 * 2**20, transcendentals=0
        ),
    )(*operands)


class Grid:
    def __init__(self, mesh):
        self.axes = ("dp", "blk")
        self.count = mesh.shape["dp"] * mesh.shape["blk"]
        self.early = self.late = ()
        self.by_hand = self.count == 32 and mesh.shape["blk"] == 2

    def send(self, value, bits, other=None):
        other = bits if other is None else other
        pairs = [(i, i ^ (other if i & 2 else bits)) for i in range(self.count)]
        return lax.ppermute(value, self.axes, pairs)

    def gather(self, block):
        if not self.by_hand:
            whole = lax.all_gather(block, self.axes, axis=0, tiled=True)
            return whole.reshape(LINES, LANES)
        got = {"held0": block}

        def send(name, value, bits, other=None, behind=()):
            got[name] = self.send(after(got[value], *(got[b] for b in behind)), bits, other)

        def put(lines, *names):
            pieces, places = [], []
            for name in names:
                even, uneven = {"held": (0, 0), "near": (4, 1), "side": (1, 4), "far": (5, 5)}[
                    name.rstrip("0123456789")
                ]
                bits = int(name.lstrip("abcdefghijklmnopqrstuvwxyz"))
                pieces += [got[name], self.send(got[name], 2)]
                places += [(bits, even, uneven), (bits ^ 2, uneven, even)]
            return collect_call(lines, pieces, places)

        send("held16", "held0", 16)
        send("near0", "held0", 4, 1)
        send("held8", "held0", 8)
        send("side0", "held0", 1, 4)
        send("far0", "near0", 1, 4)
        send("near16", "held16", 4, 1)
        send("side16", "held16", 1, 4)
        send("held24", "held16", 8)
        send("near8", "held8", 4, 1)
        send("side8", "held8", 1, 4)
        send("far8", "far0", 8)
        send("far16", "near16", 1, 4, behind=("far0",))
        send("near24", "held24", 4, 1)
        send("side24", "held24", 1, 4, behind=("near16",))
        send("far24", "far16", 8)
        lines = put(
            None, "held0", "near0", "side0", "far0", "held8", "near8", "side8", "far8", "held16",
            "near16", "side16", "far16", "held24", "near24", "side24", "far24",
        )
        self.late = (got["side24"], got["far24"])
        self.early = (got["far8"], got["side24"])
        return lines


def add_call(rows, *terms):
    def kernel(*refs):
        out = refs[-1]
        value = None
        for ref, (_, at) in zip(refs[:-1], terms, strict=True):
            part = ref[at : at + rows, :].astype(F32)
            value = part if value is None else value + part
        out[...] = value.astype(BF)

    return pl.pallas_call(
        kernel,
        in_specs=[VMEM] * len(terms),
        out_shape=pltpu.VMEM((rows, LANES), BF),
        out_specs=VMEM,
        compiler_params=pltpu.CompilerParams(vmem_limit_bytes=4 * 2**20),
        cost_estimate=pl.CostEstimate(flops=10**5, bytes_accessed=2**20, transcendentals=0),
    )(*(in_vmem(array) for array, _ in terms))


def in_hbm(value):
    return pltpu.with_memory_space_constraint(value, pltpu.HBM)


def in_vmem(value):
    return pltpu.with_memory_space_constraint(value, pltpu.VMEM)


class Reduction:
    def __init__(self, grid, far_lines, near_lines, order):
        self.grid = grid
        self.near = near_lines
        self.hops = ((2, 2), *(HOP_BITS[hop] for hop in order))
        self.rows = far_lines.shape[0] // 8
        self.head = far_lines
        self.came = []

    def hop(self, *behind):
        step = len(self.came)
        self.came.append(self.grid.send(self.head, *self.hops[step]))
        left = 8 >> (step + 1)
        count = max(left, 1) if step < 3 else 1
        begin = 8 - 2 * left if step < 3 else 7
        terms = [(after(self.near, *behind), begin * self.rows)]
        for level, value in enumerate(self.came):
            terms.append((value, (begin - (8 - (8 >> level))) * self.rows))
        self.head = add_call(count * self.rows, *terms)
        return self.head


def cross_call(low, high, at):
    rows = low.shape[0]
    lines = min(rows, PART)

    def kernel(low, high, out):
        lower = (place() & 16) == 0
        out[:lines, :] = jnp.where(lower, high[at : at + lines, :], low[:lines, :])
        if lines < rows:
            out[lines:, :] = low[lines:, :]

    return pl.pallas_call(
        kernel,
        in_specs=[VMEM] * 2,
        out_shape=pltpu.VMEM((rows, LANES), BF),
        out_specs=VMEM,
        compiler_params=pltpu.CompilerParams(vmem_limit_bytes=2**20),
        cost_estimate=pl.CostEstimate(flops=0, bytes_accessed=2**17, transcendentals=0),
    )(in_vmem(low), in_vmem(high))


def finish_kernel(high, one, one_far, two, two_far, grad, notes):
    lower = (place() & 16) == 0

    for begin, near, far in ((0, one, one_far), (PART, two, two_far)):
        upper = high[begin : begin + PART, :].astype(F32)
        mine = jnp.where(lower, near[:PART, :].astype(F32), upper)
        grad[begin : begin + PART, :] = mine + far[:PART, :].astype(F32)
    tail = one[PART:, :].astype(F32) + one_far[PART:, :].astype(F32)
    row = jnp.where(lower, tail, 0.0)
    value = grad[...]
    square = jnp.sum(jnp.sum(value * value, axis=0, keepdims=True), axis=1, keepdims=True)
    square = square + jnp.sum(jnp.sum(row * row, axis=0, keepdims=True), axis=1, keepdims=True)
    line = lax.broadcasted_iota(jnp.int32, (8, LANES), 0)
    note = jnp.where(line < 4, row[:8], square)
    for device in range(notes.shape[0]):
        notes[device] = note


def finish_call(count, *operands):
    outs = (pltpu.VMEM((BLOCK, LANES), F32), pltpu.VMEM((count, 8, LANES), F32))
    return pl.pallas_call(
        finish_kernel,
        in_specs=[VMEM] * len(operands),
        out_shape=outs,
        out_specs=tuple(VMEM for _ in outs),
        compiler_params=pltpu.CompilerParams(vmem_limit_bytes=8 * 2**20),
        cost_estimate=pl.CostEstimate(flops=10**6, bytes_accessed=2**20, transcendentals=0),
    )(*(in_vmem(value) for value in operands))


def update_kernel(
    grad, notes, first, second, weights, vectors, vector_first, vector_second,
    first_out, second_out, weights_out, vectors_first_out, vectors_second_out, vectors_out,
    bias_out, norm_out, sums,
):
    square = jnp.sum(notes[:, 4, :], axis=0, keepdims=True)
    norm = jnp.sqrt(square)
    factor = jnp.minimum(1.0, clip_norm / (norm + 1e-06))
    norm_out[...] = norm
    for row in range(sums.shape[0]):
        for j in range(D // LANES):
            sums[row : row + 1, j * LANES : (j + 1) * LANES] = notes[row, j : j + 1, :]
    first_out[...], second_out[...], weights_out[...] = adam_update(
        grad[...] * factor, first[...], second[...], weights[...], learn_rate, decay_weight
    )
    clipped = sums[...] * jnp.concatenate([factor] * (D // LANES), axis=1)
    bias_out[...] = clipped[9:10, :]
    vectors_first_out[...], vectors_second_out[...], vectors_out[...] = adam_update(
        clipped, vector_first[...], vector_second[...], vectors[...], vector_rate, 0.0
    )


def update_call(*operands):
    shape = jax.ShapeDtypeStruct
    lines, rows = operands[2].shape, operands[5].shape
    outs = (
        [shape(lines, F32)] * 3
        + [shape(rows, F32)] * 3
        + [shape((1, rows[1]), F32), shape((1, LANES), F32)]
    )
    return pl.pallas_call(
        update_kernel,
        in_specs=[VMEM] * len(operands),
        out_shape=outs,
        out_specs=[VMEM for _ in outs],
        scratch_shapes=[pltpu.VMEM(rows, F32)],
        compiler_params=pltpu.CompilerParams(vmem_limit_bytes=12 * 2**20),
        cost_estimate=pl.CostEstimate(flops=10**7, bytes_accessed=2**22, transcendentals=10**6),
    )(*operands)


def join_kernel(own_out, own_latent, pack, block_out, latent_out, out_wide, latent_wide, sem):
    side = lax.axis_index("blk")
    mine = pl.ds(side * MINE, MINE)
    other = pl.ds((1 - side) * MINE, MINE)
    half = SLOTS // 2
    copies = [
        pltpu.make_async_copy(own_out, block_out.at[mine], sem.at[0]),
        pltpu.make_async_copy(own_latent, latent_out.at[mine], sem.at[1]),
        pltpu.make_async_copy(out_wide, block_out.at[other], sem.at[2]),
        pltpu.make_async_copy(latent_wide, latent_out.at[other], sem.at[3]),
    ]
    copies[0].start()
    copies[1].start()
    for image in range(MINE):
        out_wide[image] = pack[image, :half, :].astype(F32)
        latent_wide[image, :, :D] = pack[image, half : half + KMAX // 2, :].astype(F32)
        last = pack[image, half + KMAX // 2 :, :].astype(F32)
        latent_wide[image, : KMAX // 4, D:] = last[:, : DIN - D]
        latent_wide[image, KMAX // 4 :, D:] = last[:, DIN - D :]
    copies[2].start()
    copies[3].start()
    for copy in copies:
        copy.wait()


def join_call(own_out, own_latent, pack, images):
    shape = jax.ShapeDtypeStruct
    return pl.pallas_call(
        join_kernel,
        in_specs=[VMEM] * 3,
        out_shape=(
            shape((images, *own_out.shape[1:]), F32),
            shape((images, *own_latent.shape[1:]), F32),
        ),
        out_specs=(ANY, ANY),
        scratch_shapes=[
            pltpu.VMEM(own_out.shape, F32),
            pltpu.VMEM(own_latent.shape, F32),
            pltpu.SemaphoreType.DMA((4,)),
        ],
        compiler_params=pltpu.CompilerParams(vmem_limit_bytes=4 * 2**20),
        cost_estimate=pl.CostEstimate(flops=0, bytes_accessed=2**21, transcendentals=0),
    )(own_out, own_latent, pack)


def after(value, *others):
    if not others:
        return value
    return lax.optimization_barrier((value, *others))[0]


def local(
    grid,
    latents,
    restore,
    bucket,
    cotangent,
    flat_weights,
    flat_first,
    flat_second,
    vectors,
    vector_first,
    vector_second,
):
    side = lax.axis_index("blk").astype(jnp.int32)
    by_hand = grid.by_hand

    def trade(value):
        return lax.ppermute(value, "blk", [(0, 1), (1, 0)])

    out_latents, out_cotangent, out_restore = pick_call(latents, cotangent, restore)
    lines = grid.gather(flat_weights.reshape(-1, LANES).astype(BF))
    slot = (jnp.arange(SLOTS, dtype=jnp.int32) + side * (SLOTS // 2)) & (SLOTS - 1)
    position = position_rows(slot)
    my_latents, choice, my_position = prepare_call(
        latents, trade(after(out_latents, *grid.early)), restore,
        trade(after(out_restore, *grid.early)), position,
    )
    far_cotangent = trade(after(out_cotangent, *grid.late))
    (
        probs, shares, joint, normed, start, middle, mixed, embed_w, joint_w, output_w,
    ) = forward_call(bucket, my_latents, choice, my_position, vectors, lines)
    (
        acc, hat, scale, back_out, acc_back, head_lines, far_high, near_high, expand_b,
    ) = middle_call(by_hand, bucket, middle, cotangent, far_cotangent, vectors, lines)
    if by_hand:
        high = Reduction(grid, far_high, near_high, HIGH_ORDER)
    own_out, far_out, back_middle, back_mixed, out_lines, rows_b = branch_call(
        middle, acc, hat, scale, back_out, acc_back, mixed, output_w, vectors
    )
    if by_hand:
        back_mixed = after(back_mixed, high.hop(back_mixed))
    far_one, near_one, far_two, near_two, rows_c, own_latent, pack = back_call(
        by_hand, probs, shares, joint, back_mixed, normed, start, back_middle, vectors, joint_w,
        my_latents, choice, embed_w, out_lines, head_lines, rows_b, expand_b, far_out,
    )
    if by_hand:
        mark = high.hop(far_one)
        one = Reduction(grid, after(far_one, mark), near_one, ONE_ORDER)
        two = Reduction(grid, after(far_two, mark), near_two, TWO_ORDER)
        for stream in (one, two, one, high, two, one, high, two, one, two):
            mark = stream.hop(mark)
            if stream is two:
                pack_mark = mark
        across = [
            grid.send(cross_call(stream.head, high.head, at), 16)
            for stream, at in ((one, 0), (two, PART))
        ]
        pack = after(pack, pack_mark)
    block_out, latent_out = join_call(own_out, own_latent, trade(pack), latents.shape[0])

    if by_hand:
        grad, notes = finish_call(
            grid.count, high.head, one.head, across[0], two.head, across[1]
        )
        notes = lax.all_to_all(notes, grid.axes, 0, 0, tiled=True)
        lines = [value.reshape(-1, LANES) for value in (flat_first, flat_second, flat_weights)]
        outs = update_call(grad, notes, *lines, vectors, vector_first, vector_second)
        return (
            block_out,
            latent_out,
            *(value.reshape(-1) for value in outs[:3]),
            *outs[3:6],
            outs[6].reshape(-1),
            outs[7][0, 0],
        )

    low = [
        jnp.concatenate([far, near], axis=0).reshape(16, -1, LANES)[:, :PART]
        for far, near in ((far_one, near_one), (far_two, near_two))
    ]
    flat = jnp.concatenate(
        [jnp.concatenate(low, axis=1).reshape(-1), far_high.reshape(-1), near_high.reshape(-1)]
    )
    shard_grad = lax.psum_scatter(flat, grid.axes, scatter_dimension=0, tiled=True)
    shard_grad = shard_grad.astype(F32).reshape(-1, LANES)
    vector_sum = lax.psum(rows_c[: vectors.shape[0]], grid.axes)
    square_sum = lax.psum(jnp.sum(shard_grad * shard_grad), grid.axes)
    grad_norm = jnp.sqrt(square_sum + jnp.sum(vector_sum * vector_sum))
    factor = jnp.minimum(1.0, clip_norm / (grad_norm + 1e-06))
    new_first, new_second, new_weights = adam_update(
        shard_grad.reshape(-1) * factor,
        flat_first,
        flat_second,
        flat_weights,
        learn_rate,
        decay_weight,
    )
    vector_first_new, vector_second_new, vectors_new = adam_update(
        vector_sum * factor, vector_first, vector_second, vectors, vector_rate, 0.0
    )
    reduce_bias_grad = vector_sum[9] * factor
    return (
        block_out,
        latent_out,
        new_first,
        new_second,
        new_weights,
        vector_first_new,
        vector_second_new,
        vectors_new,
        reduce_bias_grad,
        grad_norm,
    )


def solution(mesh):
    grid = Grid(mesh)
    return jax.shard_map(
        lambda *args: local(grid, *args),
        mesh=mesh,
        in_specs=(
            P("dp", "blk", None),
            P("dp", "blk"),
            P("dp"),
            P("dp", "blk", None),
            P(("dp", "blk")),
            P(("dp", "blk")),
            P(("dp", "blk")),
            P(),
            P(),
            P(),
        ),
        out_specs=(
            P("dp", "blk", None),
            P("dp", "blk", None),
            P(("dp", "blk")),
            P(("dp", "blk")),
            P(("dp", "blk")),
            P(),
            P(),
            P(),
            P(),
            P(),
        ),
        check_vma=False,
    )
```
